256 devices in a mesh: dp: 16 (over x, z_lo), tensor: 16 (over y, z_hi, core).
Axes of the slice: x: 4, y: 4, z: 8 (z_hi: 2, z_lo: 4; z = z_hi * 4 + z_lo), core: 2. Of those that a mesh axis runs over, the one named last changes fastest.
Arguments:
- gate_hidden_input: bfloat16 [32768, 4608], P(('dp', 'tensor')), may hold values from -6 to 6
- output_gradient: bfloat16 [32768, 4608], P(('dp', 'tensor')), may hold values from -6 to 6
- attention_mixture: bfloat16 [32768, 4096], P('dp', 'tensor'), may hold values from -6 to 6
- output_matrix: bfloat16 [4096, 4608], P('tensor'), may hold values from -0.09375 to 0.09375
- adapter_down_weight: bfloat16 [4096, 128], P('tensor'), may hold values from -0.09375 to 0.09375
- adapter_up_weight: bfloat16 [128, 4608], replicated, may hold values from -1.5 to 1.5
- gate_matrix: bfloat16 [8, 4608], replicated, may hold values from -0.09375 to 0.09375
Outputs:
- gate_grad: float32 [8, 4608], replicated
- attention_gradient: bfloat16 [32768, 4096], P('dp', 'tensor')
The draws below stay inside these ranges and needn't reach their ends.
All inputs are finite; a program needn't handle non-finite values.
Results may differ from the reference program's by a relative error of at most 0.0047.
Values may be sent and summed in bfloat16 or wider, within the bound.
No kernel may reach another device: no remote copies, remote signals or barrier semaphores. Data moves between devices by JAX's collectives and lax.ppermute only.
A program may use at most 128 MiB of HBM per device.

```python
import jax
import jax.numpy as jnp
from jax import lax

MODEL_WIDTH = 4608
QUERY_FEATURES = 4096
ADAPTER_COUNT = 8
ADAPTER_RANK = 16
STACKED_RANK = 128
TOKENS = 32768


def levels(stream_key, dims, split, least, largest):
    loudness, own = 1.0, jax.random.fold_in(stream_key, 6)
    for axis_at, blocks in split:
        heights = jnp.exp(jax.random.uniform(jax.random.fold_in(own, axis_at), (blocks,), jnp.float32, least / len(split), largest / len(split)))
        loudness = loudness * jnp.repeat(heights, dims[axis_at] // blocks).reshape([-1 if axis == axis_at else 1 for axis in range(len(dims))])
    return loudness


def normal_values(stream_key, dims, deviation, most, shards=(), dtype=jnp.bfloat16):
    entries = deviation * jax.random.normal(stream_key, dims, jnp.float32)
    if shards:
        entries = entries * levels(stream_key, dims, shards, -0.22, 0.18)
    return jnp.clip(entries, -most, most).astype(dtype)


def setup_inputs(seed: int = 0) -> dict:
    key_list = jax.random.split(jax.random.key(seed), 8)
    return {
        "gate_hidden_input": normal_values(key_list[0], (TOKENS, MODEL_WIDTH), 1.0, 6.0, ((0, 256),)),
        "output_gradient": normal_values(key_list[1], (TOKENS, MODEL_WIDTH), 1.0, 6.0, ((0, 256),)),
        "attention_mixture": normal_values(key_list[2], (TOKENS, QUERY_FEATURES), 1.0, 6.0, ((0, 16), (1, 16))),
        "output_matrix": normal_values(key_list[3], (QUERY_FEATURES, MODEL_WIDTH), QUERY_FEATURES ** -0.5, 0.09375, ((0, 16),)),
        "adapter_down_weight": normal_values(key_list[4], (QUERY_FEATURES, STACKED_RANK), QUERY_FEATURES ** -0.5, 0.09375, ((0, 16),)),
        "adapter_up_weight": normal_values(key_list[5], (STACKED_RANK, MODEL_WIDTH), ADAPTER_RANK ** -0.5, 1.5),
        "gate_matrix": normal_values(key_list[6], (ADAPTER_COUNT, MODEL_WIDTH), MODEL_WIDTH ** -0.5, 0.09375),
    }


def reference(gate_hidden_input, output_gradient, attention_mixture, output_matrix, adapter_down_weight, adapter_up_weight, gate_matrix):
    logits = jnp.einsum("td,kd->tk", gate_hidden_input, gate_matrix, preferred_element_type=jnp.float32)
    gates = jax.nn.sigmoid(logits)
    rank_activation = jnp.dot(attention_mixture, adapter_down_weight, preferred_element_type=jnp.float32)
    backward_pass = jnp.einsum("kw,vw->kv", output_gradient, adapter_up_weight, preferred_element_type=jnp.float32)
    adapter_tally = gates.shape[0]
    gate_delta = 2.0 * jnp.sum((rank_activation * backward_pass).reshape(adapter_tally, ADAPTER_COUNT, ADAPTER_RANK), axis=2)
    dlogit = gate_delta * gates * (1.0 - gates)
    gate_grad = jnp.dot(dlogit.T, gate_hidden_input.astype(jnp.float32), precision=lax.Precision.HIGHEST)
    blended_output = (2.0 * jnp.repeat(gates, ADAPTER_RANK, axis=1) * backward_pass).astype(jnp.bfloat16)
    base_offset = jnp.einsum("td,qd->tq", output_gradient, output_matrix, preferred_element_type=jnp.float32)
    adapter_index = jnp.einsum("ux,ix->ui", blended_output, adapter_down_weight, preferred_element_type=jnp.float32)
    attention_gradient = (base_offset + adapter_index).astype(jnp.bfloat16)
    return gate_grad, attention_gradient
```

```python
import jax
import jax.numpy as jnp
from jax import lax
from jax.sharding import Mesh
from jax.sharding import PartitionSpec as P

F32 = jnp.float32
BF16 = jnp.bfloat16
AXES = ("x", "zl", "y", "zh", "c")


def shift(value, axis, by):
    size = lax.axis_size(axis)
    return lax.ppermute(value, axis, [(i, (i + by) % size) for i in range(size)])


def swap(value, axis, mask):
    size = lax.axis_size(axis)
    return lax.ppermute(value, axis, [(i, i ^ mask) for i in range(size)])


def dot_t(left, right):
    return lax.dot_general(left, right, (((1,), (1,)), ((), ())), preferred_element_type=F32)


def ring_gather(piece, axis):
    half = piece.shape[0] // 2
    low = shift(piece, axis, 1)
    high = shift(piece, axis, -1)
    far_top = shift(low[:half], axis, 1)
    far_bottom = shift(high[half:], axis, -1)
    return low, high, far_top, far_bottom


def on_device(hidden, grad, mixture, weight, down, up, gate_matrix):
    tokens, width = grad.shape
    adapters = gate_matrix.shape[0]
    stacked = up.shape[0]
    rank = stacked // adapters
    features = weight.shape[0]
    x, y, zh, c = (lax.axis_index(a) for a in ("x", "y", "zh", "c"))

    quarter = features // 4
    mine = jnp.concatenate(
        [
            lax.dynamic_slice_in_dim(weight, x * quarter, quarter, 0),
            lax.dynamic_slice_in_dim(down, x * quarter, quarter, 0),
        ],
        axis=1,
    )
    far_piece = swap(mine, "zh", 1)

    partial = jnp.dot(mixture, down, preferred_element_type=F32).reshape(4, 2, 2, tokens, stacked)
    keep = lax.dynamic_index_in_dim(partial, c, 2, keepdims=False)
    give = lax.dynamic_index_in_dim(partial, 1 - c, 2, keepdims=False)
    act = keep + swap(give.astype(BF16), "c", 1).astype(F32)
    pick = lambda m: lax.dynamic_index_in_dim(act, y ^ m, 0, keepdims=False).astype(BF16)
    act = (lax.dynamic_index_in_dim(act, y, 0, keepdims=False) + swap(pick(1), "y", 1).astype(F32)) + (
        swap(pick(2), "y", 2).astype(F32) + swap(pick(3), "y", 3).astype(F32)
    )
    keep = lax.dynamic_index_in_dim(act, zh, 0, keepdims=False)
    give = lax.dynamic_index_in_dim(act, 1 - zh, 0, keepdims=False)
    rank_act = keep + swap(give.astype(BF16), "zh", 1).astype(F32)

    gates = jax.nn.sigmoid(dot_t(hidden, gate_matrix))
    back = dot_t(grad, up)
    mixed = (2.0 * jnp.repeat(gates, rank, axis=1) * back).astype(BF16)
    mixed_all = lax.all_gather(mixed, ("y", "c"), axis=0, tiled=True)

    gate_delta = 2.0 * jnp.sum((rank_act * back).reshape(tokens, adapters, rank), axis=2)
    dlogit = gate_delta * gates * (1.0 - gates)
    total = jnp.dot(dlogit.T, hidden.astype(F32), precision=lax.Precision.HIGHEST)
    half = width // 2
    total = lax.dynamic_slice_in_dim(total, c * half, half, 1) + swap(
        lax.dynamic_slice_in_dim(total, (1 - c) * half, half, 1), "c", 1
    )
    for axis, mask in (("x", 1), ("x", 2), ("y", 1), ("y", 2), ("zl", 1), ("zl", 2), ("zh", 1)):
        total = total + swap(total, axis, mask)
    other = swap(total, "c", 1)
    gate_grad = jnp.where(
        c == 0, jnp.concatenate([total, other], axis=1), jnp.concatenate([other, total], axis=1)
    )

    low, high, far_top, far_bottom = ring_gather(grad, "y")
    every = jnp.zeros((4, 2, tokens, width), BF16)
    for step, at, block in (
        (0, 0, grad),
        (3, 0, low),
        (1, 0, high),
        (2, 0, far_top),
        (2, tokens // 2, far_bottom),
    ):
        where = (y + step) % 4
        every = lax.dynamic_update_slice(every, block[None, None], (where, c, at, 0))
        every = lax.dynamic_update_slice(every, swap(block, "c", 1)[None, None], (where, 1 - c, at, 0))
    every = every.reshape(8 * tokens, width)

    low, high, far_top, far_bottom = ring_gather(far_piece, "x")
    far_weight = jnp.zeros((4, quarter, width + stacked), BF16)
    for step, at, block in (
        (0, 0, far_piece),
        (3, 0, low),
        (1, 0, high),
        (2, 0, far_top),
        (2, quarter // 2, far_bottom),
    ):
        far_weight = lax.dynamic_update_slice(far_weight, block[None], ((x + step) % 4, at, 0))
    far_weight = far_weight.reshape(features, width + stacked)

    far_out = (
        dot_t(every, far_weight[:, :width]) + dot_t(mixed_all, far_weight[:, width:])
    ).astype(BF16)
    own_out = (dot_t(every, weight) + dot_t(mixed_all, down)).astype(BF16)
    got = swap(far_out, "zh", 1)
    own_out, got = (v.reshape(4, 1, 2 * tokens, features) for v in (own_out, got))
    out = jnp.where(
        zh == 0, jnp.concatenate([own_out, got], axis=1), jnp.concatenate([got, own_out], axis=1)
    )
    return gate_grad, out.reshape(16 * tokens, features)


def solution(mesh):
    grid = Mesh(mesh.devices.reshape(4, 4, 4, 2, 2), AXES)
    dp, tensor = ("x", "zl"), ("y", "zh", "c")
    return jax.shard_map(
        on_device,
        mesh=grid,
        in_specs=(
            P(AXES, None),
            P(AXES, None),
            P(dp, tensor),
            P(tensor, None),
            P(tensor, None),
            P(),
            P(),
        ),
        out_specs=(P(), P(dp, tensor)),
        check_vma=False,
    )
```

```python
import functools

import jax
import jax.numpy as jnp
from jax import lax
from jax.experimental import pallas as pl
from jax.experimental.pallas import tpu as pltpu
from jax.sharding import Mesh
from jax.sharding import PartitionSpec as P

F32 = jnp.float32
BF16 = jnp.bfloat16
AXES = ("x", "zl", "y", "zh", "c")
VMEM = pl.BlockSpec(memory_space=pltpu.VMEM)
SMEM = pl.BlockSpec(memory_space=pltpu.SMEM)
ANY = pl.BlockSpec(memory_space=pl.ANY)
PARAMS = pltpu.CompilerParams(vmem_limit_bytes=48 * 1024 * 1024)


def shift(value, axis, by):
    size = lax.axis_size(axis)
    return lax.ppermute(value, axis, [(i, (i + by) % size) for i in range(size)])


def swap(value, axis, mask):
    size = lax.axis_size(axis)
    return lax.ppermute(value, axis, [(i, i ^ mask) for i in range(size)])


def dot_t(left, right, precision=None):
    return lax.dot_general(
        left, right, (((1,), (1,)), ((), ())), precision=precision, preferred_element_type=F32
    )


def shaped(shape, dtype):
    return jax.ShapeDtypeStruct(shape, dtype)


def cost(flops, moved):
    return pl.CostEstimate(flops=flops, bytes_accessed=moved, transcendentals=0)


def membership(adapters, stacked):
    row = lax.broadcasted_iota(jnp.int32, (adapters, stacked), 0)
    column = lax.broadcasted_iota(jnp.int32, (adapters, stacked), 1)
    low = row * (stacked // adapters)
    return jnp.where((column >= low) & (column < low + stacked // adapters), 1.0, 0.0)


def token_kernel(at, hidden, grad, up, gate, weight, down, tokens_out, piece, gates, back, sems):
    width = grad.shape[1]
    stacked = up.shape[0]
    quarter = piece.shape[0]
    rows = pl.ds(pl.multiple_of(at[0] * quarter, quarter), quarter)
    copies = [
        pltpu.make_async_copy(weight.at[rows], piece.at[:, pl.ds(0, width)], sems.at[0]),
        pltpu.make_async_copy(down.at[rows], piece.at[:, pl.ds(width, stacked)], sems.at[1]),
    ]
    for copy in copies:
        copy.start()
    ones = membership(gate.shape[0], stacked)
    gates[...] = jax.nn.sigmoid(dot_t(gate[...], hidden[...]))
    wide = lax.dot_general(
        ones.astype(BF16), gate[...], (((0,), (0,)), ((), ())), preferred_element_type=F32
    ).astype(BF16)
    pulled = dot_t(grad[...], up[...])
    back[...] = pulled
    mixed = 2.0 * jax.nn.sigmoid(dot_t(hidden[...], wide)) * pulled
    tokens_out[:, pl.ds(0, width)] = grad[...]
    tokens_out[:, pl.ds(width, stacked)] = mixed.astype(BF16)
    for copy in copies:
        copy.wait()


def act_kernel(at, mixture, down, tie, keep, give):
    c = at[3]
    blocks, _, tokens, depth = mixture.shape
    for out, side in ((give, 1 - c), (keep, c)):
        rows = mixture[:, side].reshape(blocks * tokens, depth)
        value = jnp.dot(rows, down[...], preferred_element_type=F32)
        out[...] = value.reshape(out.shape).astype(out.dtype)


def act_y_kernel(at, keep, got, first, second, third, rest):
    y = at[1]
    for out, mask in ((first, 1), (second, 2), (third, 3), (rest, 0)):
        row = jnp.bitwise_xor(y, mask)
        out[...] = (keep[row] + got[row].astype(F32)).astype(out.dtype)


def act_z_kernel(at, rest, first, second, third, keep, give):
    zh = at[2]
    for out, side in ((give, 1 - zh), (keep, zh)):
        total = (rest[side] + first[side].astype(F32)) + (
            second[side].astype(F32) + third[side].astype(F32)
        )
        out[...] = total.astype(out.dtype)


def gate_kernel(at, keep, got, back, gates, hidden, result, give):
    stacked = keep.shape[1]
    adapters = gates.shape[0]
    half = result.shape[1]
    product = (keep[...] + got[...].astype(F32)) * back[...]
    ones = membership(adapters, stacked)
    delta = 2.0 * dot_t(ones, product, lax.Precision.HIGHEST)
    dlogit = delta * gates[...] * (1.0 - gates[...])
    top = dlogit.astype(BF16).astype(F32)
    middle = (dlogit - top).astype(BF16).astype(F32)
    parts = jnp.concatenate([top, middle, dlogit - top - middle], axis=0).astype(BF16)
    c = at[3]
    for out, side in ((result, c), (give, 1 - c)):
        columns = pl.ds(pl.multiple_of(side * half, 128), half)
        total = jnp.dot(parts, hidden[:, columns], preferred_element_type=F32)
        out[...] = total[:adapters] + (
            total[adapters : 2 * adapters] + total[2 * adapters :]
        )


def gather_tokens(at, refs, held, sems):
    own, own_s, low, low_s, high, high_s, top, top_s, bottom, bottom_s = refs
    y, c = at[1], at[3]
    half = top.shape[0]
    full = pl.ds(0, own.shape[0])
    plan = (
        (0, ((own, c, full), (own_s, 1 - c, full))),
        (3, ((low, c, full), (low_s, 1 - c, full))),
        (1, ((high, c, full), (high_s, 1 - c, full))),
        (
            2,
            (
                (top, c, pl.ds(0, half)),
                (top_s, 1 - c, pl.ds(0, half)),
                (bottom, c, pl.ds(half, half)),
                (bottom_s, 1 - c, pl.ds(half, half)),
            ),
        ),
    )
    out, number = [], 0
    for step, parts in plan:
        row = lax.rem(y + step, 4)
        copies = []
        for ref, core, rows in parts:
            copies.append(pltpu.make_async_copy(ref, held.at[row, core, rows], sems.at[number]))
            copies[-1].start()
            number += 1
        out.append((row, copies))
    return out


def products(steps, held, weights, out):
    depth = held.shape[3]
    rows = held.shape[1] * held.shape[2]
    for row, copies in steps:
        for copy in copies:
            copy.wait()
        value = dot_t(held[row].reshape(rows, depth), weights())
        out[row] = value.astype(out.dtype)


def far_kernel(at, *refs):
    blocks, (piece, low, high, top, bottom), (out, held, weight, sems, weight_sems) = (
        refs[:10],
        refs[10:15],
        refs[15:],
    )
    x = at[0]
    half = top.shape[0]
    full = pl.ds(0, piece.shape[0])
    copies = []
    for number, (step, ref, rows) in enumerate(
        (
            (0, piece, full),
            (3, low, full),
            (1, high, full),
            (2, top, pl.ds(0, half)),
            (2, bottom, pl.ds(half, half)),
        )
    ):
        copies.append(
            pltpu.make_async_copy(
                ref, weight.at[lax.rem(x + step, 4), rows], weight_sems.at[number]
            )
        )
        copies[-1].start()
    steps = gather_tokens(at, blocks, held, sems)
    for copy in copies:
        copy.wait()
    depth = weight.shape[2]
    products(steps, held, lambda: weight[...].reshape(-1, depth), out)


def own_kernel(at, *refs):
    blocks, (first, second), (out, held, weight, result, sems, weight_sems) = (
        refs[:10],
        refs[10:12],
        refs[13:],
    )
    width = first.shape[1]
    copies = [
        pltpu.make_async_copy(first, weight.at[:, pl.ds(0, width)], weight_sems.at[0]),
        pltpu.make_async_copy(
            second, weight.at[:, pl.ds(width, second.shape[1])], weight_sems.at[1]
        ),
    ]
    for copy in copies:
        copy.start()
    steps = gather_tokens(at, blocks, held, sems)
    for copy in copies:
        copy.wait()
    products(steps, held, lambda: weight[...], result)
    copy = pltpu.make_async_copy(result, out.at[:, at[2]], weight_sems.at[2])
    copy.start()
    copy.wait()


def ring_gather(piece, axis):
    half = piece.shape[0] // 2
    low = shift(piece, axis, 1)
    high = shift(piece, axis, -1)
    return low, high, shift(low[:half], axis, 1), shift(high[half:], axis, -1)


def on_device(hidden, grad, mixture, weight, down, up, gate_matrix):
    tokens, width = grad.shape
    adapters = gate_matrix.shape[0]
    stacked = up.shape[0]
    features = weight.shape[0]
    depth = width + stacked
    quarter = features // 4
    at = jnp.stack([lax.axis_index(a) for a in ("x", "y", "zh", "c")]).astype(jnp.int32)
    c, zh = at[3], at[2]

    own, piece, gates, back = pl.pallas_call(
        token_kernel,
        in_specs=[SMEM, VMEM, VMEM, VMEM, VMEM, ANY, ANY],
        out_specs=[VMEM, ANY, VMEM, VMEM],
        out_shape=[
            shaped((tokens, depth), BF16),
            shaped((quarter, depth), BF16),
            shaped((adapters, tokens), F32),
            shaped((tokens, stacked), F32),
        ],
        scratch_shapes=[pltpu.SemaphoreType.DMA((2,))],
        compiler_params=PARAMS,
        cost_estimate=cost(6 * tokens * width * stacked, 12 * tokens * width),
        name="token_values",
    )(at, hidden, grad, up, gate_matrix, weight, down)

    far_piece = swap(piece, "zh", 1)
    low, high, top, bottom = ring_gather(own, "y")
    blocks = []
    for block in (own, low, high, top, bottom):
        blocks += [block, swap(block, "c", 1)]

    keep, give = pl.pallas_call(
        act_kernel,
        in_specs=[SMEM, VMEM, VMEM, ANY],
        out_specs=[VMEM, VMEM],
        out_shape=[
            shaped((4, 2, tokens, stacked), F32),
            shaped((4, 2, tokens, stacked), BF16),
        ],
        compiler_params=PARAMS,
        cost_estimate=cost(2 * mixture.size * stacked, 4 * mixture.size),
        name="rank_products",
    )(at, mixture.reshape(8, 2, tokens, -1), down, own)
    first, second, third, rest = pl.pallas_call(
        act_y_kernel,
        in_specs=[SMEM, VMEM, VMEM],
        out_specs=[VMEM] * 4,
        out_shape=[shaped((2, tokens, stacked), BF16)] * 3 + [shaped((2, tokens, stacked), F32)],
        compiler_params=PARAMS,
        name="rank_sum_core",
    )(at, keep, swap(give, "c", 1))
    keep, give = pl.pallas_call(
        act_z_kernel,
        in_specs=[SMEM] + [VMEM] * 4,
        out_specs=[VMEM, VMEM],
        out_shape=[shaped((tokens, stacked), F32), shaped((tokens, stacked), BF16)],
        compiler_params=PARAMS,
        name="rank_sum_y",
    )(at, rest, swap(first, "y", 1), swap(second, "y", 2), swap(third, "y", 3))

    total, give = pl.pallas_call(
        gate_kernel,
        in_specs=[SMEM] + [VMEM] * 5,
        out_specs=[VMEM, VMEM],
        out_shape=[shaped((adapters, width // 2), F32)] * 2,
        compiler_params=PARAMS,
        name="gate_products",
    )(at, keep, swap(give, "zh", 1), back, gates, hidden)
    total = total + swap(give, "c", 1)
    for axis, mask in (("x", 1), ("x", 2), ("y", 1), ("y", 2), ("zl", 1), ("zl", 2), ("zh", 1)):
        total = total + swap(total, axis, mask)
    other = swap(total, "c", 1)
    gate_grad = jnp.where(
        c == 0, jnp.concatenate([total, other], axis=1), jnp.concatenate([other, total], axis=1)
    )

    held = pltpu.VMEM((4, 2, tokens, depth), BF16)
    matmul_cost = cost(16 * tokens * depth * features, 24 * tokens * depth)
    far = pl.pallas_call(
        far_kernel,
        in_specs=[SMEM] + [ANY] * 15,
        out_specs=VMEM,
        out_shape=shaped((4, 2 * tokens, features), BF16),
        scratch_shapes=[
            held,
            pltpu.VMEM((4, quarter, depth), BF16),
            pltpu.SemaphoreType.DMA((10,)),
            pltpu.SemaphoreType.DMA((5,)),
        ],
        compiler_params=PARAMS,
        cost_estimate=matmul_cost,
        name="far_products",
    )(at, *blocks, far_piece, *ring_gather(far_piece, "x"))
    got = swap(far, "zh", 1)
    out = pl.pallas_call(
        own_kernel,
        in_specs=[SMEM] + [ANY] * 13,
        out_specs=ANY,
        out_shape=shaped((4, 2, 2 * tokens, features), BF16),
        scratch_shapes=[
            held,
            pltpu.VMEM((features, depth), BF16),
            pltpu.VMEM((4, 2 * tokens, features), BF16),
            pltpu.SemaphoreType.DMA((10,)),
            pltpu.SemaphoreType.DMA((3,)),
        ],
        compiler_params=PARAMS,
        cost_estimate=matmul_cost,
        name="own_products",
    )(at, *blocks, weight, down, far)
    out = lax.dynamic_update_slice(out, got[:, None], (0, 1 - zh, 0, 0))
    return gate_grad, out.reshape(16 * tokens, features)


def solution(mesh):
    grid = Mesh(mesh.devices.reshape(4, 4, 4, 2, 2), AXES)
    dp, tensor = ("x", "zl"), ("y", "zh", "c")
    return jax.shard_map(
        on_device,
        mesh=grid,
        in_specs=(
            P(AXES, None),
            P(AXES, None),
            P(dp, tensor),
            P(tensor, None),
            P(tensor, None),
            P(),
            P(),
        ),
        out_specs=(P(), P(dp, tensor)),
        check_vma=False,
    )
```

```python
import jax
import jax.numpy as jnp
from jax import lax
from jax.experimental import pallas as pl
from jax.experimental.pallas import tpu as pltpu
from jax.sharding import Mesh
from jax.sharding import PartitionSpec as P

F32 = jnp.float32
BF16 = jnp.bfloat16
AXES = ("x", "zl", "y", "zh", "c")
VMEM = pl.BlockSpec(memory_space=pltpu.VMEM)
SMEM = pl.BlockSpec(memory_space=pltpu.SMEM)
ANY = pl.BlockSpec(memory_space=pl.ANY)
HBM = pl.BlockSpec(memory_space=pltpu.HBM)
LARGE = pltpu.CompilerParams(vmem_limit_bytes=48 * 1024 * 1024)


def ring(value, axis):
    size = lax.axis_size(axis)
    pairs = [
        (2 * i + c, 2 * ((i + 1 - 2 * c) % size) + c) for i in range(size) for c in range(2)
    ]
    return lax.ppermute(value, (axis, "c"), pairs)


def fence_kernel(*refs):
    del refs


def fence(values, *ties):
    return pl.pallas_call(
        fence_kernel,
        in_specs=[HBM] * len(values) + [ANY] * len(ties),
        out_specs=[HBM] * len(values),
        out_shape=[shaped(v.shape, v.dtype) for v in values],
        input_output_aliases={i: i for i in range(len(values))},
        name="fence",
    )(*values, *ties)


def back_at(place, core, steps):
    return lax.rem(place - steps * (1 - 2 * core) + 4, 4)


def swap(value, axis, mask):
    size = lax.axis_size(axis)
    return lax.ppermute(value, axis, [(i, i ^ mask) for i in range(size)])


def dot_t(left, right, precision=None):
    return lax.dot_general(
        left, right, (((1,), (1,)), ((), ())), precision=precision, preferred_element_type=F32
    )


def shaped(shape, dtype):
    return jax.ShapeDtypeStruct(shape, dtype)


def cost(flops, moved):
    return pl.CostEstimate(flops=flops, bytes_accessed=moved, transcendentals=0)


def membership(adapters, stacked):
    row = lax.broadcasted_iota(jnp.int32, (adapters, stacked), 0)
    column = lax.broadcasted_iota(jnp.int32, (adapters, stacked), 1)
    low = row * (stacked // adapters)
    return jnp.where((column >= low) & (column < low + stacked // adapters), 1.0, 0.0)


def run(copies):
    for copy in copies:
        copy.start()
    for copy in copies:
        copy.wait()


def split_kernel(at, weight, down, piece, sems):
    width = weight.shape[1]
    quarter = piece.shape[0]
    rows = pl.ds(pl.multiple_of(at[0] * quarter, quarter), quarter)
    run(
        [
            pltpu.make_async_copy(weight.at[rows], piece.at[:, pl.ds(0, width)], sems.at[0]),
            pltpu.make_async_copy(
                down.at[rows], piece.at[:, pl.ds(width, down.shape[1])], sems.at[1]
            ),
        ]
    )


def token_kernel(at, hidden, grad, up, gate, mixed, gates, back, grad_in, up_in, sems):
    stacked = up.shape[0]
    copies = [
        pltpu.make_async_copy(grad, grad_in, sems.at[0]),
        pltpu.make_async_copy(up, up_in, sems.at[1]),
    ]
    for copy in copies:
        copy.start()
    ones = membership(gate.shape[0], stacked)
    gates[...] = jax.nn.sigmoid(dot_t(gate[...], hidden[...]))
    wide = lax.dot_general(
        ones.astype(BF16), gate[...], (((0,), (0,)), ((), ())), preferred_element_type=F32
    ).astype(BF16)
    factor = 2.0 * jax.nn.sigmoid(dot_t(hidden[...], wide))
    for copy in copies:
        copy.wait()
    pulled = dot_t(grad_in[...], up_in[...])
    back[...] = pulled
    mixed[...] = (factor * pulled).astype(BF16)


def act_kernel(at, mixture, down, keep, give, rows_in, down_in, sems):
    c = at[3]
    blocks, _, tokens, depth = mixture.shape
    copies = [
        pltpu.make_async_copy(down, down_in, sems.at[0]),
        pltpu.make_async_copy(mixture.at[:, 1 - c], rows_in.at[0], sems.at[1]),
        pltpu.make_async_copy(mixture.at[:, c], rows_in.at[1], sems.at[2]),
    ]
    for copy in copies:
        copy.start()
    copies[0].wait()
    for out, side in ((give, 0), (keep, 1)):
        copies[1 + side].wait()
        rows = rows_in[side].reshape(blocks * tokens, depth)
        value = jnp.dot(rows, down_in[...], preferred_element_type=F32)
        out[...] = value.reshape(out.shape).astype(out.dtype)


def act_y_kernel(at, keep, got, mixed, first, second, third, rest):
    y = at[1]
    for out, mask in ((first, 1), (second, 2), (third, 3)):
        row = jnp.bitwise_xor(y, mask)
        out[pl.ds(0, 2)] = (keep[row] + got[row].astype(F32)).astype(out.dtype)
        out[2] = mixed[...]
    rest[...] = keep[y] + got[y].astype(F32)


def act_z_kernel(at, rest, first, second, third, mixed, keep, give, all_mixed):
    y, zh = at[1], at[2]
    for out, side in ((give, 1 - zh), (keep, zh)):
        total = (rest[side] + first[side].astype(F32)) + (
            second[side].astype(F32) + third[side].astype(F32)
        )
        out[...] = total.astype(out.dtype)
    all_mixed[y] = mixed[...]
    for ref, mask in ((first, 1), (second, 2), (third, 3)):
        all_mixed[jnp.bitwise_xor(y, mask)] = ref[2]


def gate_kernel(at, keep, got, back, gates, hidden, result, give):
    stacked = keep.shape[1]
    adapters = gates.shape[0]
    half = result.shape[1]
    product = (keep[...] + got[...].astype(F32)) * back[...]
    ones = membership(adapters, stacked)
    delta = 2.0 * dot_t(ones, product, lax.Precision.HIGHEST)
    dlogit = delta * gates[...] * (1.0 - gates[...])
    top = dlogit.astype(BF16).astype(F32)
    middle = (dlogit - top).astype(BF16).astype(F32)
    parts = jnp.concatenate([top, middle, dlogit - top - middle], axis=0).astype(BF16)
    c = at[3]
    for out, side in ((result, c), (give, 1 - c)):
        columns = pl.ds(pl.multiple_of(side * half, 128), half)
        total = jnp.dot(parts, hidden[:, columns], preferred_element_type=F32)
        out[...] = total[:adapters] + (
            total[adapters : 2 * adapters] + total[2 * adapters :]
        )


def add_kernel(left, right, *refs):
    refs[-1][...] = left[...] + right[...]


def add4_kernel(first, second, third, fourth, *refs):
    refs[-1][...] = (first[...] + second[...]) + (third[...] + fourth[...])


def rows_product(at, steps, refs, mixed, weights, downs, out):
    y, c = at[1], at[3]
    both = jnp.concatenate([ref[...] for ref in refs], axis=0)
    ranks = jnp.concatenate(
        [mixed[0][back_at(y, c, steps)], mixed[1][back_at(y, 1 - c, steps)]], axis=0
    )
    value = dot_t(both, weights[...]) + dot_t(ranks, downs[...])
    out[...] = value.astype(out.dtype)


def far_kernel(at, own, own_s, one, one_s, two, two_s, mixed, mixed_s, *refs):
    pieces, (out, weight, down) = refs[:4], refs[4:]
    width = weight.shape[1]
    rows = pieces[0].shape[0]
    for steps, ref in enumerate(pieces):
        place = pl.ds(pl.multiple_of(back_at(at[0], at[3], steps) * rows, rows), rows)
        weight[place, :] = ref[:, :width]
        down[place, :] = ref[:, width:]
    for steps, group in enumerate(((own, own_s), (one, one_s), (two, two_s))):
        rows_product(at, steps, group, (mixed, mixed_s), weight, down, out.at[steps])


def far_last_kernel(at, three, three_s, mixed, mixed_s, weight, down, out):
    rows_product(at, 3, (three, three_s), (mixed, mixed_s), weight, down, out)


def own_kernel(
    at, own, own_s, one, one_s, two, two_s, three, three_s, mixed, mixed_s, weight, down, tie, out
):
    groups = ((own, own_s), (one, one_s), (two, two_s), (three, three_s))
    for steps, group in enumerate(groups):
        rows_product(at, steps, group, (mixed, mixed_s), weight, down, out.at[steps])


def place_kernel(at, own, got, last, out, sems):
    y, zh, c = at[1], at[2], at[3]
    tokens = out.shape[3]
    copies = []
    for steps in range(4):
        other = got.at[steps] if steps < 3 else last
        for ref, side in ((own.at[steps], zh), (other, 1 - zh)):
            for half, core in ((0, c), (1, 1 - c)):
                copies.append(
                    pltpu.make_async_copy(
                        ref.at[pl.ds(half * tokens, tokens)],
                        out.at[back_at(y, core, steps), side, core],
                        sems.at[len(copies)],
                    )
                )
    run(copies)


def on_device(hidden, grad, mixture, weight, down, up, gate_matrix):
    tokens, width = grad.shape
    adapters = gate_matrix.shape[0]
    stacked = up.shape[0]
    features = weight.shape[0]
    depth = width + stacked
    quarter = features // 4
    at = jnp.stack([lax.axis_index(a) for a in ("x", "y", "zh", "c")]).astype(jnp.int32)
    c, zh = at[3], at[2]

    piece = pl.pallas_call(
        split_kernel,
        in_specs=[SMEM, HBM, HBM],
        out_specs=HBM,
        out_shape=shaped((quarter, depth), BF16),
        scratch_shapes=[pltpu.SemaphoreType.DMA((2,))],
        name="split",
    )(at, weight, down)
    with jax.named_scope("weight_z"):
        far_piece = swap(piece, "zh", 1)
    with jax.named_scope("tokens_y"):
        one = ring(grad, "y")

    keep, give = pl.pallas_call(
        act_kernel,
        in_specs=[SMEM, HBM, HBM],
        out_specs=[VMEM, VMEM],
        out_shape=[
            shaped((4, 2, tokens, stacked), F32),
            shaped((4, 2, tokens, stacked), BF16),
        ],
        scratch_shapes=[
            pltpu.VMEM((2, 8, tokens, features), BF16),
            pltpu.VMEM((features, stacked), BF16),
            pltpu.SemaphoreType.DMA((3,)),
        ],
        compiler_params=LARGE,
        cost_estimate=cost(2 * mixture.size * stacked, 4 * mixture.size),
        name="rank_products",
    )(at, mixture.reshape(8, 2, tokens, -1), down)
    with jax.named_scope("act_core"):
        got = swap(give, "c", 1)
    mixed, gates, back = pl.pallas_call(
        token_kernel,
        in_specs=[SMEM, VMEM, HBM, HBM, VMEM],
        out_specs=[VMEM, VMEM, VMEM],
        out_shape=[
            shaped((tokens, stacked), BF16),
            shaped((adapters, tokens), F32),
            shaped((tokens, stacked), F32),
        ],
        scratch_shapes=[
            pltpu.VMEM((tokens, width), BF16),
            pltpu.VMEM((stacked, width), BF16),
            pltpu.SemaphoreType.DMA((2,)),
        ],
        compiler_params=LARGE,
        cost_estimate=cost(6 * tokens * width * stacked, 12 * tokens * width),
        name="token_values",
    )(at, hidden, grad, up, gate_matrix)
    first, second, third, rest = pl.pallas_call(
        act_y_kernel,
        in_specs=[SMEM, VMEM, VMEM, VMEM],
        out_specs=[VMEM] * 4,
        out_shape=[shaped((3, tokens, stacked), BF16)] * 3 + [shaped((2, tokens, stacked), F32)],
        name="rank_sum_core",
    )(at, keep, got, mixed)
    with jax.named_scope("act_y"):
        first, second, third = (
            swap(v, "y", mask) for v, mask in ((first, 1), (second, 2), (third, 3))
        )
    keep, give, all_mixed = pl.pallas_call(
        act_z_kernel,
        in_specs=[SMEM] + [VMEM] * 5,
        out_specs=[VMEM] * 3,
        out_shape=[
            shaped((tokens, stacked), F32),
            shaped((tokens, stacked), BF16),
            shaped((4, tokens, stacked), BF16),
        ],
        name="rank_sum_y",
    )(at, rest, first, second, third, mixed)
    one, far_piece = fence((one, far_piece), give)
    with jax.named_scope("tokens_y"):
        two = ring(one, "y")
    with jax.named_scope("weight_x"):
        w_one = ring(far_piece, "x")
    with jax.named_scope("act_z"):
        got = swap(give, "zh", 1)
    with jax.named_scope("mixed_core"):
        mixed_s = swap(all_mixed, "c", 1)
    with jax.named_scope("tokens_core"):
        own_s, one_s = swap(grad, "c", 1), swap(one, "c", 1)

    total, give = pl.pallas_call(
        gate_kernel,
        in_specs=[SMEM] + [VMEM] * 5,
        out_specs=[VMEM, VMEM],
        out_shape=[shaped((adapters, width // 2), F32)] * 2,
        name="gate_products",
    )(at, keep, got, back, gates, hidden)

    def add(left, right, *ties):
        return pl.pallas_call(
            add_kernel,
            in_specs=[VMEM, VMEM] + [ANY] * len(ties),
            out_specs=VMEM,
            out_shape=shaped(left.shape, F32),
            name="gate_sum",
        )(left, right, *ties)

    def add4(*parts):
        return pl.pallas_call(
            add4_kernel,
            in_specs=[VMEM] * 4 + [ANY] * (len(parts) - 4),
            out_specs=VMEM,
            out_shape=shaped(parts[0].shape, F32),
            name="gate_sum",
        )(*parts)

    def step(total, axis, *ties):
        with jax.named_scope("gate_" + axis):
            got = [swap(total, axis, mask) for mask in (1, 2, 3)]
        return add4(total, *got, *ties)

    with jax.named_scope("gate_core"):
        got = swap(give, "c", 1)
    total = add(total, got)
    (w_one,) = fence((w_one,), total)
    with jax.named_scope("weight_x"):
        w_two = ring(w_one, "x")
    total = step(total, "zl", w_one)
    (two,) = fence((two,), total)
    with jax.named_scope("tokens_y"):
        three = ring(two, "y")
    with jax.named_scope("gate_zh"):
        got = swap(total, "zh", 1)
    total = add(total, got, two)
    (w_two,) = fence((w_two,), total)
    with jax.named_scope("weight_x"):
        w_three = ring(w_two, "x")
    with jax.named_scope("tokens_core"):
        two_s, three_s = swap(two, "c", 1), swap(three, "c", 1)
    near = (grad, own_s, one, one_s, two, two_s)
    total = step(total, "x", w_two)

    far, far_weight, far_down = pl.pallas_call(
        far_kernel,
        in_specs=[SMEM] + [VMEM] * 12,
        out_specs=[VMEM] * 3,
        out_shape=[
            shaped((3, 2 * tokens, features), BF16),
            shaped((features, width), BF16),
            shaped((features, stacked), BF16),
        ],
        cost_estimate=cost(12 * tokens * depth * features, 18 * tokens * depth),
        name="far_products",
    )(at, *near, all_mixed, mixed_s, far_piece, w_one, w_two, w_three)
    with jax.named_scope("out_z"):
        far_got = swap(far, "zh", 1)

    last = pl.pallas_call(
        far_last_kernel,
        in_specs=[SMEM] + [VMEM] * 6,
        out_specs=VMEM,
        out_shape=shaped((2 * tokens, features), BF16),
        cost_estimate=cost(4 * tokens * depth * features, 6 * tokens * depth),
        name="far_products_last",
    )(at, three, three_s, all_mixed, mixed_s, far_weight, far_down)
    with jax.named_scope("out_z_last"):
        last_got = swap(last, "zh", 1)

    total = step(total, "y", far)
    with jax.named_scope("gate_core_back"):
        other = swap(total, "c", 1)
    gate_grad = jnp.where(
        c == 0, jnp.concatenate([total, other], axis=1), jnp.concatenate([other, total], axis=1)
    )

    own_out = pl.pallas_call(
        own_kernel,
        in_specs=[SMEM] + [VMEM] * 12 + [ANY],
        out_specs=VMEM,
        out_shape=shaped((4, 2 * tokens, features), BF16),
        cost_estimate=cost(16 * tokens * depth * features, 24 * tokens * depth),
        name="own_products",
    )(at, *near, three, three_s, all_mixed, mixed_s, weight, down, last)
    out = pl.pallas_call(
        place_kernel,
        in_specs=[SMEM, VMEM, VMEM, VMEM],
        out_specs=HBM,
        out_shape=shaped((4, 2, 2, tokens, features), BF16),
        scratch_shapes=[pltpu.SemaphoreType.DMA((16,))],
        name="place",
    )(at, own_out, far_got, last_got)
    return gate_grad, out.reshape(16 * tokens, features)


def solution(mesh):
    grid = Mesh(mesh.devices.reshape(4, 4, 4, 2, 2), AXES)
    dp, tensor = ("x", "zl"), ("y", "zh", "c")
    return jax.shard_map(
        on_device,
        mesh=grid,
        in_specs=(
            P(AXES, None),
            P(AXES, None),
            P(dp, tensor),
            P(tensor, None),
            P(tensor, None),
            P(),
            P(),
        ),
        out_specs=(P(), P(dp, tensor)),
        check_vma=False,
    )
```

```python
import jax
import jax.numpy as jnp
from jax import lax
from jax.experimental import pallas as pl
from jax.experimental.pallas import tpu as pltpu
from jax.sharding import Mesh
from jax.sharding import PartitionSpec as P

F32 = jnp.float32
BF16 = jnp.bfloat16
AXES = ("x", "zl", "y", "zh", "c")
VMEM = pl.BlockSpec(memory_space=pltpu.VMEM)
SMEM = pl.BlockSpec(memory_space=pltpu.SMEM)
ANY = pl.BlockSpec(memory_space=pl.ANY)
HBM = pl.BlockSpec(memory_space=pltpu.HBM)
SMALL = pltpu.CompilerParams(vmem_limit_bytes=8 * 1024 * 1024)
MIDDLE = pltpu.CompilerParams(vmem_limit_bytes=24 * 1024 * 1024)


def ring(value, axis):
    size = lax.axis_size(axis)
    pairs = [
        (2 * i + c, 2 * ((i + 1 - 2 * c) % size) + c) for i in range(size) for c in range(2)
    ]
    return lax.ppermute(value, (axis, "c"), pairs)


def pairs(value, axis, first):
    size = lax.axis_size(axis)
    partner = lambda i, c: i ^ 1 if (c == 0) == first else size - 1 - i
    return lax.ppermute(
        value, (axis, "c"), [(2 * i + c, 2 * partner(i, c) + c) for i in range(size) for c in range(2)]
    )


def fence_kernel(*refs):
    del refs


def fence(values, *ties):
    return pl.pallas_call(
        fence_kernel,
        in_specs=[ANY] * (len(values) + len(ties)),
        out_specs=[ANY] * len(values),
        out_shape=[shaped(v.shape, v.dtype) for v in values],
        input_output_aliases={i: i for i in range(len(values))},
        compiler_params=SMALL,
        name="fence",
    )(*values, *ties)


def back_at(place, core, steps):
    return lax.rem(place - steps * (1 - 2 * core) + 4, 4)


def swap(value, axis, mask):
    size = lax.axis_size(axis)
    return lax.ppermute(value, axis, [(i, i ^ mask) for i in range(size)])


def dot_t(left, right, precision=None):
    return lax.dot_general(
        left, right, (((1,), (1,)), ((), ())), precision=precision, preferred_element_type=F32
    )


def shaped(shape, dtype):
    return jax.ShapeDtypeStruct(shape, dtype)


def cost(flops, moved):
    return pl.CostEstimate(flops=flops, bytes_accessed=moved, transcendentals=0)


def membership(adapters, stacked):
    row = lax.broadcasted_iota(jnp.int32, (adapters, stacked), 0)
    column = lax.broadcasted_iota(jnp.int32, (adapters, stacked), 1)
    low = row * (stacked // adapters)
    return jnp.where((column >= low) & (column < low + stacked // adapters), 1.0, 0.0)


def run(copies):
    for copy in copies:
        copy.start()
    for copy in copies:
        copy.wait()


def split_kernel(at, weight, down, piece, sems):
    width = weight.shape[1]
    quarter = piece.shape[0]
    rows = pl.ds(pl.multiple_of(at[4] * quarter, quarter), quarter)
    run(
        [
            pltpu.make_async_copy(weight.at[rows], piece.at[:, pl.ds(0, width)], sems.at[0]),
            pltpu.make_async_copy(
                down.at[rows], piece.at[:, pl.ds(width, down.shape[1])], sems.at[1]
            ),
        ]
    )


def join_kernel(at, mine, got, tie, out):
    quarter = mine.shape[0]
    side = lax.rem(at[4], 2)
    for place, ref in ((side, mine), (1 - side, got)):
        out[pl.ds(pl.multiple_of(place * quarter, quarter), quarter), :] = ref[...]


def token_kernel(at, hidden, grad, up, gate, mixed, gates, back, hidden_in, grad_in, up_in, sems):
    stacked = up.shape[0]
    copies = [
        pltpu.make_async_copy(hidden, hidden_in, sems.at[0]),
        pltpu.make_async_copy(grad, grad_in, sems.at[1]),
        pltpu.make_async_copy(up, up_in, sems.at[2]),
    ]
    for copy in copies:
        copy.start()
    ones = membership(gate.shape[0], stacked)
    wide = lax.dot_general(
        ones.astype(BF16), gate[...], (((0,), (0,)), ((), ())), preferred_element_type=F32
    ).astype(BF16)
    copies[0].wait()
    gates[...] = jax.nn.sigmoid(dot_t(gate[...], hidden_in[...]))
    factor = 2.0 * jax.nn.sigmoid(dot_t(hidden_in[...], wide))
    for copy in copies[1:]:
        copy.wait()
    pulled = dot_t(grad_in[...], up_in[...])
    back[...] = pulled
    mixed[...] = (factor * pulled).astype(BF16)


def act_kernel(at, mixture, down, keep, give, rows_in, down_in, sems):
    c = at[3]
    blocks, _, tokens, depth = mixture.shape
    copies = [
        pltpu.make_async_copy(down, down_in, sems.at[0]),
        pltpu.make_async_copy(mixture.at[:, 1 - c], rows_in.at[0], sems.at[1]),
        pltpu.make_async_copy(mixture.at[:, c], rows_in.at[1], sems.at[2]),
    ]
    for copy in copies:
        copy.start()
    copies[0].wait()
    for out, side in ((give, 0), (keep, 1)):
        copies[1 + side].wait()
        rows = rows_in[side].reshape(blocks * tokens, depth)
        value = jnp.dot(rows, down_in[...], preferred_element_type=F32)
        out[...] = value.reshape(out.shape).astype(out.dtype)


def act_y_kernel(at, keep, got, mixed, first, second, third, rest):
    y = at[1]
    for out, mask in ((first, 1), (second, 2), (third, 3)):
        row = jnp.bitwise_xor(y, mask)
        out[pl.ds(0, 2)] = (keep[row] + got[row].astype(F32)).astype(out.dtype)
        out[2] = mixed[...]
    rest[...] = keep[y] + got[y].astype(F32)


def act_z_kernel(at, rest, first, second, third, mixed, tie, keep, give, all_mixed):
    y, zh = at[1], at[2]
    for out, side in ((give, 1 - zh), (keep, zh)):
        total = (rest[side] + first[side].astype(F32)) + (
            second[side].astype(F32) + third[side].astype(F32)
        )
        out[...] = total.astype(out.dtype)
    all_mixed[y] = mixed[...]
    for ref, mask in ((first, 1), (second, 2), (third, 3)):
        all_mixed[jnp.bitwise_xor(y, mask)] = ref[2]


def gate_kernel(at, keep, got, back, gates, hidden, result, give):
    stacked = keep.shape[1]
    adapters = gates.shape[0]
    half = result.shape[1]
    product = (keep[...] + got[...].astype(F32)) * back[...]
    ones = membership(adapters, stacked)
    delta = 2.0 * dot_t(ones, product, lax.Precision.HIGHEST)
    dlogit = delta * gates[...] * (1.0 - gates[...])
    top = dlogit.astype(BF16).astype(F32)
    middle = (dlogit - top).astype(BF16).astype(F32)
    parts = jnp.concatenate([top, middle, dlogit - top - middle], axis=0).astype(BF16)
    c = at[3]
    for out, side in ((result, c), (give, 1 - c)):
        columns = pl.ds(pl.multiple_of(side * half, 128), half)
        total = jnp.dot(parts, hidden[:, columns], preferred_element_type=F32)
        out[...] = total[:adapters] + (
            total[adapters : 2 * adapters] + total[2 * adapters :]
        )


def add_kernel(left, right, *refs):
    refs[-1][...] = left[...] + right[...]


def add4_kernel(first, second, third, fourth, *refs):
    refs[-1][...] = (first[...] + second[...]) + (third[...] + fourth[...])


def rows_product(at, steps, refs, mixed, weights, downs, out):
    y, c = at[1], at[3]
    both = jnp.concatenate([ref[...] for ref in refs], axis=0)
    ranks = jnp.concatenate(
        [mixed[0][back_at(y, c, steps)], mixed[1][back_at(y, 1 - c, steps)]], axis=0
    )
    value = dot_t(both, weights[...]) + dot_t(ranks, downs[...])
    out[...] = value.astype(out.dtype)


def far_kernel(at, own, own_s, one, one_s, two, two_s, mixed, mixed_s, mine, got, tie, out, weight, down):
    width = weight.shape[1]
    rows = mine.shape[0]
    block = at[4] // 2
    for number, ref in ((block, mine), (1 - block, got)):
        place = pl.ds(pl.multiple_of(number * rows, rows), rows)
        weight[place, :] = ref[:, :width]
        down[place, :] = ref[:, width:]
    for steps, group in enumerate(((own, own_s), (one, one_s), (two, two_s))):
        rows_product(at, steps, group, (mixed, mixed_s), weight, down, out.at[steps])


def far_last_kernel(at, three, three_s, mixed, mixed_s, weight, down, out):
    rows_product(at, 3, (three, three_s), (mixed, mixed_s), weight, down, out)


def own_kernel(
    at, own, own_s, one, one_s, two, two_s, three, three_s, mixed, mixed_s, weight, down, tie, out
):
    groups = ((own, own_s), (one, one_s), (two, two_s), (three, three_s))
    for steps, group in enumerate(groups):
        rows_product(at, steps, group, (mixed, mixed_s), weight, down, out.at[steps])


def place_kernel(at, own, got, last, out, sems):
    y, zh, c = at[1], at[2], at[3]
    tokens = out.shape[3]
    copies = []
    for steps in range(4):
        other = got.at[steps] if steps < 3 else last
        for ref, side in ((own.at[steps], zh), (other, 1 - zh)):
            for half, core in ((0, c), (1, 1 - c)):
                copies.append(
                    pltpu.make_async_copy(
                        ref.at[pl.ds(half * tokens, tokens)],
                        out.at[back_at(y, core, steps), side, core],
                        sems.at[len(copies)],
                    )
                )
    run(copies)


def on_device(hidden, grad, mixture, weight, down, up, gate_matrix):
    tokens, width = grad.shape
    adapters = gate_matrix.shape[0]
    stacked = up.shape[0]
    features = weight.shape[0]
    depth = width + stacked
    quarter = features // 4
    x, y, zh, c = (lax.axis_index(a) for a in ("x", "y", "zh", "c"))
    turned = jnp.where(x == 0, 0, jnp.where(x == 3, 1, x + 1))
    at = jnp.stack([x, y, zh, c, jnp.where(c == 0, x, turned)]).astype(jnp.int32)

    piece = pl.pallas_call(
        split_kernel,
        in_specs=[SMEM, HBM, HBM],
        out_specs=VMEM,
        out_shape=shaped((quarter, depth), BF16),
        scratch_shapes=[pltpu.SemaphoreType.DMA((2,))],
        name="split",
    )(at, weight, down)
    with jax.named_scope("weight_z"):
        far_piece = swap(piece, "zh", 1)
    with jax.named_scope("tokens_y"):
        one = ring(grad, "y")
    with jax.named_scope("tokens_core"):
        own_s = swap(grad, "c", 1)

    keep, give = pl.pallas_call(
        act_kernel,
        in_specs=[SMEM, HBM, HBM],
        out_specs=[VMEM, VMEM],
        out_shape=[
            shaped((4, 2, tokens, stacked), F32),
            shaped((4, 2, tokens, stacked), BF16),
        ],
        scratch_shapes=[
            pltpu.VMEM((2, 8, tokens, features), BF16),
            pltpu.VMEM((features, stacked), BF16),
            pltpu.SemaphoreType.DMA((3,)),
        ],
        cost_estimate=cost(2 * mixture.size * stacked, 4 * mixture.size),
        name="rank_products",
    )(at, mixture.reshape(8, 2, tokens, -1), down)
    with jax.named_scope("act_core"):
        got = swap(give, "c", 1)
    mixed, gates, back = pl.pallas_call(
        token_kernel,
        in_specs=[SMEM, HBM, HBM, HBM, VMEM],
        out_specs=[VMEM, VMEM, VMEM],
        out_shape=[
            shaped((tokens, stacked), BF16),
            shaped((adapters, tokens), F32),
            shaped((tokens, stacked), F32),
        ],
        scratch_shapes=[
            pltpu.VMEM((tokens, width), BF16),
            pltpu.VMEM((tokens, width), BF16),
            pltpu.VMEM((stacked, width), BF16),
            pltpu.SemaphoreType.DMA((3,)),
        ],
        cost_estimate=cost(6 * tokens * width * stacked, 12 * tokens * width),
        name="token_values",
    )(at, hidden, grad, up, gate_matrix)
    first, second, third, rest = pl.pallas_call(
        act_y_kernel,
        in_specs=[SMEM, VMEM, VMEM, VMEM],
        out_specs=[VMEM] * 4,
        out_shape=[shaped((3, tokens, stacked), BF16)] * 3 + [shaped((2, tokens, stacked), F32)],
        compiler_params=SMALL,
        name="rank_sum_core",
    )(at, keep, got, mixed)
    with jax.named_scope("act_y"):
        first, second, third = (
            swap(v, "y", mask) for v, mask in ((first, 1), (second, 2), (third, 3))
        )
    keep, give, all_mixed = pl.pallas_call(
        act_z_kernel,
        in_specs=[SMEM] + [VMEM] * 5 + [ANY],
        out_specs=[VMEM] * 3,
        out_shape=[
            shaped((tokens, stacked), F32),
            shaped((tokens, stacked), BF16),
            shaped((4, tokens, stacked), BF16),
        ],
        compiler_params=SMALL,
        name="rank_sum_y",
    )(at, rest, first, second, third, mixed, own_s)
    one, far_piece = fence((one, far_piece), give)
    with jax.named_scope("tokens_y"):
        two = ring(one, "y")
    with jax.named_scope("act_z"):
        got = swap(give, "zh", 1)
    with jax.named_scope("mixed_core"):
        mixed_s = swap(all_mixed, "c", 1)
    with jax.named_scope("tokens_core"):
        one_s = swap(one, "c", 1)
    with jax.named_scope("weight_x"):
        w_one = pairs(far_piece, "x", True)

    total, give = pl.pallas_call(
        gate_kernel,
        in_specs=[SMEM] + [VMEM] * 5,
        out_specs=[VMEM, VMEM],
        out_shape=[shaped((adapters, width // 2), F32)] * 2,
        compiler_params=SMALL,
        name="gate_products",
    )(at, keep, got, back, gates, hidden)

    def add(left, right, *ties):
        return pl.pallas_call(
            add_kernel,
            in_specs=[VMEM, VMEM] + [ANY] * len(ties),
            out_specs=VMEM,
            out_shape=shaped(left.shape, F32),
            compiler_params=SMALL,
        name="gate_sum",
        )(left, right, *ties)

    def add4(*parts):
        return pl.pallas_call(
            add4_kernel,
            in_specs=[VMEM] * 4 + [ANY] * (len(parts) - 4),
            out_specs=VMEM,
            out_shape=shaped(parts[0].shape, F32),
            compiler_params=SMALL,
        name="gate_sum",
        )(*parts)

    def step(total, axis, *ties):
        with jax.named_scope("gate_" + axis):
            got = [swap(total, axis, mask) for mask in (1, 2, 3)]
        return add4(total, *got, *ties)

    with jax.named_scope("gate_core"):
        got = swap(give, "c", 1)
    total = add(total, got, one_s)
    w_mine = pl.pallas_call(
        join_kernel,
        in_specs=[SMEM, VMEM, VMEM, ANY],
        out_specs=VMEM,
        out_shape=shaped((2 * quarter, depth), BF16),
        compiler_params=SMALL,
        name="join",
    )(at, far_piece, w_one, total)
    with jax.named_scope("weight_x"):
        w_got = pairs(w_mine, "x", False)
    total = step(total, "zl", w_mine, mixed_s)
    (two,) = fence((two,), total)
    with jax.named_scope("tokens_y"):
        three = ring(two, "y")
    with jax.named_scope("gate_zh"):
        got = swap(total, "zh", 1)
    with jax.named_scope("tokens_core"):
        two_s = swap(two, "c", 1)
    total = add(total, got, two)
    near = (grad, own_s, one, one_s, two, two_s)
    total = step(total, "x", two_s)
    (three,) = fence((three,), total)
    with jax.named_scope("tokens_core"):
        three_s = swap(three, "c", 1)

    far, far_weight, far_down = pl.pallas_call(
        far_kernel,
        in_specs=[SMEM] + [VMEM] * 10 + [ANY],
        out_specs=[VMEM] * 3,
        out_shape=[
            shaped((3, 2 * tokens, features), BF16),
            shaped((features, width), BF16),
            shaped((features, stacked), BF16),
        ],
        cost_estimate=cost(12 * tokens * depth * features, 18 * tokens * depth),
        compiler_params=MIDDLE,
        name="far_products",
    )(at, *near, all_mixed, mixed_s, w_mine, w_got, total)
    with jax.named_scope("out_z"):
        far_got = swap(far, "zh", 1)

    last = pl.pallas_call(
        far_last_kernel,
        in_specs=[SMEM] + [VMEM] * 6,
        out_specs=VMEM,
        out_shape=shaped((2 * tokens, features), BF16),
        cost_estimate=cost(4 * tokens * depth * features, 6 * tokens * depth),
        compiler_params=MIDDLE,
        name="far_products_last",
    )(at, three, three_s, all_mixed, mixed_s, far_weight, far_down)
    with jax.named_scope("out_z_last"):
        last_got = swap(last, "zh", 1)

    (total,) = fence((total,), last)
    total = step(total, "y")
    own_out = pl.pallas_call(
        own_kernel,
        in_specs=[SMEM] + [VMEM] * 12 + [ANY],
        out_specs=VMEM,
        out_shape=shaped((4, 2 * tokens, features), BF16),
        cost_estimate=cost(16 * tokens * depth * features, 24 * tokens * depth),
        compiler_params=MIDDLE,
        name="own_products",
    )(at, *near, three, three_s, all_mixed, mixed_s, weight, down, last)
    (total,) = fence((total,), far_got, own_out)
    with jax.named_scope("gate_core_back"):
        other = swap(total, "c", 1)
    gate_grad = jnp.where(
        c == 0, jnp.concatenate([total, other], axis=1), jnp.concatenate([other, total], axis=1)
    )

    out = pl.pallas_call(
        place_kernel,
        in_specs=[SMEM, VMEM, VMEM, VMEM],
        out_specs=HBM,
        out_shape=shaped((4, 2, 2, tokens, features), BF16),
        scratch_shapes=[pltpu.SemaphoreType.DMA((16,))],
        compiler_params=MIDDLE,
        name="place",
    )(at, own_out, far_got, last_got)
    return gate_grad, out.reshape(16 * tokens, features)


def solution(mesh):
    grid = Mesh(mesh.devices.reshape(4, 4, 4, 2, 2), AXES)
    dp, tensor = ("x", "zl"), ("y", "zh", "c")
    return jax.shard_map(
        on_device,
        mesh=grid,
        in_specs=(
            P(AXES, None),
            P(AXES, None),
            P(dp, tensor),
            P(tensor, None),
            P(tensor, None),
            P(),
            P(),
        ),
        out_specs=(P(), P(dp, tensor)),
        check_vma=False,
    )
```

```python
import jax
import jax.numpy as jnp
from jax import lax
from jax.experimental import pallas as pl
from jax.experimental.pallas import tpu as pltpu
from jax.sharding import Mesh
from jax.sharding import PartitionSpec as P

F32 = jnp.float32
BF16 = jnp.bfloat16
AXES = ("x", "zl", "y", "zh", "c")
VMEM = pl.BlockSpec(memory_space=pltpu.VMEM)
SMEM = pl.BlockSpec(memory_space=pltpu.SMEM)
ANY = pl.BlockSpec(memory_space=pl.ANY)
HBM = pl.BlockSpec(memory_space=pltpu.HBM)
SMALL = pltpu.CompilerParams(vmem_limit_bytes=8 * 1024 * 1024)
MIDDLE = pltpu.CompilerParams(vmem_limit_bytes=24 * 1024 * 1024)


def ring(value, axis):
    size = lax.axis_size(axis)
    pairs = [
        (2 * i + c, 2 * ((i + 1 - 2 * c) % size) + c) for i in range(size) for c in range(2)
    ]
    return lax.ppermute(value, (axis, "c"), pairs)


def pairs(value, axis, first):
    size = lax.axis_size(axis)
    partner = lambda i, c: i ^ 1 if (c == 0) == first else size - 1 - i
    return lax.ppermute(
        value, (axis, "c"), [(2 * i + c, 2 * partner(i, c) + c) for i in range(size) for c in range(2)]
    )


def fence_kernel(*refs):
    del refs


def fence(values, *ties):
    return pl.pallas_call(
        fence_kernel,
        in_specs=[ANY] * (len(values) + len(ties)),
        out_specs=[ANY] * len(values),
        out_shape=[shaped(v.shape, v.dtype) for v in values],
        input_output_aliases={i: i for i in range(len(values))},
        compiler_params=SMALL,
        name="fence",
    )(*values, *ties)


def back_at(place, core, steps):
    return lax.rem(place - steps * (1 - 2 * core) + 4, 4)


def swap(value, axis, mask):
    size = lax.axis_size(axis)
    return lax.ppermute(value, axis, [(i, i ^ mask) for i in range(size)])


def dot_t(left, right, precision=None):
    return lax.dot_general(
        left, right, (((1,), (1,)), ((), ())), precision=precision, preferred_element_type=F32
    )


def shaped(shape, dtype):
    return jax.ShapeDtypeStruct(shape, dtype)


def cost(flops, moved):
    return pl.CostEstimate(flops=flops, bytes_accessed=moved, transcendentals=0)


def membership(adapters, stacked):
    row = lax.broadcasted_iota(jnp.int32, (adapters, stacked), 0)
    column = lax.broadcasted_iota(jnp.int32, (adapters, stacked), 1)
    low = row * (stacked // adapters)
    return jnp.where((column >= low) & (column < low + stacked // adapters), 1.0, 0.0)


def join_kernel(at, mine, got, tie, out):
    quarter = mine.shape[0]
    side = lax.rem(at[4], 2)
    for place, ref in ((side, mine), (1 - side, got)):
        out[pl.ds(pl.multiple_of(place * quarter, quarter), quarter), :] = ref[...]


def token_kernel(at, hidden, grad, up, gate, mixed, gates, back):
    stacked = up.shape[0]
    ones = membership(gate.shape[0], stacked)
    wide = lax.dot_general(
        ones.astype(BF16), gate[...], (((0,), (0,)), ((), ())), preferred_element_type=F32
    ).astype(BF16)
    gates[...] = jax.nn.sigmoid(dot_t(gate[...], hidden[...]))
    factor = 2.0 * jax.nn.sigmoid(dot_t(hidden[...], wide))
    pulled = dot_t(grad[...], up[...])
    back[...] = pulled
    mixed[...] = (factor * pulled).astype(BF16)


def act_kernel(at, mixture, down, keep, give):
    c = at[3]
    blocks, _, tokens, depth = mixture.shape
    for out, side in ((give, 1 - c), (keep, c)):
        rows = mixture[:, side].reshape(blocks * tokens, depth)
        value = jnp.dot(rows, down[...], preferred_element_type=F32)
        out[...] = value.reshape(out.shape).astype(out.dtype)


def act_y_kernel(at, keep, got, mixed, first, second, third, rest):
    y = at[1]
    for out, mask in ((first, 1), (second, 2), (third, 3)):
        row = jnp.bitwise_xor(y, mask)
        out[pl.ds(0, 2)] = (keep[row] + got[row].astype(F32)).astype(out.dtype)
        out[2] = mixed[...]
    rest[...] = keep[y] + got[y].astype(F32)


def act_z_kernel(at, rest, first, second, third, mixed, down, tie, keep, give, all_mixed):
    y, zh = at[1], at[2]
    tokens = keep.shape[0]
    for out, side in ((give, 1 - zh), (keep, zh)):
        total = (rest[side] + first[side].astype(F32)) + (
            second[side].astype(F32) + third[side].astype(F32)
        )
        out[pl.ds(0, tokens), :] = total.astype(out.dtype)
    give[pl.ds(tokens, down.shape[0]), :] = down[...]
    all_mixed[y] = mixed[...]
    for ref, mask in ((first, 1), (second, 2), (third, 3)):
        all_mixed[jnp.bitwise_xor(y, mask)] = ref[2]


def gate_kernel(at, keep, got, back, gates, hidden, result, give):
    stacked = keep.shape[1]
    adapters = gates.shape[0]
    half = result.shape[1]
    product = (keep[...] + got[pl.ds(0, keep.shape[0]), :].astype(F32)) * back[...]
    ones = membership(adapters, stacked)
    delta = 2.0 * dot_t(ones, product, lax.Precision.HIGHEST)
    dlogit = delta * gates[...] * (1.0 - gates[...])
    top = dlogit.astype(BF16).astype(F32)
    middle = (dlogit - top).astype(BF16).astype(F32)
    parts = jnp.concatenate([top, middle, dlogit - top - middle], axis=0).astype(BF16)
    c = at[3]
    for out, side in ((result, c), (give, 1 - c)):
        columns = pl.ds(pl.multiple_of(side * half, 128), half)
        total = jnp.dot(parts, hidden[:, columns], preferred_element_type=F32)
        out[...] = total[:adapters] + (
            total[adapters : 2 * adapters] + total[2 * adapters :]
        )


def add_kernel(left, right, *refs):
    refs[-1][...] = left[...] + right[...]


def add4_kernel(first, second, third, fourth, *refs):
    refs[-1][...] = (first[...] + second[...]) + (third[...] + fourth[...])


def rows_product(at, steps, refs, mixed, weights, downs, out):
    y, c = at[1], at[3]
    both = jnp.concatenate([ref[...] for ref in refs], axis=0)
    ranks = jnp.concatenate(
        [mixed[0][back_at(y, c, steps)], mixed[1][back_at(y, 1 - c, steps)]], axis=0
    )
    value = dot_t(both, weights[...]) + dot_t(ranks, downs[...])
    out[...] = value.astype(out.dtype)


def far_kernel(at, own, own_s, one, one_s, two, two_s, mixed, mixed_s, mine, got, downs, out, weight):
    rows = mine.shape[0]
    block = at[4] // 2
    for number, ref in ((block, mine), (1 - block, got)):
        weight[pl.ds(pl.multiple_of(number * rows, rows), rows), :] = ref[...]
    down = downs.at[pl.ds(own.shape[0], weight.shape[0])]
    for steps, group in enumerate(((own, own_s), (one, one_s), (two, two_s))):
        rows_product(at, steps, group, (mixed, mixed_s), weight, down, out.at[steps])


def far_last_kernel(at, three, three_s, mixed, mixed_s, weight, downs, out):
    down = downs.at[pl.ds(three.shape[0], weight.shape[0])]
    rows_product(at, 3, (three, three_s), (mixed, mixed_s), weight, down, out)


def own_kernel(
    at, own, own_s, one, one_s, two, two_s, three, three_s, mixed, mixed_s, weight, down, tie, out
):
    groups = ((own, own_s), (one, one_s), (two, two_s), (three, three_s))
    for steps, group in enumerate(groups):
        rows_product(at, steps, group, (mixed, mixed_s), weight, down, out.at[steps])


def place_kernel(at, own, got, last, out, sems):
    y, zh, c = at[1], at[2], at[3]
    tokens = out.shape[3]
    copies = []
    for steps in range(4):
        other = got.at[steps] if steps < 3 else last
        for ref, side in ((own.at[steps], zh), (other, 1 - zh)):
            for half, core in ((0, c), (1, 1 - c)):
                copies.append(
                    pltpu.make_async_copy(
                        ref.at[pl.ds(half * tokens, tokens)],
                        out.at[back_at(y, core, steps), side, core],
                        sems.at[len(copies)],
                    )
                )
    for copy in copies:
        copy.start()
    for copy in copies:
        copy.wait()


def on_device(hidden, grad, mixture, weight, down, up, gate_matrix):
    tokens, width = grad.shape
    adapters = gate_matrix.shape[0]
    stacked = up.shape[0]
    features = weight.shape[0]
    depth = width + stacked
    quarter = features // 4
    x, y, zh, c = (lax.axis_index(a) for a in ("x", "y", "zh", "c"))
    turned = jnp.where(x == 0, 0, jnp.where(x == 3, 1, x + 1))
    number = jnp.where(c == 0, x, turned)
    at = jnp.stack([x, y, zh, c, number]).astype(jnp.int32)

    with jax.named_scope("weight_z"):
        piece = lax.dynamic_slice_in_dim(weight, number * quarter, quarter, 0)
        far_piece = swap(piece, "zh", 1)
    with jax.named_scope("tokens_y"):
        one = ring(grad, "y")
    with jax.named_scope("tokens_core"):
        own_s = swap(grad, "c", 1)

    keep, give = pl.pallas_call(
        act_kernel,
        in_specs=[SMEM, VMEM, VMEM],
        out_specs=[VMEM, VMEM],
        out_shape=[
            shaped((4, 2, tokens, stacked), F32),
            shaped((4, 2, tokens, stacked), BF16),
        ],
        compiler_params=SMALL,
        cost_estimate=cost(2 * mixture.size * stacked, 4 * mixture.size),
        name="rank_products",
    )(at, mixture.reshape(8, 2, tokens, -1), down)
    with jax.named_scope("act_core"):
        got = swap(give, "c", 1)
    mixed, gates, back = pl.pallas_call(
        token_kernel,
        in_specs=[SMEM] + [VMEM] * 4,
        out_specs=[VMEM, VMEM, VMEM],
        out_shape=[
            shaped((tokens, stacked), BF16),
            shaped((adapters, tokens), F32),
            shaped((tokens, stacked), F32),
        ],
        compiler_params=SMALL,
        cost_estimate=cost(6 * tokens * width * stacked, 12 * tokens * width),
        name="token_values",
    )(at, hidden, grad, up, gate_matrix)
    first, second, third, rest = pl.pallas_call(
        act_y_kernel,
        in_specs=[SMEM, VMEM, VMEM, VMEM],
        out_specs=[VMEM] * 4,
        out_shape=[shaped((3, tokens, stacked), BF16)] * 3 + [shaped((2, tokens, stacked), F32)],
        compiler_params=SMALL,
        name="rank_sum_core",
    )(at, keep, got, mixed)
    with jax.named_scope("act_y"):
        first, second, third = (
            swap(v, "y", mask) for v, mask in ((first, 1), (second, 2), (third, 3))
        )
    keep, give, all_mixed = pl.pallas_call(
        act_z_kernel,
        in_specs=[SMEM] + [VMEM] * 6 + [ANY],
        out_specs=[VMEM] * 3,
        out_shape=[
            shaped((tokens, stacked), F32),
            shaped((tokens + features, stacked), BF16),
            shaped((4, tokens, stacked), BF16),
        ],
        compiler_params=SMALL,
        name="rank_sum_y",
    )(at, rest, first, second, third, mixed, down, own_s)
    one, far_piece = fence((one, far_piece), give)
    with jax.named_scope("tokens_y"):
        two = ring(one, "y")
    with jax.named_scope("act_z"):
        message = swap(give, "zh", 1)
    with jax.named_scope("mixed_core"):
        mixed_s = swap(all_mixed, "c", 1)
    with jax.named_scope("tokens_core"):
        one_s = swap(one, "c", 1)
    with jax.named_scope("weight_x"):
        w_one = pairs(far_piece, "x", True)

    total, give = pl.pallas_call(
        gate_kernel,
        in_specs=[SMEM] + [VMEM] * 5,
        out_specs=[VMEM, VMEM],
        out_shape=[shaped((adapters, width // 2), F32)] * 2,
        compiler_params=SMALL,
        name="gate_products",
    )(at, keep, message, back, gates, hidden)

    def add(left, right, *ties):
        return pl.pallas_call(
            add_kernel,
            in_specs=[VMEM, VMEM] + [ANY] * len(ties),
            out_specs=VMEM,
            out_shape=shaped(left.shape, F32),
            compiler_params=SMALL,
        name="gate_sum",
        )(left, right, *ties)

    def add4(*parts):
        return pl.pallas_call(
            add4_kernel,
            in_specs=[VMEM] * 4 + [ANY] * (len(parts) - 4),
            out_specs=VMEM,
            out_shape=shaped(parts[0].shape, F32),
            compiler_params=SMALL,
        name="gate_sum",
        )(*parts)

    def step(total, axis, *ties):
        with jax.named_scope("gate_" + axis):
            got = [swap(total, axis, mask) for mask in (1, 2, 3)]
        return add4(total, *got, *ties)

    with jax.named_scope("gate_core"):
        got = swap(give, "c", 1)
    total = add(total, got, one_s, w_one)
    w_mine = pl.pallas_call(
        join_kernel,
        in_specs=[SMEM, VMEM, VMEM, ANY],
        out_specs=VMEM,
        out_shape=shaped((2 * quarter, width), BF16),
        compiler_params=SMALL,
        name="join",
    )(at, far_piece, w_one, total)
    with jax.named_scope("weight_x"):
        w_got = pairs(w_mine, "x", False)
    total = step(total, "zl", w_mine, mixed_s)
    (two,) = fence((two,), total)
    with jax.named_scope("tokens_y"):
        three = ring(two, "y")
    with jax.named_scope("gate_zh"):
        got = swap(total, "zh", 1)
    with jax.named_scope("tokens_core"):
        two_s = swap(two, "c", 1)
    total = add(total, got, two_s, w_got)
    near = (grad, own_s, one, one_s, two, two_s)
    far, far_weight = pl.pallas_call(
        far_kernel,
        in_specs=[SMEM] + [VMEM] * 11,
        out_specs=[VMEM] * 2,
        out_shape=[
            shaped((3, 2 * tokens, features), BF16),
            shaped((features, width), BF16),
        ],
        compiler_params=MIDDLE,
        cost_estimate=cost(12 * tokens * depth * features, 18 * tokens * depth),
        name="far_products",
    )(at, *near, all_mixed, mixed_s, w_mine, w_got, message)
    (three,) = fence((three,), far)
    with jax.named_scope("tokens_core"):
        three_s = swap(three, "c", 1)
    total = step(total, "x", far)
    with jax.named_scope("out_z"):
        far_got = swap(far, "zh", 1)

    last = pl.pallas_call(
        far_last_kernel,
        in_specs=[SMEM] + [VMEM] * 6,
        out_specs=VMEM,
        out_shape=shaped((2 * tokens, features), BF16),
        cost_estimate=cost(4 * tokens * depth * features, 6 * tokens * depth),
        compiler_params=MIDDLE,
        name="far_products_last",
    )(at, three, three_s, all_mixed, mixed_s, far_weight, message)
    with jax.named_scope("out_z_last"):
        last_got = swap(last, "zh", 1)

    (total,) = fence((total,), last)
    total = step(total, "y")
    own_out = pl.pallas_call(
        own_kernel,
        in_specs=[SMEM] + [VMEM] * 12 + [ANY],
        out_specs=VMEM,
        out_shape=shaped((4, 2 * tokens, features), BF16),
        cost_estimate=cost(16 * tokens * depth * features, 24 * tokens * depth),
        compiler_params=MIDDLE,
        name="own_products",
    )(at, *near, three, three_s, all_mixed, mixed_s, weight, down, last)
    (total,) = fence((total,), far_got, own_out)
    with jax.named_scope("gate_core_back"):
        other = swap(total, "c", 1)
    gate_grad = jnp.where(
        c == 0, jnp.concatenate([total, other], axis=1), jnp.concatenate([other, total], axis=1)
    )

    out = pl.pallas_call(
        place_kernel,
        in_specs=[SMEM, VMEM, VMEM, VMEM],
        out_specs=HBM,
        out_shape=shaped((4, 2, 2, tokens, features), BF16),
        scratch_shapes=[pltpu.SemaphoreType.DMA((16,))],
        compiler_params=MIDDLE,
        name="place",
    )(at, own_out, far_got, last_got)
    return gate_grad, out.reshape(16 * tokens, features)


def solution(mesh):
    grid = Mesh(mesh.devices.reshape(4, 4, 4, 2, 2), AXES)
    dp, tensor = ("x", "zl"), ("y", "zh", "c")
    return jax.shard_map(
        on_device,
        mesh=grid,
        in_specs=(
            P(AXES, None),
            P(AXES, None),
            P(dp, tensor),
            P(tensor, None),
            P(tensor, None),
            P(),
            P(),
        ),
        out_specs=(P(), P(dp, tensor)),
        check_vma=False,
    )
```

```python
import functools

import jax
import jax.numpy as jnp
from jax import lax
from jax.experimental import pallas as pl
from jax.experimental.pallas import tpu as pltpu
from jax.sharding import Mesh
from jax.sharding import PartitionSpec as P

F32 = jnp.float32
BF16 = jnp.bfloat16
AXES = ("x", "zl", "y", "zh", "c")
VMEM = pl.BlockSpec(memory_space=pltpu.VMEM)
SMEM = pl.BlockSpec(memory_space=pltpu.SMEM)
ANY = pl.BlockSpec(memory_space=pl.ANY)
HBM = pl.BlockSpec(memory_space=pltpu.HBM)
SMALL = pltpu.CompilerParams(vmem_limit_bytes=8 * 1024 * 1024)
MIDDLE = pltpu.CompilerParams(vmem_limit_bytes=24 * 1024 * 1024)


def ring(value, axis):
    size = lax.axis_size(axis)
    pairs = [
        (2 * i + c, 2 * ((i + 1 - 2 * c) % size) + c) for i in range(size) for c in range(2)
    ]
    return lax.ppermute(value, (axis, "c"), pairs)


def pairs(value, axis, first):
    size = lax.axis_size(axis)
    partner = lambda i, c: i ^ 1 if (c == 0) == first else size - 1 - i
    return lax.ppermute(
        value, (axis, "c"), [(2 * i + c, 2 * partner(i, c) + c) for i in range(size) for c in range(2)]
    )


def fence_kernel(*refs):
    del refs


def fence(values, *ties):
    return pl.pallas_call(
        fence_kernel,
        in_specs=[ANY] * (len(values) + len(ties)),
        out_specs=[ANY] * len(values),
        out_shape=[shaped(v.shape, v.dtype) for v in values],
        input_output_aliases={i: i for i in range(len(values))},
        compiler_params=SMALL,
        name="fence",
    )(*values, *ties)


def back_at(place, core, steps):
    return lax.rem(place - steps * (1 - 2 * core) + 4, 4)


def swap(value, axis, mask):
    size = lax.axis_size(axis)
    return lax.ppermute(value, axis, [(i, i ^ mask) for i in range(size)])


def dot_t(left, right, precision=None):
    return lax.dot_general(
        left, right, (((1,), (1,)), ((), ())), precision=precision, preferred_element_type=F32
    )


def shaped(shape, dtype):
    return jax.ShapeDtypeStruct(shape, dtype)


def cost(flops, moved):
    return pl.CostEstimate(flops=flops, bytes_accessed=moved, transcendentals=0)


def membership(adapters, stacked):
    row = lax.broadcasted_iota(jnp.int32, (adapters, stacked), 0)
    column = lax.broadcasted_iota(jnp.int32, (adapters, stacked), 1)
    low = row * (stacked // adapters)
    return jnp.where((column >= low) & (column < low + stacked // adapters), 1.0, 0.0)


def join_kernel(side, mine, got, tie, out):
    rows = mine.shape[0]
    for place, ref in ((side[0], mine), (1 - side[0], got)):
        out[pl.ds(pl.multiple_of(place * rows, rows), rows), :] = ref[...]


def join(side, mine, got, tie):
    return pl.pallas_call(
        join_kernel,
        in_specs=[SMEM, VMEM, VMEM, ANY],
        out_specs=VMEM,
        out_shape=shaped((2 * mine.shape[0], mine.shape[1]), mine.dtype),
        compiler_params=SMALL,
        name="join",
    )(side.reshape(1), mine, got, tie)


def token_kernel(at, hidden, grad, up, gate, mixed, gates, back):
    stacked = up.shape[0]
    ones = membership(gate.shape[0], stacked)
    wide = lax.dot_general(
        ones.astype(BF16), gate[...], (((0,), (0,)), ((), ())), preferred_element_type=F32
    ).astype(BF16)
    gates[...] = jax.nn.sigmoid(dot_t(gate[...], hidden[...]))
    factor = 2.0 * jax.nn.sigmoid(dot_t(hidden[...], wide))
    pulled = dot_t(grad[...], up[...])
    back[...] = pulled
    mixed[...] = (factor * pulled).astype(BF16)


def act_kernel(at, mixture, down, keep, give):
    c = at[3]
    blocks, _, tokens, depth = mixture.shape
    for out, side in ((give, 1 - c), (keep, c)):
        rows = mixture[:, side].reshape(blocks * tokens, depth)
        value = jnp.dot(rows, down[...], preferred_element_type=F32)
        out[...] = value.reshape(out.shape).astype(out.dtype)


def act_y_kernel(at, keep, got, mixed, first, second, third, rest):
    y = at[1]
    for out, mask in ((first, 1), (second, 2), (third, 3)):
        row = jnp.bitwise_xor(y, mask)
        out[pl.ds(0, 2)] = (keep[row] + got[row].astype(F32)).astype(out.dtype)
        out[2] = mixed[...]
    rest[...] = keep[y] + got[y].astype(F32)


def act_z_kernel(at, rest, first, second, third, mixed, tie, tie_too, keep, give, all_mixed):
    y, zh = at[1], at[2]
    for out, side in ((give, 1 - zh), (keep, zh)):
        total = (rest[side] + first[side].astype(F32)) + (
            second[side].astype(F32) + third[side].astype(F32)
        )
        out[...] = total.astype(out.dtype)
    all_mixed[y] = mixed[...]
    for ref, mask in ((first, 1), (second, 2), (third, 3)):
        all_mixed[jnp.bitwise_xor(y, mask)] = ref[2]


def gate_kernel(at, keep, got, back, gates, hidden, tie, result, give):
    stacked = keep.shape[1]
    adapters = gates.shape[0]
    half = result.shape[1]
    product = (keep[...] + got[...].astype(F32)) * back[...]
    ones = membership(adapters, stacked)
    delta = 2.0 * dot_t(ones, product, lax.Precision.HIGHEST)
    dlogit = delta * gates[...] * (1.0 - gates[...])
    top = dlogit.astype(BF16).astype(F32)
    middle = (dlogit - top).astype(BF16).astype(F32)
    parts = jnp.concatenate([top, middle, dlogit - top - middle], axis=0).astype(BF16)
    c = at[3]
    for out, side in ((result, c), (give, 1 - c)):
        columns = pl.ds(pl.multiple_of(side * half, 128), half)
        total = jnp.dot(parts, hidden[:, columns], preferred_element_type=F32)
        out[...] = total[:adapters] + (
            total[adapters : 2 * adapters] + total[2 * adapters :]
        )


def add_kernel(left, right, *refs):
    refs[-1][...] = left[...] + right[...]


def add4_kernel(first, second, third, fourth, *refs):
    refs[-1][...] = (first[...] + second[...]) + (third[...] + fourth[...])


def rows_product(at, steps, refs, mixed, weights, downs, out):
    y, c = at[1], at[3]
    both = jnp.concatenate([ref[...] for ref in refs], axis=0)
    ranks = jnp.concatenate(
        [mixed[0][back_at(y, c, steps)], mixed[1][back_at(y, 1 - c, steps)]], axis=0
    )
    value = dot_t(both, weights[...]) + dot_t(ranks, downs[...])
    out[...] = value.astype(out.dtype)


def far_kernel(at, own, own_s, one, one_s, two, two_s, mixed, mixed_s, mine, got, tie, out, weight, down):
    width = weight.shape[1]
    rows = mine.shape[0]
    block = at[4] // 2
    for number, ref in ((block, mine), (1 - block, got)):
        place = pl.ds(pl.multiple_of(number * rows, rows), rows)
        weight[place, :] = ref[:, :width]
        down[place, :] = ref[:, width:]
    for steps, group in enumerate(((own, own_s), (one, one_s), (two, two_s))):
        rows_product(at, steps, group, (mixed, mixed_s), weight, down, out.at[steps])


def far_last_kernel(at, three, three_s, mixed, mixed_s, weight, down, out):
    rows_product(at, 3, (three, three_s), (mixed, mixed_s), weight, down, out)


def own_kernel(first, at, near, near_s, more, more_s, mixed, mixed_s, weight, down, tie, out):
    for number, group in enumerate(((near, near_s), (more, more_s))):
        rows_product(at, first + number, group, (mixed, mixed_s), weight, down, out.at[number])


def place_kernel(at, near, rest, got, last, out, sems):
    y, zh, c = at[1], at[2], at[3]
    tokens = out.shape[3]
    copies = []
    for steps in range(4):
        own = near.at[steps] if steps < 2 else rest.at[steps - 2]
        other = got.at[steps] if steps < 3 else last
        for ref, side in ((own, zh), (other, 1 - zh)):
            for half, core in ((0, c), (1, 1 - c)):
                copies.append(
                    pltpu.make_async_copy(
                        ref.at[pl.ds(half * tokens, tokens)],
                        out.at[back_at(y, core, steps), side, core],
                        sems.at[len(copies)],
                    )
                )
    for copy in copies:
        copy.start()
    for copy in copies:
        copy.wait()


def on_device(hidden, grad, mixture, weight, down, up, gate_matrix):
    tokens, width = grad.shape
    adapters = gate_matrix.shape[0]
    stacked = up.shape[0]
    features = weight.shape[0]
    depth = width + stacked
    quarter = features // 4
    x, y, zl, zh, c = (lax.axis_index(a) for a in ("x", "y", "zl", "zh", "c"))
    turned = jnp.where(x == 0, 0, jnp.where(x == 3, 1, x + 1))
    number = jnp.where(c == 0, x, turned)
    at = jnp.stack([x, y, zh, c, number]).astype(jnp.int32)

    with jax.named_scope("weight_z"):
        start = number * quarter + (zl % 2) * (quarter // 2)
        piece = jnp.concatenate(
            [lax.dynamic_slice_in_dim(v, start, quarter // 2, 0) for v in (weight, down)], axis=1
        )
        far_piece = swap(piece, "zh", 1)
    with jax.named_scope("tokens_y"):
        one = ring(grad, "y")
    with jax.named_scope("tokens_core"):
        own_s = swap(grad, "c", 1)

    keep, give = pl.pallas_call(
        act_kernel,
        in_specs=[SMEM, VMEM, VMEM],
        out_specs=[VMEM, VMEM],
        out_shape=[
            shaped((4, 2, tokens, stacked), F32),
            shaped((4, 2, tokens, stacked), BF16),
        ],
        compiler_params=SMALL,
        cost_estimate=cost(2 * mixture.size * stacked, 4 * mixture.size),
        name="rank_products",
    )(at, mixture.reshape(8, 2, tokens, -1), down)
    with jax.named_scope("act_core"):
        got = swap(give, "c", 1)
    mixed, gates, back = pl.pallas_call(
        token_kernel,
        in_specs=[SMEM] + [VMEM] * 4,
        out_specs=[VMEM, VMEM, VMEM],
        out_shape=[
            shaped((tokens, stacked), BF16),
            shaped((adapters, tokens), F32),
            shaped((tokens, stacked), F32),
        ],
        compiler_params=SMALL,
        cost_estimate=cost(6 * tokens * width * stacked, 12 * tokens * width),
        name="token_values",
    )(at, hidden, grad, up, gate_matrix)
    first, second, third, rest = pl.pallas_call(
        act_y_kernel,
        in_specs=[SMEM, VMEM, VMEM, VMEM],
        out_specs=[VMEM] * 4,
        out_shape=[shaped((3, tokens, stacked), BF16)] * 3 + [shaped((2, tokens, stacked), F32)],
        compiler_params=SMALL,
        name="rank_sum_core",
    )(at, keep, got, mixed)
    (far_piece,) = fence((far_piece,), rest)
    with jax.named_scope("weight_zl"):
        z_got = swap(far_piece, "zl", 1)
    with jax.named_scope("act_y"):
        first, second, third = (
            swap(v, "y", mask) for v, mask in ((first, 1), (second, 2), (third, 3))
        )
    keep, give, all_mixed = pl.pallas_call(
        act_z_kernel,
        in_specs=[SMEM] + [VMEM] * 5 + [ANY] * 2,
        out_specs=[VMEM] * 3,
        out_shape=[
            shaped((tokens, stacked), F32),
            shaped((tokens, stacked), BF16),
            shaped((4, tokens, stacked), BF16),
        ],
        compiler_params=SMALL,
        name="rank_sum_y",
    )(at, rest, first, second, third, mixed, own_s, z_got)
    (one,) = fence((one,), give)
    with jax.named_scope("tokens_y"):
        two = ring(one, "y")
    far_quarter = join(zl % 2, far_piece, z_got, give)
    with jax.named_scope("weight_x"):
        w_one = pairs(far_quarter, "x", True)
    with jax.named_scope("act_z"):
        message = swap(give, "zh", 1)
    with jax.named_scope("mixed_core"):
        mixed_s = swap(all_mixed, "c", 1)
    with jax.named_scope("tokens_core"):
        one_s = swap(one, "c", 1)

    def own_products(first, near, near_s, more, more_s, tie):
        return pl.pallas_call(
            functools.partial(own_kernel, first),
            in_specs=[SMEM] + [VMEM] * 8 + [ANY],
            out_specs=VMEM,
            out_shape=shaped((2, 2 * tokens, features), BF16),
            compiler_params=MIDDLE,
            cost_estimate=cost(8 * tokens * depth * features, 12 * tokens * depth),
            name="own_products",
        )(at, near, near_s, more, more_s, all_mixed, mixed_s, weight, down, tie)

    own_near = own_products(0, grad, own_s, one, one_s, give)

    total, give = pl.pallas_call(
        gate_kernel,
        in_specs=[SMEM] + [VMEM] * 5 + [ANY],
        out_specs=[VMEM, VMEM],
        out_shape=[shaped((adapters, width // 2), F32)] * 2,
        compiler_params=SMALL,
        name="gate_products",
    )(at, keep, message, back, gates, hidden, own_near)

    def add(left, right, *ties):
        return pl.pallas_call(
            add_kernel,
            in_specs=[VMEM, VMEM] + [ANY] * len(ties),
            out_specs=VMEM,
            out_shape=shaped(left.shape, F32),
            compiler_params=SMALL,
        name="gate_sum",
        )(left, right, *ties)

    def add4(*parts):
        return pl.pallas_call(
            add4_kernel,
            in_specs=[VMEM] * 4 + [ANY] * (len(parts) - 4),
            out_specs=VMEM,
            out_shape=shaped(parts[0].shape, F32),
            compiler_params=SMALL,
        name="gate_sum",
        )(*parts)

    def step(total, axis, *ties):
        with jax.named_scope("gate_" + axis):
            got = [swap(total, axis, mask) for mask in (1, 2, 3)]
        return add4(total, *got, *ties)

    with jax.named_scope("gate_core"):
        got = swap(give, "c", 1)
    total = add(total, got, w_one)
    w_mine = join(number % 2, far_quarter, w_one, total)
    with jax.named_scope("weight_x"):
        w_got = pairs(w_mine, "x", False)
    total = step(total, "zl", w_mine, mixed_s)
    (two,) = fence((two,), total)
    with jax.named_scope("tokens_y"):
        three = ring(two, "y")
    with jax.named_scope("gate_zh"):
        got = swap(total, "zh", 1)
    with jax.named_scope("tokens_core"):
        two_s = swap(two, "c", 1)
    total = add(total, got, two_s, w_got)
    near = (grad, own_s, one, one_s, two, two_s)
    far, far_weight, far_down = pl.pallas_call(
        far_kernel,
        in_specs=[SMEM] + [VMEM] * 10 + [ANY],
        out_specs=[VMEM] * 3,
        out_shape=[
            shaped((3, 2 * tokens, features), BF16),
            shaped((features, width), BF16),
            shaped((features, stacked), BF16),
        ],
        compiler_params=MIDDLE,
        cost_estimate=cost(12 * tokens * depth * features, 18 * tokens * depth),
        name="far_products",
    )(at, *near, all_mixed, mixed_s, w_mine, w_got, total)
    (three,) = fence((three,), far)
    with jax.named_scope("tokens_core"):
        three_s = swap(three, "c", 1)
    total = step(total, "x", far)
    with jax.named_scope("out_z"):
        far_got = swap(far, "zh", 1)

    last = pl.pallas_call(
        far_last_kernel,
        in_specs=[SMEM] + [VMEM] * 6,
        out_specs=VMEM,
        out_shape=shaped((2 * tokens, features), BF16),
        cost_estimate=cost(4 * tokens * depth * features, 6 * tokens * depth),
        compiler_params=MIDDLE,
        name="far_products_last",
    )(at, three, three_s, all_mixed, mixed_s, far_weight, far_down)
    with jax.named_scope("out_z_last"):
        last_got = swap(last, "zh", 1)

    (total,) = fence((total,), last)
    total = step(total, "y")
    own_rest = own_products(2, two, two_s, three, three_s, last)
    (total,) = fence((total,), far_got, own_rest)
    with jax.named_scope("gate_core_back"):
        other = swap(total, "c", 1)
    gate_grad = jnp.where(
        c == 0, jnp.concatenate([total, other], axis=1), jnp.concatenate([other, total], axis=1)
    )

    out = pl.pallas_call(
        place_kernel,
        in_specs=[SMEM] + [VMEM] * 4,
        out_specs=HBM,
        out_shape=shaped((4, 2, 2, tokens, features), BF16),
        scratch_shapes=[pltpu.SemaphoreType.DMA((16,))],
        compiler_params=MIDDLE,
        name="place",
    )(at, own_near, own_rest, far_got, last_got)
    return gate_grad, out.reshape(16 * tokens, features)


def solution(mesh):
    grid = Mesh(mesh.devices.reshape(4, 4, 4, 2, 2), AXES)
    dp, tensor = ("x", "zl"), ("y", "zh", "c")
    return jax.shard_map(
        on_device,
        mesh=grid,
        in_specs=(
            P(AXES, None),
            P(AXES, None),
            P(dp, tensor),
            P(tensor, None),
            P(tensor, None),
            P(),
            P(),
        ),
        out_specs=(P(), P(dp, tensor)),
        check_vma=False,
    )
```

```python
import functools

import jax
import jax.numpy as jnp
from jax import lax
from jax.experimental import pallas as pl
from jax.experimental.pallas import tpu as pltpu
from jax.sharding import Mesh
from jax.sharding import PartitionSpec as P

F32 = jnp.float32
BF16 = jnp.bfloat16
AXES = ("x", "zl", "y", "zh", "c")
VMEM = pl.BlockSpec(memory_space=pltpu.VMEM)
SMEM = pl.BlockSpec(memory_space=pltpu.SMEM)
ANY = pl.BlockSpec(memory_space=pl.ANY)
HBM = pl.BlockSpec(memory_space=pltpu.HBM)
SMALL = pltpu.CompilerParams(vmem_limit_bytes=8 * 1024 * 1024)
MIDDLE = pltpu.CompilerParams(vmem_limit_bytes=24 * 1024 * 1024)


def ring(value, axis):
    size = lax.axis_size(axis)
    pairs = [
        (2 * i + c, 2 * ((i + 1 - 2 * c) % size) + c) for i in range(size) for c in range(2)
    ]
    return lax.ppermute(value, (axis, "c"), pairs)


def pairs(value, axis, first):
    size = lax.axis_size(axis)
    partner = lambda i, c: i ^ 1 if (c == 0) == first else size - 1 - i
    return lax.ppermute(
        value, (axis, "c"), [(2 * i + c, 2 * partner(i, c) + c) for i in range(size) for c in range(2)]
    )


def fence_kernel(*refs):
    del refs


def fence(values, *ties):
    return pl.pallas_call(
        fence_kernel,
        in_specs=[ANY] * (len(values) + len(ties)),
        out_specs=[ANY] * len(values),
        out_shape=[shaped(v.shape, v.dtype) for v in values],
        input_output_aliases={i: i for i in range(len(values))},
        compiler_params=SMALL,
        name="fence",
    )(*values, *ties)


def back_at(place, core, steps):
    return lax.rem(place - steps * (1 - 2 * core) + 4, 4)


def swap(value, axis, mask):
    size = lax.axis_size(axis)
    return lax.ppermute(value, axis, [(i, i ^ mask) for i in range(size)])


def dot_t(left, right, precision=None):
    return lax.dot_general(
        left, right, (((1,), (1,)), ((), ())), precision=precision, preferred_element_type=F32
    )


def shaped(shape, dtype):
    return jax.ShapeDtypeStruct(shape, dtype)


def cost(flops, moved):
    return pl.CostEstimate(flops=flops, bytes_accessed=moved, transcendentals=0)


def membership(adapters, stacked):
    row = lax.broadcasted_iota(jnp.int32, (adapters, stacked), 0)
    column = lax.broadcasted_iota(jnp.int32, (adapters, stacked), 1)
    low = row * (stacked // adapters)
    return jnp.where((column >= low) & (column < low + stacked // adapters), 1.0, 0.0)


def join_kernel(side, mine, got, tie, out):
    rows = mine.shape[0]
    for place, ref in ((side[0], mine), (1 - side[0], got)):
        out[pl.ds(pl.multiple_of(place * rows, rows), rows), :] = ref[...]


def join(side, mine, got, tie):
    return pl.pallas_call(
        join_kernel,
        in_specs=[SMEM, VMEM, VMEM, ANY],
        out_specs=VMEM,
        out_shape=shaped((2 * mine.shape[0], mine.shape[1]), mine.dtype),
        compiler_params=SMALL,
        name="join",
    )(side.reshape(1), mine, got, tie)


def token_kernel(at, hidden, grad, up, gate, mixed, gates, back):
    stacked = up.shape[0]
    ones = membership(gate.shape[0], stacked)
    wide = lax.dot_general(
        ones.astype(BF16), gate[...], (((0,), (0,)), ((), ())), preferred_element_type=F32
    ).astype(BF16)
    gates[...] = jax.nn.sigmoid(dot_t(gate[...], hidden[...]))
    factor = 2.0 * jax.nn.sigmoid(dot_t(hidden[...], wide))
    pulled = dot_t(grad[...], up[...])
    back[...] = pulled
    mixed[...] = (factor * pulled).astype(BF16)


def act_kernel(at, mixture, down, keep, give):
    c = at[3]
    blocks, _, tokens, depth = mixture.shape
    for out, side in ((give, 1 - c), (keep, c)):
        rows = mixture[:, side].reshape(blocks * tokens, depth)
        value = jnp.dot(rows, down[...], preferred_element_type=F32)
        out[...] = value.reshape(out.shape).astype(out.dtype)


def act_y_kernel(at, keep, got, mixed, first, second, third, rest):
    y = at[1]
    for out, mask in ((first, 1), (second, 2), (third, 3)):
        row = jnp.bitwise_xor(y, mask)
        out[pl.ds(0, 2)] = (keep[row] + got[row].astype(F32)).astype(out.dtype)
        out[2] = mixed[...]
    rest[...] = keep[y] + got[y].astype(F32)


def act_z_kernel(at, rest, first, second, third, mixed, tie, tie_too, keep, give, all_mixed):
    y, zh = at[1], at[2]
    for out, side in ((give, 1 - zh), (keep, zh)):
        total = (rest[side] + first[side].astype(F32)) + (
            second[side].astype(F32) + third[side].astype(F32)
        )
        out[...] = total.astype(out.dtype)
    all_mixed[y] = mixed[...]
    for ref, mask in ((first, 1), (second, 2), (third, 3)):
        all_mixed[jnp.bitwise_xor(y, mask)] = ref[2]


def gate_kernel(at, keep, got, back, gates, hidden, tie, tie_too, result, give):
    stacked = keep.shape[1]
    adapters = gates.shape[0]
    half = result.shape[1]
    product = (keep[...] + got[...].astype(F32)) * back[...]
    ones = membership(adapters, stacked)
    delta = 2.0 * dot_t(ones, product, lax.Precision.HIGHEST)
    dlogit = delta * gates[...] * (1.0 - gates[...])
    top = dlogit.astype(BF16).astype(F32)
    middle = (dlogit - top).astype(BF16).astype(F32)
    parts = jnp.concatenate([top, middle, dlogit - top - middle], axis=0).astype(BF16)
    c = at[3]
    for out, side in ((result, c), (give, 1 - c)):
        columns = pl.ds(pl.multiple_of(side * half, 128), half)
        total = jnp.dot(parts, hidden[:, columns], preferred_element_type=F32)
        out[...] = total[:adapters] + (
            total[adapters : 2 * adapters] + total[2 * adapters :]
        )


def add_kernel(left, right, *refs):
    refs[-1][...] = left[...] + right[...]


def add4_kernel(first, second, third, fourth, *refs):
    refs[-1][...] = (first[...] + second[...]) + (third[...] + fourth[...])


def rows_product(at, steps, refs, mixed, weights, downs, out):
    y, c = at[1], at[3]
    both = jnp.concatenate([ref[...] for ref in refs], axis=0)
    ranks = jnp.concatenate(
        [mixed[0][back_at(y, c, steps)], mixed[1][back_at(y, 1 - c, steps)]], axis=0
    )
    value = dot_t(both, weights[...]) + dot_t(ranks, downs[...])
    out[...] = value.astype(out.dtype)


def far_kernel(at, own, own_s, one, one_s, mixed, mixed_s, mine, got, tie, out, weight, down):
    width = weight.shape[1]
    rows = mine.shape[0]
    block = at[4] // 2
    for number, ref in ((block, mine), (1 - block, got)):
        place = pl.ds(pl.multiple_of(number * rows, rows), rows)
        weight[place, :] = ref[:, :width]
        down[place, :] = ref[:, width:]
    for steps, group in enumerate(((own, own_s), (one, one_s))):
        rows_product(at, steps, group, (mixed, mixed_s), weight, down, out.at[steps])


def product_kernel(first, at, near, near_s, more, more_s, mixed, mixed_s, weight, down, tie, out):
    for number, group in enumerate(((near, near_s), (more, more_s))):
        rows_product(at, first + number, group, (mixed, mixed_s), weight, down, out.at[number])


def place_kernel(at, near, rest, far_near, far_rest, out, sems):
    y, zh, c = at[1], at[2], at[3]
    tokens = out.shape[3]
    copies = []
    for steps in range(4):
        own, other = (near, far_near) if steps < 2 else (rest, far_rest)
        for ref, side in ((own, zh), (other, 1 - zh)):
            for half, core in ((0, c), (1, 1 - c)):
                copies.append(
                    pltpu.make_async_copy(
                        ref.at[steps % 2, pl.ds(half * tokens, tokens)],
                        out.at[back_at(y, core, steps), side, core],
                        sems.at[len(copies)],
                    )
                )
    for copy in copies:
        copy.start()
    for copy in copies:
        copy.wait()


def on_device(hidden, grad, mixture, weight, down, up, gate_matrix):
    tokens, width = grad.shape
    adapters = gate_matrix.shape[0]
    stacked = up.shape[0]
    features = weight.shape[0]
    depth = width + stacked
    quarter = features // 4
    x, y, zl, zh, c = (lax.axis_index(a) for a in ("x", "y", "zl", "zh", "c"))
    turned = jnp.where(x == 0, 0, jnp.where(x == 3, 1, x + 1))
    number = jnp.where(c == 0, x, turned)
    at = jnp.stack([x, y, zh, c, number]).astype(jnp.int32)

    with jax.named_scope("weight_z"):
        start = number * quarter + (zl % 2) * (quarter // 2)
        piece = jnp.concatenate(
            [lax.dynamic_slice_in_dim(v, start, quarter // 2, 0) for v in (weight, down)], axis=1
        )
        far_piece = swap(piece, "zh", 1)
    with jax.named_scope("tokens_y"):
        one = ring(grad, "y")
    with jax.named_scope("tokens_core"):
        own_s = swap(grad, "c", 1)

    keep, give = pl.pallas_call(
        act_kernel,
        in_specs=[SMEM, VMEM, VMEM],
        out_specs=[VMEM, VMEM],
        out_shape=[
            shaped((4, 2, tokens, stacked), F32),
            shaped((4, 2, tokens, stacked), BF16),
        ],
        compiler_params=SMALL,
        cost_estimate=cost(2 * mixture.size * stacked, 4 * mixture.size),
        name="rank_products",
    )(at, mixture.reshape(8, 2, tokens, -1), down)
    with jax.named_scope("act_core"):
        got = swap(give, "c", 1)
    mixed, gates, back = pl.pallas_call(
        token_kernel,
        in_specs=[SMEM] + [VMEM] * 4,
        out_specs=[VMEM, VMEM, VMEM],
        out_shape=[
            shaped((tokens, stacked), BF16),
            shaped((adapters, tokens), F32),
            shaped((tokens, stacked), F32),
        ],
        compiler_params=SMALL,
        cost_estimate=cost(6 * tokens * width * stacked, 12 * tokens * width),
        name="token_values",
    )(at, hidden, grad, up, gate_matrix)
    first, second, third, rest = pl.pallas_call(
        act_y_kernel,
        in_specs=[SMEM, VMEM, VMEM, VMEM],
        out_specs=[VMEM] * 4,
        out_shape=[shaped((3, tokens, stacked), BF16)] * 3 + [shaped((2, tokens, stacked), F32)],
        compiler_params=SMALL,
        name="rank_sum_core",
    )(at, keep, got, mixed)
    (far_piece,) = fence((far_piece,), rest)
    with jax.named_scope("weight_zl"):
        z_got = swap(far_piece, "zl", 1)
    with jax.named_scope("act_y"):
        first, second, third = (
            swap(v, "y", mask) for v, mask in ((first, 1), (second, 2), (third, 3))
        )
    keep, give, all_mixed = pl.pallas_call(
        act_z_kernel,
        in_specs=[SMEM] + [VMEM] * 5 + [ANY] * 2,
        out_specs=[VMEM] * 3,
        out_shape=[
            shaped((tokens, stacked), F32),
            shaped((tokens, stacked), BF16),
            shaped((4, tokens, stacked), BF16),
        ],
        compiler_params=SMALL,
        name="rank_sum_y",
    )(at, rest, first, second, third, mixed, own_s, far_piece)
    (one,) = fence((one,), give)
    with jax.named_scope("tokens_y"):
        two = ring(one, "y")
    with jax.named_scope("act_z"):
        message = swap(give, "zh", 1)
    with jax.named_scope("mixed_core"):
        mixed_s = swap(all_mixed, "c", 1)
    with jax.named_scope("tokens_core"):
        one_s = swap(one, "c", 1)

    def products(name, first, near, near_s, more, more_s, weights, downs, tie):
        return pl.pallas_call(
            functools.partial(product_kernel, first),
            in_specs=[SMEM] + [VMEM] * 8 + [ANY],
            out_specs=VMEM,
            out_shape=shaped((2, 2 * tokens, features), BF16),
            compiler_params=MIDDLE,
            cost_estimate=cost(8 * tokens * depth * features, 12 * tokens * depth),
            name=name,
        )(at, near, near_s, more, more_s, all_mixed, mixed_s, weights, downs, tie)

    own_near = products("own_near", 0, grad, own_s, one, one_s, weight, down, give)
    far_quarter = join(zl % 2, far_piece, z_got, message)
    with jax.named_scope("weight_x"):
        w_one = pairs(far_quarter, "x", True)

    total, give = pl.pallas_call(
        gate_kernel,
        in_specs=[SMEM] + [VMEM] * 5 + [ANY] * 2,
        out_specs=[VMEM, VMEM],
        out_shape=[shaped((adapters, width // 2), F32)] * 2,
        compiler_params=SMALL,
        name="gate_products",
    )(at, keep, message, back, gates, hidden, own_near, far_quarter)

    def add(left, right, *ties):
        return pl.pallas_call(
            add_kernel,
            in_specs=[VMEM, VMEM] + [ANY] * len(ties),
            out_specs=VMEM,
            out_shape=shaped(left.shape, F32),
            compiler_params=SMALL,
        name="gate_sum",
        )(left, right, *ties)

    def add4(*parts):
        return pl.pallas_call(
            add4_kernel,
            in_specs=[VMEM] * 4 + [ANY] * (len(parts) - 4),
            out_specs=VMEM,
            out_shape=shaped(parts[0].shape, F32),
            compiler_params=SMALL,
        name="gate_sum",
        )(*parts)

    def step(total, axis, *ties):
        with jax.named_scope("gate_" + axis):
            got = [swap(total, axis, mask) for mask in (1, 2, 3)]
        return add4(total, *got, *ties)

    with jax.named_scope("gate_core"):
        got = swap(give, "c", 1)
    total = add(total, got)
    total = step(total, "x", w_one)
    w_mine = join(number % 2, far_quarter, w_one, total)
    with jax.named_scope("weight_x"):
        w_got = pairs(w_mine, "x", False)
    total = step(total, "y", w_mine)
    (two,) = fence((two,), total)
    with jax.named_scope("tokens_y"):
        three = ring(two, "y")
    with jax.named_scope("tokens_core"):
        two_s = swap(two, "c", 1)
    total = step(total, "zl", two_s, w_got)

    far_near, far_weight, far_down = pl.pallas_call(
        far_kernel,
        in_specs=[SMEM] + [VMEM] * 8 + [ANY],
        out_specs=[VMEM] * 3,
        out_shape=[
            shaped((2, 2 * tokens, features), BF16),
            shaped((features, width), BF16),
            shaped((features, stacked), BF16),
        ],
        compiler_params=MIDDLE,
        cost_estimate=cost(8 * tokens * depth * features, 12 * tokens * depth),
        name="far_near",
    )(at, grad, own_s, one, one_s, all_mixed, mixed_s, w_mine, w_got, total)
    with jax.named_scope("out_z"):
        got_near = swap(far_near, "zh", 1)
    (total,) = fence((total,), far_near)
    with jax.named_scope("gate_zh"):
        got = swap(total, "zh", 1)
    (three,) = fence((three,), total)
    with jax.named_scope("tokens_core"):
        three_s = swap(three, "c", 1)
    far_rest = products("far_rest", 2, two, two_s, three, three_s, far_weight, far_down, far_near)
    with jax.named_scope("out_z_rest"):
        got_rest = swap(far_rest, "zh", 1)
    own_rest = products("own_rest", 2, two, two_s, three, three_s, weight, down, got_near)

    total = add(total, got, three_s)
    with jax.named_scope("gate_core_back"):
        other = swap(total, "c", 1)
    gate_grad = jnp.where(
        c == 0, jnp.concatenate([total, other], axis=1), jnp.concatenate([other, total], axis=1)
    )

    out = pl.pallas_call(
        place_kernel,
        in_specs=[SMEM] + [VMEM] * 4,
        out_specs=HBM,
        out_shape=shaped((4, 2, 2, tokens, features), BF16),
        scratch_shapes=[pltpu.SemaphoreType.DMA((16,))],
        compiler_params=MIDDLE,
        name="place",
    )(at, own_near, own_rest, got_near, got_rest)
    return gate_grad, out.reshape(16 * tokens, features)


def solution(mesh):
    grid = Mesh(mesh.devices.reshape(4, 4, 4, 2, 2), AXES)
    dp, tensor = ("x", "zl"), ("y", "zh", "c")
    return jax.shard_map(
        on_device,
        mesh=grid,
        in_specs=(
            P(AXES, None),
            P(AXES, None),
            P(dp, tensor),
            P(tensor, None),
            P(tensor, None),
            P(),
            P(),
        ),
        out_specs=(P(), P(dp, tensor)),
        check_vma=False,
    )
```

```python
import functools

import jax
import jax.numpy as jnp
from jax import lax
from jax.experimental import pallas as pl
from jax.experimental.pallas import tpu as pltpu
from jax.sharding import Mesh
from jax.sharding import PartitionSpec as P

F32 = jnp.float32
BF16 = jnp.bfloat16
AXES = ("x", "zl", "y", "zh", "c")
VMEM = pl.BlockSpec(memory_space=pltpu.VMEM)
SMEM = pl.BlockSpec(memory_space=pltpu.SMEM)
ANY = pl.BlockSpec(memory_space=pl.ANY)
HBM = pl.BlockSpec(memory_space=pltpu.HBM)
SMALL = pltpu.CompilerParams(vmem_limit_bytes=8 * 1024 * 1024)
MIDDLE = pltpu.CompilerParams(vmem_limit_bytes=24 * 1024 * 1024)


def ring(value, axis):
    size = lax.axis_size(axis)
    pairs = [
        (2 * i + c, 2 * ((i + 1 - 2 * c) % size) + c) for i in range(size) for c in range(2)
    ]
    return lax.ppermute(value, (axis, "c"), pairs)


def pairs(value, axis, first):
    size = lax.axis_size(axis)
    partner = lambda i, c: i ^ 1 if (c == 0) == first else size - 1 - i
    return lax.ppermute(
        value, (axis, "c"), [(2 * i + c, 2 * partner(i, c) + c) for i in range(size) for c in range(2)]
    )


def fence_kernel(*refs):
    del refs


def fence(values, *ties):
    return pl.pallas_call(
        fence_kernel,
        in_specs=[ANY] * (len(values) + len(ties)),
        out_specs=[ANY] * len(values),
        out_shape=[shaped(v.shape, v.dtype) for v in values],
        input_output_aliases={i: i for i in range(len(values))},
        compiler_params=SMALL,
        name="fence",
    )(*values, *ties)


def back_at(place, core, steps):
    return lax.rem(place - steps * (1 - 2 * core) + 4, 4)


def swap(value, axis, mask):
    size = lax.axis_size(axis)
    return lax.ppermute(value, axis, [(i, i ^ mask) for i in range(size)])


def dot_t(left, right, precision=None):
    return lax.dot_general(
        left, right, (((1,), (1,)), ((), ())), precision=precision, preferred_element_type=F32
    )


def shaped(shape, dtype):
    return jax.ShapeDtypeStruct(shape, dtype)


def cost(flops, moved):
    return pl.CostEstimate(flops=flops, bytes_accessed=moved, transcendentals=0)


def membership(adapters, stacked):
    row = lax.broadcasted_iota(jnp.int32, (adapters, stacked), 0)
    column = lax.broadcasted_iota(jnp.int32, (adapters, stacked), 1)
    low = row * (stacked // adapters)
    return jnp.where((column >= low) & (column < low + stacked // adapters), 1.0, 0.0)


def token_kernel(at, hidden, grad, up, gate, mixed, gates, back):
    stacked = up.shape[0]
    ones = membership(gate.shape[0], stacked)
    wide = lax.dot_general(
        ones.astype(BF16), gate[...], (((0,), (0,)), ((), ())), preferred_element_type=F32
    ).astype(BF16)
    gates[...] = jax.nn.sigmoid(dot_t(gate[...], hidden[...]))
    factor = 2.0 * jax.nn.sigmoid(dot_t(hidden[...], wide))
    pulled = dot_t(grad[...], up[...])
    back[...] = pulled
    mixed[...] = (factor * pulled).astype(BF16)


def act_kernel(at, mixture, down, keep, give):
    c = at[3]
    blocks, _, tokens, depth = mixture.shape
    for out, side in ((give, 1 - c), (keep, c)):
        rows = mixture[:, side].reshape(blocks * tokens, depth)
        value = jnp.dot(rows, down[...], preferred_element_type=F32)
        out[...] = value.reshape(out.shape).astype(out.dtype)


def act_y_kernel(at, keep, got, mixed, first, second, third, rest):
    y = at[1]
    for out, mask in ((first, 1), (second, 2), (third, 3)):
        row = jnp.bitwise_xor(y, mask)
        out[pl.ds(0, 2)] = (keep[row] + got[row].astype(F32)).astype(out.dtype)
        out[2] = mixed[...]
    rest[...] = keep[y] + got[y].astype(F32)


def act_z_kernel(at, rest, first, second, third, mixed, tie, keep, give, all_mixed):
    y, zh = at[1], at[2]
    for out, side in ((give, 1 - zh), (keep, zh)):
        total = (rest[side] + first[side].astype(F32)) + (
            second[side].astype(F32) + third[side].astype(F32)
        )
        out[...] = total.astype(out.dtype)
    all_mixed[y] = mixed[...]
    for ref, mask in ((first, 1), (second, 2), (third, 3)):
        all_mixed[jnp.bitwise_xor(y, mask)] = ref[2]


def gate_kernel(at, keep, got, back, gates, hidden, tie, result, give):
    stacked = keep.shape[1]
    adapters = gates.shape[0]
    half = result.shape[1]
    product = (keep[...] + got[...].astype(F32)) * back[...]
    ones = membership(adapters, stacked)
    delta = 2.0 * dot_t(ones, product, lax.Precision.HIGHEST)
    dlogit = delta * gates[...] * (1.0 - gates[...])
    top = dlogit.astype(BF16).astype(F32)
    middle = (dlogit - top).astype(BF16).astype(F32)
    parts = jnp.concatenate([top, middle, dlogit - top - middle], axis=0).astype(BF16)
    c = at[3]
    for out, side in ((result, c), (give, 1 - c)):
        columns = pl.ds(pl.multiple_of(side * half, 128), half)
        total = jnp.dot(parts, hidden[:, columns], preferred_element_type=F32)
        out[...] = total[:adapters] + (
            total[adapters : 2 * adapters] + total[2 * adapters :]
        )


def add_kernel(left, right, *refs):
    refs[-1][...] = left[...] + right[...]


def add4_kernel(first, second, third, fourth, *refs):
    refs[-1][...] = (first[...] + second[...]) + (third[...] + fourth[...])


def rows_product(at, steps, refs, mixed, weights, downs, out):
    y, c = at[1], at[3]
    both = jnp.concatenate([ref[...] for ref in refs], axis=0)
    ranks = jnp.concatenate(
        [mixed[0][back_at(y, c, steps)], mixed[1][back_at(y, 1 - c, steps)]], axis=0
    )
    value = dot_t(both, weights[...]) + dot_t(ranks, downs[...])
    out[...] = value.astype(out.dtype)


def far_kernel(at, own, own_s, one, one_s, two, two_s, mixed, mixed_s, *refs):
    pieces, (tie, out, weight, down) = refs[:4], refs[4:]
    width = weight.shape[1]
    rows = pieces[0].shape[0]
    x, c = at[0], at[3]
    up, turned = jnp.bitwise_xor(x, 1), 3 - x
    first, second = jnp.where(c == 0, up, turned), jnp.where(c == 0, turned, up)
    for place, ref in zip((x, first, second, jnp.bitwise_xor(x, 2)), pieces):
        place = pl.ds(pl.multiple_of(place * rows, rows), rows)
        weight[place, :] = ref[:, :width]
        down[place, :] = ref[:, width:]
    for steps, group in enumerate(((own, own_s), (one, one_s), (two, two_s))):
        rows_product(at, steps, group, (mixed, mixed_s), weight, down, out.at[steps])


def far_last_kernel(at, three, three_s, mixed, mixed_s, weight, down, out):
    rows_product(at, 3, (three, three_s), (mixed, mixed_s), weight, down, out)


def product_kernel(first, at, near, near_s, more, more_s, mixed, mixed_s, weight, down, tie, out):
    for number, group in enumerate(((near, near_s), (more, more_s))):
        rows_product(at, first + number, group, (mixed, mixed_s), weight, down, out.at[number])


def place_kernel(at, near, rest, got, last, out, sems):
    y, zh, c = at[1], at[2], at[3]
    tokens = out.shape[3]
    copies = []
    for steps in range(4):
        own = near.at[steps] if steps < 2 else rest.at[steps - 2]
        other = got.at[steps] if steps < 3 else last
        for ref, side in ((own, zh), (other, 1 - zh)):
            for half, core in ((0, c), (1, 1 - c)):
                copies.append(
                    pltpu.make_async_copy(
                        ref.at[pl.ds(half * tokens, tokens)],
                        out.at[back_at(y, core, steps), side, core],
                        sems.at[len(copies)],
                    )
                )
    for copy in copies:
        copy.start()
    for copy in copies:
        copy.wait()


def on_device(hidden, grad, mixture, weight, down, up, gate_matrix):
    tokens, width = grad.shape
    adapters = gate_matrix.shape[0]
    stacked = up.shape[0]
    features = weight.shape[0]
    depth = width + stacked
    quarter = features // 4
    x, y, zh, c = (lax.axis_index(a) for a in ("x", "y", "zh", "c"))
    at = jnp.stack([x, y, zh, c]).astype(jnp.int32)

    with jax.named_scope("weight_z"):
        piece = jnp.concatenate(
            [lax.dynamic_slice_in_dim(v, x * quarter, quarter, 0) for v in (weight, down)], axis=1
        )
        far_piece = swap(piece, "zh", 1)
    with jax.named_scope("tokens_y"):
        one = ring(grad, "y")
    with jax.named_scope("tokens_core"):
        own_s = swap(grad, "c", 1)

    keep, give = pl.pallas_call(
        act_kernel,
        in_specs=[SMEM, VMEM, VMEM],
        out_specs=[VMEM, VMEM],
        out_shape=[
            shaped((4, 2, tokens, stacked), F32),
            shaped((4, 2, tokens, stacked), BF16),
        ],
        compiler_params=SMALL,
        cost_estimate=cost(2 * mixture.size * stacked, 4 * mixture.size),
        name="rank_products",
    )(at, mixture.reshape(8, 2, tokens, -1), down)
    with jax.named_scope("act_core"):
        got = swap(give, "c", 1)
    mixed, gates, back = pl.pallas_call(
        token_kernel,
        in_specs=[SMEM] + [VMEM] * 4,
        out_specs=[VMEM, VMEM, VMEM],
        out_shape=[
            shaped((tokens, stacked), BF16),
            shaped((adapters, tokens), F32),
            shaped((tokens, stacked), F32),
        ],
        compiler_params=SMALL,
        cost_estimate=cost(6 * tokens * width * stacked, 12 * tokens * width),
        name="token_values",
    )(at, hidden, grad, up, gate_matrix)
    first, second, third, rest = pl.pallas_call(
        act_y_kernel,
        in_specs=[SMEM, VMEM, VMEM, VMEM],
        out_specs=[VMEM] * 4,
        out_shape=[shaped((3, tokens, stacked), BF16)] * 3 + [shaped((2, tokens, stacked), F32)],
        compiler_params=SMALL,
        name="rank_sum_core",
    )(at, keep, got, mixed)
    with jax.named_scope("act_y"):
        first, second, third = (
            swap(v, "y", mask) for v, mask in ((first, 1), (second, 2), (third, 3))
        )
    keep, give, all_mixed = pl.pallas_call(
        act_z_kernel,
        in_specs=[SMEM] + [VMEM] * 5 + [ANY],
        out_specs=[VMEM] * 3,
        out_shape=[
            shaped((tokens, stacked), F32),
            shaped((tokens, stacked), BF16),
            shaped((4, tokens, stacked), BF16),
        ],
        compiler_params=SMALL,
        name="rank_sum_y",
    )(at, rest, first, second, third, mixed, own_s)
    one, far_piece = fence((one, far_piece), give)
    with jax.named_scope("tokens_y"):
        two = ring(one, "y")
    with jax.named_scope("tokens_core"):
        one_s = swap(one, "c", 1)
    with jax.named_scope("weight_x"):
        w_first = pairs(far_piece, "x", True)
        w_second = pairs(far_piece, "x", False)
    with jax.named_scope("act_z"):
        message = swap(give, "zh", 1)
    with jax.named_scope("mixed_core"):
        mixed_s = swap(all_mixed, "c", 1)

    def products(name, first, near, near_s, more, more_s, weights, downs, tie):
        return pl.pallas_call(
            functools.partial(product_kernel, first),
            in_specs=[SMEM] + [VMEM] * 8 + [ANY],
            out_specs=VMEM,
            out_shape=shaped((2, 2 * tokens, features), BF16),
            compiler_params=MIDDLE,
            cost_estimate=cost(8 * tokens * depth * features, 12 * tokens * depth),
            name=name,
        )(at, near, near_s, more, more_s, all_mixed, mixed_s, weights, downs, tie)

    own_near = products("own_near", 0, grad, own_s, one, one_s, weight, down, give)

    total, give = pl.pallas_call(
        gate_kernel,
        in_specs=[SMEM] + [VMEM] * 5 + [ANY],
        out_specs=[VMEM, VMEM],
        out_shape=[shaped((adapters, width // 2), F32)] * 2,
        compiler_params=SMALL,
        name="gate_products",
    )(at, keep, message, back, gates, hidden, own_near)

    def add(left, right, *ties):
        return pl.pallas_call(
            add_kernel,
            in_specs=[VMEM, VMEM] + [ANY] * len(ties),
            out_specs=VMEM,
            out_shape=shaped(left.shape, F32),
            compiler_params=SMALL,
        name="gate_sum",
        )(left, right, *ties)

    def add4(*parts):
        return pl.pallas_call(
            add4_kernel,
            in_specs=[VMEM] * 4 + [ANY] * (len(parts) - 4),
            out_specs=VMEM,
            out_shape=shaped(parts[0].shape, F32),
            compiler_params=SMALL,
        name="gate_sum",
        )(*parts)

    def step(total, axis, *ties):
        with jax.named_scope("gate_" + axis):
            got = [swap(total, axis, mask) for mask in (1, 2, 3)]
        return add4(total, *got, *ties)

    with jax.named_scope("gate_core"):
        got = swap(give, "c", 1)
    total = add(total, got, w_first, w_second)
    (w_first,) = fence((w_first,), total)
    with jax.named_scope("weight_x_far"):
        w_far = pairs(w_first, "x", False)
    total = step(total, "zl", mixed_s, w_far)
    (two,) = fence((two,), total)
    with jax.named_scope("tokens_y"):
        three = ring(two, "y")
    with jax.named_scope("tokens_core"):
        two_s = swap(two, "c", 1)
    with jax.named_scope("gate_zh"):
        got = swap(total, "zh", 1)
    total = add(total, got, two_s, w_far)

    far, far_weight, far_down = pl.pallas_call(
        far_kernel,
        in_specs=[SMEM] + [VMEM] * 12 + [ANY],
        out_specs=[VMEM] * 3,
        out_shape=[
            shaped((3, 2 * tokens, features), BF16),
            shaped((features, width), BF16),
            shaped((features, stacked), BF16),
        ],
        compiler_params=MIDDLE,
        cost_estimate=cost(12 * tokens * depth * features, 18 * tokens * depth),
        name="far_products",
    )(
        at, grad, own_s, one, one_s, two, two_s, all_mixed, mixed_s,
        far_piece, w_first, w_second, w_far, total,
    )
    with jax.named_scope("out_z"):
        far_got = swap(far, "zh", 1)
    (three,) = fence((three,), far)
    with jax.named_scope("tokens_core"):
        three_s = swap(three, "c", 1)
    total = step(total, "x", far)

    last = pl.pallas_call(
        far_last_kernel,
        in_specs=[SMEM] + [VMEM] * 6,
        out_specs=VMEM,
        out_shape=shaped((2 * tokens, features), BF16),
        cost_estimate=cost(4 * tokens * depth * features, 6 * tokens * depth),
        compiler_params=MIDDLE,
        name="far_products_last",
    )(at, three, three_s, all_mixed, mixed_s, far_weight, far_down)
    with jax.named_scope("out_z_last"):
        last_got = swap(last, "zh", 1)

    (total,) = fence((total,), last)
    total = step(total, "y")
    own_rest = products("own_rest", 2, two, two_s, three, three_s, weight, down, last)
    (total,) = fence((total,), far_got, own_rest)
    with jax.named_scope("gate_core_back"):
        other = swap(total, "c", 1)
    gate_grad = jnp.where(
        c == 0, jnp.concatenate([total, other], axis=1), jnp.concatenate([other, total], axis=1)
    )

    out = pl.pallas_call(
        place_kernel,
        in_specs=[SMEM] + [VMEM] * 4,
        out_specs=HBM,
        out_shape=shaped((4, 2, 2, tokens, features), BF16),
        scratch_shapes=[pltpu.SemaphoreType.DMA((16,))],
        compiler_params=MIDDLE,
        name="place",
    )(at, own_near, own_rest, far_got, last_got)
    return gate_grad, out.reshape(16 * tokens, features)


def solution(mesh):
    grid = Mesh(mesh.devices.reshape(4, 4, 4, 2, 2), AXES)
    dp, tensor = ("x", "zl"), ("y", "zh", "c")
    return jax.shard_map(
        on_device,
        mesh=grid,
        in_specs=(
            P(AXES, None),
            P(AXES, None),
            P(dp, tensor),
            P(tensor, None),
            P(tensor, None),
            P(),
            P(),
        ),
        out_specs=(P(), P(dp, tensor)),
        check_vma=False,
    )
```

```python
import functools

import jax
import jax.numpy as jnp
from jax import lax
from jax.experimental import pallas as pl
from jax.experimental.pallas import tpu as pltpu
from jax.sharding import Mesh
from jax.sharding import PartitionSpec as P

F32 = jnp.float32
BF16 = jnp.bfloat16
AXES = ("x", "zl", "y", "zh", "c")
VMEM = pl.BlockSpec(memory_space=pltpu.VMEM)
SMEM = pl.BlockSpec(memory_space=pltpu.SMEM)
ANY = pl.BlockSpec(memory_space=pl.ANY)
HBM = pl.BlockSpec(memory_space=pltpu.HBM)
SMALL = pltpu.CompilerParams(vmem_limit_bytes=8 * 1024 * 1024)
MIDDLE = pltpu.CompilerParams(vmem_limit_bytes=24 * 1024 * 1024)


def ring(value, axis):
    size = lax.axis_size(axis)
    pairs = [
        (2 * i + c, 2 * ((i + 1 - 2 * c) % size) + c) for i in range(size) for c in range(2)
    ]
    return lax.ppermute(value, (axis, "c"), pairs)


def pairs(value, axis, first):
    size = lax.axis_size(axis)
    partner = lambda i, c: i ^ 1 if (c == 0) == first else size - 1 - i
    return lax.ppermute(
        value, (axis, "c"), [(2 * i + c, 2 * partner(i, c) + c) for i in range(size) for c in range(2)]
    )


def fence_kernel(*refs):
    del refs


def fence(values, *ties):
    return pl.pallas_call(
        fence_kernel,
        in_specs=[ANY] * (len(values) + len(ties)),
        out_specs=[ANY] * len(values),
        out_shape=[shaped(v.shape, v.dtype) for v in values],
        input_output_aliases={i: i for i in range(len(values))},
        compiler_params=SMALL,
        name="fence",
    )(*values, *ties)


def back_at(place, core, steps):
    return lax.rem(place - steps * (1 - 2 * core) + 4, 4)


def swap(value, axis, mask):
    size = lax.axis_size(axis)
    return lax.ppermute(value, axis, [(i, i ^ mask) for i in range(size)])


def dot_t(left, right, precision=None):
    return lax.dot_general(
        left, right, (((1,), (1,)), ((), ())), precision=precision, preferred_element_type=F32
    )


def shaped(shape, dtype):
    return jax.ShapeDtypeStruct(shape, dtype)


def cost(flops, moved):
    return pl.CostEstimate(flops=flops, bytes_accessed=moved, transcendentals=0)


def membership(adapters, stacked):
    row = lax.broadcasted_iota(jnp.int32, (adapters, stacked), 0)
    column = lax.broadcasted_iota(jnp.int32, (adapters, stacked), 1)
    low = row * (stacked // adapters)
    return jnp.where((column >= low) & (column < low + stacked // adapters), 1.0, 0.0)


def token_kernel(at, hidden, grad, up, gate, mixed, gates, back):
    stacked = up.shape[0]
    ones = membership(gate.shape[0], stacked)
    wide = lax.dot_general(
        ones.astype(BF16), gate[...], (((0,), (0,)), ((), ())), preferred_element_type=F32
    ).astype(BF16)
    gates[...] = jax.nn.sigmoid(dot_t(gate[...], hidden[...]))
    factor = 2.0 * jax.nn.sigmoid(dot_t(hidden[...], wide))
    pulled = dot_t(grad[...], up[...])
    back[...] = pulled
    mixed[...] = (factor * pulled).astype(BF16)


def act_kernel(at, mixture, down, keep, give):
    c = at[3]
    blocks, _, tokens, depth = mixture.shape
    for out, side in ((give, 1 - c), (keep, c)):
        rows = mixture[:, side].reshape(blocks * tokens, depth)
        value = jnp.dot(rows, down[...], preferred_element_type=F32)
        out[...] = value.reshape(out.shape).astype(out.dtype)


def act_y_kernel(at, keep, got, mixed, first, second, third, rest):
    y = at[1]
    for out, mask in ((first, 1), (second, 2), (third, 3)):
        row = jnp.bitwise_xor(y, mask)
        out[pl.ds(0, 2)] = (keep[row] + got[row].astype(F32)).astype(out.dtype)
        out[2] = mixed[...]
    rest[...] = keep[y] + got[y].astype(F32)


def act_z_kernel(at, rest, first, second, third, mixed, tie, keep, give, all_mixed):
    y, zh = at[1], at[2]
    for out, side in ((give, 1 - zh), (keep, zh)):
        total = (rest[side] + first[side].astype(F32)) + (
            second[side].astype(F32) + third[side].astype(F32)
        )
        out[...] = total.astype(out.dtype)
    all_mixed[y] = mixed[...]
    for ref, mask in ((first, 1), (second, 2), (third, 3)):
        all_mixed[jnp.bitwise_xor(y, mask)] = ref[2]


def gate_kernel(at, keep, got, back, gates, hidden, tie, result, give):
    stacked = keep.shape[1]
    adapters = gates.shape[0]
    half = result.shape[1]
    product = (keep[...] + got[...].astype(F32)) * back[...]
    ones = membership(adapters, stacked)
    delta = 2.0 * dot_t(ones, product, lax.Precision.HIGHEST)
    dlogit = delta * gates[...] * (1.0 - gates[...])
    top = dlogit.astype(BF16).astype(F32)
    middle = (dlogit - top).astype(BF16).astype(F32)
    parts = jnp.concatenate([top, middle, dlogit - top - middle], axis=0).astype(BF16)
    c = at[3]
    for out, side in ((result, c), (give, 1 - c)):
        columns = pl.ds(pl.multiple_of(side * half, 128), half)
        total = jnp.dot(parts, hidden[:, columns], preferred_element_type=F32)
        out[...] = total[:adapters] + (
            total[adapters : 2 * adapters] + total[2 * adapters :]
        )


def add_kernel(left, right, *refs):
    refs[-1][...] = left[...] + right[...]


def add4_kernel(first, second, third, fourth, *refs):
    own = first[...].astype(second.dtype).astype(F32)
    refs[-1][...] = (own + second[...].astype(F32)) + (
        third[...].astype(F32) + fourth[...].astype(F32)
    )


def rows_product(at, steps, refs, mixed, weights, downs, out):
    y, c = at[1], at[3]
    both = jnp.concatenate([ref[...] for ref in refs], axis=0)
    ranks = jnp.concatenate(
        [mixed[0][back_at(y, c, steps)], mixed[1][back_at(y, 1 - c, steps)]], axis=0
    )
    value = dot_t(both, weights[...]) + dot_t(ranks, downs[...])
    out[...] = value.astype(out.dtype)


def far_kernel(at, own, own_s, one, one_s, two, two_s, mixed, mixed_s, *refs):
    pieces, (tie, out, weight, down) = refs[:4], refs[4:]
    width = weight.shape[1]
    rows = pieces[0].shape[0]
    x, c = at[0], at[3]
    up, turned = jnp.bitwise_xor(x, 1), 3 - x
    first, second = jnp.where(c == 0, up, turned), jnp.where(c == 0, turned, up)
    for place, ref in zip((x, first, second, jnp.bitwise_xor(x, 2)), pieces):
        place = pl.ds(pl.multiple_of(place * rows, rows), rows)
        weight[place, :] = ref[:, :width]
        down[place, :] = ref[:, width:]
    for steps, group in enumerate(((own, own_s), (one, one_s), (two, two_s))):
        rows_product(at, steps, group, (mixed, mixed_s), weight, down, out.at[steps])


def far_last_kernel(at, three, three_s, mixed, mixed_s, weight, down, tie, out):
    rows_product(at, 3, (three, three_s), (mixed, mixed_s), weight, down, out)


def product_kernel(first, at, near, near_s, more, more_s, mixed, mixed_s, weight, down, tie, out):
    for number, group in enumerate(((near, near_s), (more, more_s))):
        rows_product(at, first + number, group, (mixed, mixed_s), weight, down, out.at[number])


def place_kernel(at, near, rest, got, last, out, sems):
    y, zh, c = at[1], at[2], at[3]
    tokens = out.shape[3]
    copies = []
    for steps in range(4):
        own = near.at[steps] if steps < 2 else rest.at[steps - 2]
        other = got.at[steps] if steps < 3 else last
        for ref, side in ((own, zh), (other, 1 - zh)):
            for half, core in ((0, c), (1, 1 - c)):
                copies.append(
                    pltpu.make_async_copy(
                        ref.at[pl.ds(half * tokens, tokens)],
                        out.at[back_at(y, core, steps), side, core],
                        sems.at[len(copies)],
                    )
                )
    for copy in copies:
        copy.start()
    for copy in copies:
        copy.wait()


def on_device(hidden, grad, mixture, weight, down, up, gate_matrix):
    tokens, width = grad.shape
    adapters = gate_matrix.shape[0]
    stacked = up.shape[0]
    features = weight.shape[0]
    depth = width + stacked
    quarter = features // 4
    x, y, zh, c = (lax.axis_index(a) for a in ("x", "y", "zh", "c"))
    at = jnp.stack([x, y, zh, c]).astype(jnp.int32)

    with jax.named_scope("weight_z"):
        piece = jnp.concatenate(
            [lax.dynamic_slice_in_dim(v, x * quarter, quarter, 0) for v in (weight, down)], axis=1
        )
        far_piece = swap(piece, "zh", 1)
    with jax.named_scope("tokens_y"):
        one = ring(grad, "y")
    with jax.named_scope("tokens_core"):
        own_s = swap(grad, "c", 1)

    keep, give = pl.pallas_call(
        act_kernel,
        in_specs=[SMEM, VMEM, VMEM],
        out_specs=[VMEM, VMEM],
        out_shape=[
            shaped((4, 2, tokens, stacked), F32),
            shaped((4, 2, tokens, stacked), BF16),
        ],
        compiler_params=SMALL,
        cost_estimate=cost(2 * mixture.size * stacked, 4 * mixture.size),
        name="rank_products",
    )(at, mixture.reshape(8, 2, tokens, -1), down)
    with jax.named_scope("act_core"):
        got = swap(give, "c", 1)
    mixed, gates, back = pl.pallas_call(
        token_kernel,
        in_specs=[SMEM] + [VMEM] * 4,
        out_specs=[VMEM, VMEM, VMEM],
        out_shape=[
            shaped((tokens, stacked), BF16),
            shaped((adapters, tokens), F32),
            shaped((tokens, stacked), F32),
        ],
        compiler_params=SMALL,
        cost_estimate=cost(6 * tokens * width * stacked, 12 * tokens * width),
        name="token_values",
    )(at, hidden, grad, up, gate_matrix)
    first, second, third, rest = pl.pallas_call(
        act_y_kernel,
        in_specs=[SMEM, VMEM, VMEM, VMEM],
        out_specs=[VMEM] * 4,
        out_shape=[shaped((3, tokens, stacked), BF16)] * 3 + [shaped((2, tokens, stacked), F32)],
        compiler_params=SMALL,
        name="rank_sum_core",
    )(at, keep, got, mixed)
    with jax.named_scope("act_y"):
        first, second, third = (
            swap(v, "y", mask) for v, mask in ((first, 1), (second, 2), (third, 3))
        )
    keep, give, all_mixed = pl.pallas_call(
        act_z_kernel,
        in_specs=[SMEM] + [VMEM] * 5 + [ANY],
        out_specs=[VMEM] * 3,
        out_shape=[
            shaped((tokens, stacked), F32),
            shaped((tokens, stacked), BF16),
            shaped((4, tokens, stacked), BF16),
        ],
        compiler_params=SMALL,
        name="rank_sum_y",
    )(at, rest, first, second, third, mixed, own_s)
    one, far_piece = fence((one, far_piece), give)
    with jax.named_scope("tokens_y"):
        two = ring(one, "y")
    with jax.named_scope("tokens_core"):
        one_s = swap(one, "c", 1)
    with jax.named_scope("weight_x"):
        w_first = pairs(far_piece, "x", True)
        w_second = pairs(far_piece, "x", False)
    with jax.named_scope("act_z"):
        message = swap(give, "zh", 1)
    with jax.named_scope("mixed_core"):
        mixed_s = swap(all_mixed, "c", 1)

    def products(name, first, near, near_s, more, more_s, weights, downs, tie):
        return pl.pallas_call(
            functools.partial(product_kernel, first),
            in_specs=[SMEM] + [VMEM] * 8 + [ANY],
            out_specs=VMEM,
            out_shape=shaped((2, 2 * tokens, features), BF16),
            compiler_params=MIDDLE,
            cost_estimate=cost(8 * tokens * depth * features, 12 * tokens * depth),
            name=name,
        )(at, near, near_s, more, more_s, all_mixed, mixed_s, weights, downs, tie)

    own_near = products("own_near", 0, grad, own_s, one, one_s, weight, down, give)

    total, give = pl.pallas_call(
        gate_kernel,
        in_specs=[SMEM] + [VMEM] * 5 + [ANY],
        out_specs=[VMEM, VMEM],
        out_shape=[shaped((adapters, width // 2), F32)] * 2,
        compiler_params=SMALL,
        name="gate_products",
    )(at, keep, message, back, gates, hidden, own_near)

    def add(left, right, *ties):
        return pl.pallas_call(
            add_kernel,
            in_specs=[VMEM, VMEM] + [ANY] * len(ties),
            out_specs=VMEM,
            out_shape=shaped(left.shape, F32),
            compiler_params=SMALL,
        name="gate_sum",
        )(left, right, *ties)

    def add4(*parts):
        return pl.pallas_call(
            add4_kernel,
            in_specs=[VMEM] * 4 + [ANY] * (len(parts) - 4),
            out_specs=VMEM,
            out_shape=shaped(parts[0].shape, F32),
            compiler_params=SMALL,
        name="gate_sum",
        )(*parts)

    def step(total, axis, *ties, dtype=F32):
        with jax.named_scope("gate_" + axis):
            got = [swap(total.astype(dtype), axis, mask) for mask in (1, 2, 3)]
        return add4(total, *got, *ties)

    with jax.named_scope("gate_core"):
        got = swap(give, "c", 1)
    total = add(total, got, w_first, w_second)
    (w_first,) = fence((w_first,), total)
    with jax.named_scope("weight_x_far"):
        w_far = pairs(w_first, "x", False)
    (two,) = fence((two,), w_first)
    with jax.named_scope("tokens_y"):
        three = ring(two, "y")
    total = step(total, "zl", mixed_s, w_far, two, dtype=BF16)
    with jax.named_scope("tokens_core"):
        two_s = swap(two, "c", 1)

    far, far_weight, far_down = pl.pallas_call(
        far_kernel,
        in_specs=[SMEM] + [VMEM] * 12 + [ANY],
        out_specs=[VMEM] * 3,
        out_shape=[
            shaped((3, 2 * tokens, features), BF16),
            shaped((features, width), BF16),
            shaped((features, stacked), BF16),
        ],
        compiler_params=MIDDLE,
        cost_estimate=cost(12 * tokens * depth * features, 18 * tokens * depth),
        name="far_products",
    )(
        at, grad, own_s, one, one_s, two, two_s, all_mixed, mixed_s,
        far_piece, w_first, w_second, w_far, total,
    )
    with jax.named_scope("out_z"):
        far_got = swap(far, "zh", 1)
    total = step(total, "x", far)
    (three,) = fence((three,), total)
    with jax.named_scope("tokens_core"):
        three_s = swap(three, "c", 1)

    total = step(total, "y")
    last = pl.pallas_call(
        far_last_kernel,
        in_specs=[SMEM] + [VMEM] * 6 + [ANY],
        out_specs=VMEM,
        out_shape=shaped((2 * tokens, features), BF16),
        cost_estimate=cost(4 * tokens * depth * features, 6 * tokens * depth),
        compiler_params=MIDDLE,
        name="far_products_last",
    )(at, three, three_s, all_mixed, mixed_s, far_weight, far_down, total)
    with jax.named_scope("out_z_last"):
        last_got = swap(last, "zh", 1)

    own_rest = products("own_rest", 2, two, two_s, three, three_s, weight, down, far)
    with jax.named_scope("gate_zh"):
        got = swap(total, "zh", 1)
    total = add(total, got, last, far_got)
    with jax.named_scope("gate_core_back"):
        other = swap(total, "c", 1)
    gate_grad = jnp.where(
        c == 0, jnp.concatenate([total, other], axis=1), jnp.concatenate([other, total], axis=1)
    )

    out = pl.pallas_call(
        place_kernel,
        in_specs=[SMEM] + [VMEM] * 4,
        out_specs=HBM,
        out_shape=shaped((4, 2, 2, tokens, features), BF16),
        scratch_shapes=[pltpu.SemaphoreType.DMA((16,))],
        compiler_params=MIDDLE,
        name="place",
    )(at, own_near, own_rest, far_got, last_got)
    return gate_grad, out.reshape(16 * tokens, features)


def solution(mesh):
    grid = Mesh(mesh.devices.reshape(4, 4, 4, 2, 2), AXES)
    dp, tensor = ("x", "zl"), ("y", "zh", "c")
    return jax.shard_map(
        on_device,
        mesh=grid,
        in_specs=(
            P(AXES, None),
            P(AXES, None),
            P(dp, tensor),
            P(tensor, None),
            P(tensor, None),
            P(),
            P(),
        ),
        out_specs=(P(), P(dp, tensor)),
        check_vma=False,
    )
```

```python
import functools

import jax
import jax.numpy as jnp
from jax import lax
from jax.experimental import pallas as pl
from jax.experimental.pallas import tpu as pltpu
from jax.sharding import Mesh
from jax.sharding import PartitionSpec as P

F32 = jnp.float32
BF16 = jnp.bfloat16
AXES = ("x", "zl", "y", "zh", "c")
VMEM = pl.BlockSpec(memory_space=pltpu.VMEM)
SMEM = pl.BlockSpec(memory_space=pltpu.SMEM)
ANY = pl.BlockSpec(memory_space=pl.ANY)
HBM = pl.BlockSpec(memory_space=pltpu.HBM)
SMALL = pltpu.CompilerParams(vmem_limit_bytes=8 * 1024 * 1024)
MIDDLE = pltpu.CompilerParams(vmem_limit_bytes=16 * 1024 * 1024)


def ring(value, axis):
    size = lax.axis_size(axis)
    pairs = [
        (2 * i + c, 2 * ((i + 1 - 2 * c) % size) + c) for i in range(size) for c in range(2)
    ]
    return lax.ppermute(value, (axis, "c"), pairs)


def pairs(value, axis, first):
    size = lax.axis_size(axis)
    partner = lambda i, c: i ^ 1 if (c == 0) == first else size - 1 - i
    return lax.ppermute(
        value, (axis, "c"), [(2 * i + c, 2 * partner(i, c) + c) for i in range(size) for c in range(2)]
    )


def fence_kernel(*refs):
    del refs


def fence(values, *ties):
    return pl.pallas_call(
        fence_kernel,
        in_specs=[ANY] * (len(values) + len(ties)),
        out_specs=[ANY] * len(values),
        out_shape=[shaped(v.shape, v.dtype) for v in values],
        input_output_aliases={i: i for i in range(len(values))},
        compiler_params=SMALL,
        name="fence",
    )(*values, *ties)


def back_at(place, core, steps):
    return lax.rem(place - steps * (1 - 2 * core) + 4, 4)


def swap(value, axis, mask):
    size = lax.axis_size(axis)
    return lax.ppermute(value, axis, [(i, i ^ mask) for i in range(size)])


def dot_t(left, right, precision=None):
    return lax.dot_general(
        left, right, (((1,), (1,)), ((), ())), precision=precision, preferred_element_type=F32
    )


def shaped(shape, dtype):
    return jax.ShapeDtypeStruct(shape, dtype)


def cost(flops, moved):
    return pl.CostEstimate(flops=flops, bytes_accessed=moved, transcendentals=0)


def membership(adapters, stacked):
    row = lax.broadcasted_iota(jnp.int32, (adapters, stacked), 0)
    column = lax.broadcasted_iota(jnp.int32, (adapters, stacked), 1)
    low = row * (stacked // adapters)
    return jnp.where((column >= low) & (column < low + stacked // adapters), 1.0, 0.0)


def join_kernel(side, mine, got, tie, out):
    rows = mine.shape[0]
    for place, ref in ((side[0], mine), (1 - side[0], got)):
        out[pl.ds(pl.multiple_of(place * rows, rows), rows), :] = ref[...]


def join(side, mine, got, tie):
    return pl.pallas_call(
        join_kernel,
        in_specs=[SMEM, VMEM, VMEM, ANY],
        out_specs=VMEM,
        out_shape=shaped((2 * mine.shape[0], mine.shape[1]), mine.dtype),
        compiler_params=SMALL,
        name="join",
    )(side.reshape(1), mine, got, tie)


def token_kernel(at, hidden, grad, up, gate, mixed, gates, back):
    stacked = up.shape[0]
    ones = membership(gate.shape[0], stacked)
    wide = lax.dot_general(
        ones.astype(BF16), gate[...], (((0,), (0,)), ((), ())), preferred_element_type=F32
    ).astype(BF16)
    gates[...] = jax.nn.sigmoid(dot_t(gate[...], hidden[...]))
    factor = 2.0 * jax.nn.sigmoid(dot_t(hidden[...], wide))
    pulled = dot_t(grad[...], up[...])
    back[...] = pulled
    mixed[...] = (factor * pulled).astype(BF16)


def act_kernel(at, mixture, down, keep, give):
    c = at[3]
    blocks, _, tokens, depth = mixture.shape
    for out, side in ((give, 1 - c), (keep, c)):
        rows = mixture[:, side].reshape(blocks * tokens, depth)
        value = jnp.dot(rows, down[...], preferred_element_type=F32)
        out[...] = value.reshape(out.shape).astype(out.dtype)


def act_y_kernel(at, keep, got, mixed, first, second, third, rest):
    y = at[1]
    for out, mask in ((first, 1), (second, 2), (third, 3)):
        row = jnp.bitwise_xor(y, mask)
        out[pl.ds(0, 2)] = (keep[row] + got[row].astype(F32)).astype(out.dtype)
        out[2] = mixed[...]
    rest[...] = keep[y] + got[y].astype(F32)


def act_z_kernel(at, rest, first, second, third, mixed, tie, tie_too, keep, give, all_mixed):
    y, zh = at[1], at[2]
    for out, side in ((give, 1 - zh), (keep, zh)):
        total = (rest[side] + first[side].astype(F32)) + (
            second[side].astype(F32) + third[side].astype(F32)
        )
        out[...] = total.astype(out.dtype)
    all_mixed[y] = mixed[...]
    for ref, mask in ((first, 1), (second, 2), (third, 3)):
        all_mixed[jnp.bitwise_xor(y, mask)] = ref[2]


def gate_kernel(at, keep, got, back, gates, hidden, tie, result, give):
    stacked = keep.shape[1]
    adapters = gates.shape[0]
    half = result.shape[1]
    product = (keep[...] + got[...].astype(F32)) * back[...]
    ones = membership(adapters, stacked)
    delta = 2.0 * dot_t(ones, product, lax.Precision.HIGHEST)
    dlogit = delta * gates[...] * (1.0 - gates[...])
    top = dlogit.astype(BF16).astype(F32)
    middle = (dlogit - top).astype(BF16).astype(F32)
    parts = jnp.concatenate([top, middle, dlogit - top - middle], axis=0).astype(BF16)
    c = at[3]
    for out, side in ((result, c), (give, 1 - c)):
        columns = pl.ds(pl.multiple_of(side * half, 128), half)
        total = jnp.dot(parts, hidden[:, columns], preferred_element_type=F32)
        out[...] = total[:adapters] + (
            total[adapters : 2 * adapters] + total[2 * adapters :]
        )


def add_kernel(left, right, *refs):
    refs[-1][...] = left[...] + right[...]


def add4_kernel(first, second, third, fourth, *refs):
    own = first[...].astype(second.dtype).astype(F32)
    refs[-1][...] = (own + second[...].astype(F32)) + (
        third[...].astype(F32) + fourth[...].astype(F32)
    )


def rows_product(at, steps, refs, mixed, weights, downs, out):
    y, c = at[1], at[3]
    both = jnp.concatenate([ref[...] for ref in refs], axis=0)
    ranks = jnp.concatenate(
        [mixed[0][back_at(y, c, steps)], mixed[1][back_at(y, 1 - c, steps)]], axis=0
    )
    value = dot_t(both, weights[...]) + dot_t(ranks, downs[...])
    out[...] = value.astype(out.dtype)


def far_kernel(at, own, own_s, one, one_s, two, two_s, mixed, mixed_s, *refs):
    pieces, (tie, out, weight, down) = refs[:4], refs[4:]
    width = weight.shape[1]
    rows = pieces[0].shape[0]
    x, c = at[0], at[3]
    up, turned = jnp.bitwise_xor(x, 1), 3 - x
    first, second = jnp.where(c == 0, up, turned), jnp.where(c == 0, turned, up)
    for place, ref in zip((x, first, second, jnp.bitwise_xor(x, 2)), pieces):
        place = pl.ds(pl.multiple_of(place * rows, rows), rows)
        weight[place, :] = ref[:, :width]
        down[place, :] = ref[:, width:]
    for steps, group in enumerate(((own, own_s), (one, one_s), (two, two_s))):
        rows_product(at, steps, group, (mixed, mixed_s), weight, down, out.at[steps])


def far_last_kernel(at, three, three_s, mixed, mixed_s, weight, down, tie, out):
    rows_product(at, 3, (three, three_s), (mixed, mixed_s), weight, down, out)


def product_kernel(first, at, near, near_s, more, more_s, mixed, mixed_s, weight, down, tie, out):
    for number, group in enumerate(((near, near_s), (more, more_s))):
        rows_product(at, first + number, group, (mixed, mixed_s), weight, down, out.at[number])


def place_kernel(at, near, rest, got, last, out, sems):
    y, zh, c = at[1], at[2], at[3]
    tokens = out.shape[3]
    copies = []
    for steps in range(4):
        own = near.at[steps] if steps < 2 else rest.at[steps - 2]
        other = got.at[steps] if steps < 3 else last
        for ref, side in ((own, zh), (other, 1 - zh)):
            for half, core in ((0, c), (1, 1 - c)):
                copies.append(
                    pltpu.make_async_copy(
                        ref.at[pl.ds(half * tokens, tokens)],
                        out.at[back_at(y, core, steps), side, core],
                        sems.at[len(copies)],
                    )
                )
    for copy in copies:
        copy.start()
    for copy in copies:
        copy.wait()


def on_device(hidden, grad, mixture, weight, down, up, gate_matrix):
    tokens, width = grad.shape
    adapters = gate_matrix.shape[0]
    stacked = up.shape[0]
    features = weight.shape[0]
    depth = width + stacked
    quarter = features // 4
    x, y, zl, zh, c = (lax.axis_index(a) for a in ("x", "y", "zl", "zh", "c"))
    at = jnp.stack([x, y, zh, c]).astype(jnp.int32)

    with jax.named_scope("weight_z"):
        start = x * quarter + (zl % 2) * (quarter // 2)
        piece = jnp.concatenate(
            [lax.dynamic_slice_in_dim(v, start, quarter // 2, 0) for v in (weight, down)], axis=1
        )
        far_piece = swap(piece, "zh", 1)
    with jax.named_scope("tokens_y"):
        one = ring(grad, "y")
    with jax.named_scope("tokens_core"):
        own_s = swap(grad, "c", 1)

    keep, give = pl.pallas_call(
        act_kernel,
        in_specs=[SMEM, VMEM, VMEM],
        out_specs=[VMEM, VMEM],
        out_shape=[
            shaped((4, 2, tokens, stacked), F32),
            shaped((4, 2, tokens, stacked), BF16),
        ],
        compiler_params=SMALL,
        cost_estimate=cost(2 * mixture.size * stacked, 4 * mixture.size),
        name="rank_products",
    )(at, mixture.reshape(8, 2, tokens, -1), down)
    with jax.named_scope("act_core"):
        got = swap(give, "c", 1)
    mixed, gates, back = pl.pallas_call(
        token_kernel,
        in_specs=[SMEM] + [VMEM] * 4,
        out_specs=[VMEM, VMEM, VMEM],
        out_shape=[
            shaped((tokens, stacked), BF16),
            shaped((adapters, tokens), F32),
            shaped((tokens, stacked), F32),
        ],
        compiler_params=SMALL,
        cost_estimate=cost(6 * tokens * width * stacked, 12 * tokens * width),
        name="token_values",
    )(at, hidden, grad, up, gate_matrix)
    first, second, third, rest = pl.pallas_call(
        act_y_kernel,
        in_specs=[SMEM, VMEM, VMEM, VMEM],
        out_specs=[VMEM] * 4,
        out_shape=[shaped((3, tokens, stacked), BF16)] * 3 + [shaped((2, tokens, stacked), F32)],
        compiler_params=SMALL,
        name="rank_sum_core",
    )(at, keep, got, mixed)
    (far_piece,) = fence((far_piece,), rest)
    with jax.named_scope("weight_zl"):
        z_got = swap(far_piece, "zl", 1)
    with jax.named_scope("act_y"):
        first, second, third = (
            swap(v, "y", mask) for v, mask in ((first, 1), (second, 2), (third, 3))
        )
    keep, give, all_mixed = pl.pallas_call(
        act_z_kernel,
        in_specs=[SMEM] + [VMEM] * 5 + [ANY] * 2,
        out_specs=[VMEM] * 3,
        out_shape=[
            shaped((tokens, stacked), F32),
            shaped((tokens, stacked), BF16),
            shaped((4, tokens, stacked), BF16),
        ],
        compiler_params=SMALL,
        name="rank_sum_y",
    )(at, rest, first, second, third, mixed, own_s, z_got)
    far_piece = join(zl % 2, far_piece, z_got, give)
    (give,) = fence((give,), far_piece)
    with jax.named_scope("act_z"):
        message = swap(give, "zh", 1)
    with jax.named_scope("weight_x"):
        w_first = pairs(far_piece, "x", True)
        w_second = pairs(far_piece, "x", False)
    (one,) = fence((one,), message)
    with jax.named_scope("tokens_y"):
        two = ring(one, "y")
    with jax.named_scope("tokens_core"):
        one_s = swap(one, "c", 1)
    with jax.named_scope("mixed_core"):
        mixed_s = swap(all_mixed, "c", 1)

    def products(name, first, near, near_s, more, more_s, weights, downs, tie):
        return pl.pallas_call(
            functools.partial(product_kernel, first),
            in_specs=[SMEM] + [VMEM] * 8 + [ANY],
            out_specs=VMEM,
            out_shape=shaped((2, 2 * tokens, features), BF16),
            compiler_params=MIDDLE,
            cost_estimate=cost(8 * tokens * depth * features, 12 * tokens * depth),
            name=name,
        )(at, near, near_s, more, more_s, all_mixed, mixed_s, weights, downs, tie)

    total, give = pl.pallas_call(
        gate_kernel,
        in_specs=[SMEM] + [VMEM] * 5 + [ANY],
        out_specs=[VMEM, VMEM],
        out_shape=[shaped((adapters, width // 2), F32)] * 2,
        compiler_params=SMALL,
        name="gate_products",
    )(at, keep, message, back, gates, hidden, far_piece)

    def add(left, right, *ties):
        return pl.pallas_call(
            add_kernel,
            in_specs=[VMEM, VMEM] + [ANY] * len(ties),
            out_specs=VMEM,
            out_shape=shaped(left.shape, F32),
            compiler_params=SMALL,
        name="gate_sum",
        )(left, right, *ties)

    def add4(*parts):
        return pl.pallas_call(
            add4_kernel,
            in_specs=[VMEM] * 4 + [ANY] * (len(parts) - 4),
            out_specs=VMEM,
            out_shape=shaped(parts[0].shape, F32),
            compiler_params=SMALL,
        name="gate_sum",
        )(*parts)

    def step(total, axis, *ties, dtype=F32):
        with jax.named_scope("gate_" + axis):
            got = [swap(total.astype(dtype), axis, mask) for mask in (1, 2, 3)]
        return add4(total, *got, *ties)

    with jax.named_scope("gate_core"):
        got = swap(give, "c", 1)
    total = add(total, got)
    total = step(total, "zl", mixed_s, w_first, w_second, dtype=BF16)
    (w_first,) = fence((w_first,), total)
    with jax.named_scope("weight_x_far"):
        w_far = pairs(w_first, "x", False)
    (two,) = fence((two,), total)
    with jax.named_scope("tokens_y"):
        three = ring(two, "y")
    with jax.named_scope("gate_zh"):
        got = swap(total, "zh", 1)
    with jax.named_scope("tokens_core"):
        two_s = swap(two, "c", 1)
    total = add(total, got, two_s, w_far)

    far, far_weight, far_down = pl.pallas_call(
        far_kernel,
        in_specs=[SMEM] + [VMEM] * 12 + [ANY],
        out_specs=[VMEM] * 3,
        out_shape=[
            shaped((3, 2 * tokens, features), BF16),
            shaped((features, width), BF16),
            shaped((features, stacked), BF16),
        ],
        compiler_params=MIDDLE,
        cost_estimate=cost(12 * tokens * depth * features, 18 * tokens * depth),
        name="far_products",
    )(
        at, grad, own_s, one, one_s, two, two_s, all_mixed, mixed_s,
        far_piece, w_first, w_second, w_far, total,
    )
    with jax.named_scope("out_z"):
        far_got = swap(far, "zh", 1)
    total = step(total, "x", far)
    (three,) = fence((three,), total)
    with jax.named_scope("tokens_core"):
        three_s = swap(three, "c", 1)

    total = step(total, "y")
    last = pl.pallas_call(
        far_last_kernel,
        in_specs=[SMEM] + [VMEM] * 6 + [ANY],
        out_specs=VMEM,
        out_shape=shaped((2 * tokens, features), BF16),
        cost_estimate=cost(4 * tokens * depth * features, 6 * tokens * depth),
        compiler_params=MIDDLE,
        name="far_products_last",
    )(at, three, three_s, all_mixed, mixed_s, far_weight, far_down, total)
    with jax.named_scope("out_z_last"):
        last_got = swap(last, "zh", 1)

    own_near = products("own_near", 0, grad, own_s, one, one_s, weight, down, far)
    own_rest = products("own_rest", 2, two, two_s, three, three_s, weight, down, far)
    (total,) = fence((total,), last)
    with jax.named_scope("gate_core_back"):
        other = swap(total, "c", 1)
    gate_grad = jnp.where(
        c == 0, jnp.concatenate([total, other], axis=1), jnp.concatenate([other, total], axis=1)
    )

    out = pl.pallas_call(
        place_kernel,
        in_specs=[SMEM] + [VMEM] * 4,
        out_specs=HBM,
        out_shape=shaped((4, 2, 2, tokens, features), BF16),
        scratch_shapes=[pltpu.SemaphoreType.DMA((16,))],
        compiler_params=MIDDLE,
        name="place",
    )(at, own_near, own_rest, far_got, last_got)
    return gate_grad, out.reshape(16 * tokens, features)


def solution(mesh):
    grid = Mesh(mesh.devices.reshape(4, 4, 4, 2, 2), AXES)
    dp, tensor = ("x", "zl"), ("y", "zh", "c")
    return jax.shard_map(
        on_device,
        mesh=grid,
        in_specs=(
            P(AXES, None),
            P(AXES, None),
            P(dp, tensor),
            P(tensor, None),
            P(tensor, None),
            P(),
            P(),
        ),
        out_specs=(P(), P(dp, tensor)),
        check_vma=False,
    )
```

```python
import functools

import jax
import jax.numpy as jnp
from jax import lax
from jax.experimental import pallas as pl
from jax.experimental.pallas import tpu as pltpu
from jax.sharding import Mesh
from jax.sharding import PartitionSpec as P

F32 = jnp.float32
BF16 = jnp.bfloat16
AXES = ("x", "zl", "y", "zh", "c")
VMEM = pl.BlockSpec(memory_space=pltpu.VMEM)
SMEM = pl.BlockSpec(memory_space=pltpu.SMEM)
ANY = pl.BlockSpec(memory_space=pl.ANY)
HBM = pl.BlockSpec(memory_space=pltpu.HBM)
SMALL = pltpu.CompilerParams(vmem_limit_bytes=8 * 1024 * 1024)
MIDDLE = pltpu.CompilerParams(vmem_limit_bytes=16 * 1024 * 1024)


def ring(value, axis):
    size = lax.axis_size(axis)
    pairs = [
        (2 * i + c, 2 * ((i + 1 - 2 * c) % size) + c) for i in range(size) for c in range(2)
    ]
    return lax.ppermute(value, (axis, "c"), pairs)


def pairs(value, axis, first):
    size = lax.axis_size(axis)
    partner = lambda i, c: i ^ 1 if (c == 0) == first else size - 1 - i
    return lax.ppermute(
        value, (axis, "c"), [(2 * i + c, 2 * partner(i, c) + c) for i in range(size) for c in range(2)]
    )


def fence_kernel(*refs):
    del refs


def fence(values, *ties):
    return pl.pallas_call(
        fence_kernel,
        in_specs=[ANY] * (len(values) + len(ties)),
        out_specs=[ANY] * len(values),
        out_shape=[shaped(v.shape, v.dtype) for v in values],
        input_output_aliases={i: i for i in range(len(values))},
        compiler_params=SMALL,
        name="fence",
    )(*values, *ties)


def back_at(place, core, steps):
    return lax.rem(place - steps * (1 - 2 * core) + 4, 4)


def swap(value, axis, mask):
    size = lax.axis_size(axis)
    return lax.ppermute(value, axis, [(i, i ^ mask) for i in range(size)])


def dot_t(left, right, precision=None):
    return lax.dot_general(
        left, right, (((1,), (1,)), ((), ())), precision=precision, preferred_element_type=F32
    )


def shaped(shape, dtype):
    return jax.ShapeDtypeStruct(shape, dtype)


def cost(flops, moved):
    return pl.CostEstimate(flops=flops, bytes_accessed=moved, transcendentals=0)


def membership(adapters, stacked):
    row = lax.broadcasted_iota(jnp.int32, (adapters, stacked), 0)
    column = lax.broadcasted_iota(jnp.int32, (adapters, stacked), 1)
    low = row * (stacked // adapters)
    return jnp.where((column >= low) & (column < low + stacked // adapters), 1.0, 0.0)


def token_kernel(at, hidden, grad, up, gate, mixed, gates, back):
    stacked = up.shape[0]
    ones = membership(gate.shape[0], stacked)
    wide = lax.dot_general(
        ones.astype(BF16), gate[...], (((0,), (0,)), ((), ())), preferred_element_type=F32
    ).astype(BF16)
    gates[...] = jax.nn.sigmoid(dot_t(gate[...], hidden[...]))
    factor = 2.0 * jax.nn.sigmoid(dot_t(hidden[...], wide))
    pulled = dot_t(grad[...], up[...])
    back[...] = pulled
    mixed[...] = (factor * pulled).astype(BF16)


def act_kernel(at, mixture, down, keep, give):
    c = at[3]
    blocks, _, tokens, depth = mixture.shape
    for out, side in ((give, 1 - c), (keep, c)):
        rows = mixture[:, side].reshape(blocks * tokens, depth)
        value = jnp.dot(rows, down[...], preferred_element_type=F32)
        out[...] = value.reshape(out.shape).astype(out.dtype)


def act_y_kernel(at, keep, got, mixed, first, second, third, rest):
    y = at[1]
    for out, mask in ((first, 1), (second, 2), (third, 3)):
        row = jnp.bitwise_xor(y, mask)
        out[pl.ds(0, 2)] = (keep[row] + got[row].astype(F32)).astype(out.dtype)
        out[2] = mixed[...]
    rest[...] = keep[y] + got[y].astype(F32)


def act_z_kernel(at, rest, first, second, third, mixed, tie, keep, give, all_mixed):
    y, zh = at[1], at[2]
    for out, side in ((give, 1 - zh), (keep, zh)):
        total = (rest[side] + first[side].astype(F32)) + (
            second[side].astype(F32) + third[side].astype(F32)
        )
        out[...] = total.astype(out.dtype)
    all_mixed[y] = mixed[...]
    for ref, mask in ((first, 1), (second, 2), (third, 3)):
        all_mixed[jnp.bitwise_xor(y, mask)] = ref[2]


def gate_kernel(at, keep, got, back, gates, hidden, tie, result, give):
    stacked = keep.shape[1]
    adapters = gates.shape[0]
    half = result.shape[1]
    product = (keep[...] + got[...].astype(F32)) * back[...]
    ones = membership(adapters, stacked)
    delta = 2.0 * dot_t(ones, product, lax.Precision.HIGHEST)
    dlogit = delta * gates[...] * (1.0 - gates[...])
    top = dlogit.astype(BF16).astype(F32)
    middle = (dlogit - top).astype(BF16).astype(F32)
    parts = jnp.concatenate([top, middle, dlogit - top - middle], axis=0).astype(BF16)
    c = at[3]
    for out, side in ((result, c), (give, 1 - c)):
        columns = pl.ds(pl.multiple_of(side * half, 128), half)
        total = jnp.dot(parts, hidden[:, columns], preferred_element_type=F32)
        out[...] = total[:adapters] + (
            total[adapters : 2 * adapters] + total[2 * adapters :]
        )


def add_kernel(left, right, *refs):
    total = left[...] + right[...]
    refs[-2][...] = total
    refs[-1][...] = total.astype(refs[-1].dtype)


def halves_kernel(at, mine, other, out):
    half = mine.shape[1]
    c = at[3]
    for side, ref in ((c, mine), (1 - c, other)):
        out[:, pl.ds(pl.multiple_of(side * half, 128), half)] = ref[...]


def add4_kernel(first, second, third, fourth, *refs):
    own = first[...].astype(second.dtype).astype(F32)
    refs[-1][...] = (own + second[...].astype(F32)) + (
        third[...].astype(F32) + fourth[...].astype(F32)
    )


def rows_product(at, steps, refs, mixed, weights, downs, out):
    y, c = at[1], at[3]
    both = jnp.concatenate([ref[...] for ref in refs], axis=0)
    ranks = jnp.concatenate(
        [mixed[0][back_at(y, c, steps)], mixed[1][back_at(y, 1 - c, steps)]], axis=0
    )
    value = dot_t(both, weights[...]) + dot_t(ranks, downs[...])
    out[...] = value.astype(out.dtype)


def far_kernel(at, own, own_s, one, one_s, two, two_s, mixed, mixed_s, *refs):
    pieces, (tie, out, weight, down) = refs[:4], refs[4:]
    width = weight.shape[1]
    rows = pieces[0].shape[0]
    x, c = at[0], at[3]
    up, turned = jnp.bitwise_xor(x, 1), 3 - x
    first, second = jnp.where(c == 0, up, turned), jnp.where(c == 0, turned, up)
    for place, ref in zip((x, first, second, jnp.bitwise_xor(x, 2)), pieces):
        place = pl.ds(pl.multiple_of(place * rows, rows), rows)
        weight[place, :] = ref[:, :width]
        down[place, :] = ref[:, width:]
    for steps, group in enumerate(((own, own_s), (one, one_s), (two, two_s))):
        rows_product(at, steps, group, (mixed, mixed_s), weight, down, out.at[steps])


def far_last_kernel(at, three, three_s, mixed, mixed_s, weight, down, tie, out):
    rows_product(at, 3, (three, three_s), (mixed, mixed_s), weight, down, out)


def product_kernel(first, at, near, near_s, more, more_s, mixed, mixed_s, weight, down, tie, out):
    for number, group in enumerate(((near, near_s), (more, more_s))):
        rows_product(at, first + number, group, (mixed, mixed_s), weight, down, out.at[number])


def place_kernel(at, near, rest, got, last, out, sems):
    y, zh, c = at[1], at[2], at[3]
    tokens = out.shape[3]
    copies = []
    for steps in range(4):
        own = near.at[steps] if steps < 2 else rest.at[steps - 2]
        other = got.at[steps] if steps < 3 else last
        for ref, side in ((own, zh), (other, 1 - zh)):
            for half, core in ((0, c), (1, 1 - c)):
                copies.append(
                    pltpu.make_async_copy(
                        ref.at[pl.ds(half * tokens, tokens)],
                        out.at[back_at(y, core, steps), side, core],
                        sems.at[len(copies)],
                    )
                )
    for copy in copies:
        copy.start()
    for copy in copies:
        copy.wait()


def on_device(hidden, grad, mixture, weight, down, up, gate_matrix):
    tokens, width = grad.shape
    adapters = gate_matrix.shape[0]
    stacked = up.shape[0]
    features = weight.shape[0]
    depth = width + stacked
    quarter = features // 4
    x, y, zh, c = (lax.axis_index(a) for a in ("x", "y", "zh", "c"))
    at = jnp.stack([x, y, zh, c]).astype(jnp.int32)

    with jax.named_scope("weight_z"):
        piece = jnp.concatenate(
            [lax.dynamic_slice_in_dim(v, x * quarter, quarter, 0) for v in (weight, down)], axis=1
        )
        far_piece = swap(piece, "zh", 1)
    with jax.named_scope("tokens_y"):
        one = ring(grad, "y")
    with jax.named_scope("tokens_core"):
        own_s = swap(grad, "c", 1)

    keep, give = pl.pallas_call(
        act_kernel,
        in_specs=[SMEM, VMEM, VMEM],
        out_specs=[VMEM, VMEM],
        out_shape=[
            shaped((4, 2, tokens, stacked), F32),
            shaped((4, 2, tokens, stacked), BF16),
        ],
        compiler_params=SMALL,
        cost_estimate=cost(2 * mixture.size * stacked, 4 * mixture.size),
        name="rank_products",
    )(at, mixture.reshape(8, 2, tokens, -1), down)
    with jax.named_scope("act_core"):
        got = swap(give, "c", 1)
    mixed, gates, back = pl.pallas_call(
        token_kernel,
        in_specs=[SMEM] + [VMEM] * 4,
        out_specs=[VMEM, VMEM, VMEM],
        out_shape=[
            shaped((tokens, stacked), BF16),
            shaped((adapters, tokens), F32),
            shaped((tokens, stacked), F32),
        ],
        compiler_params=SMALL,
        cost_estimate=cost(6 * tokens * width * stacked, 12 * tokens * width),
        name="token_values",
    )(at, hidden, grad, up, gate_matrix)
    first, second, third, rest = pl.pallas_call(
        act_y_kernel,
        in_specs=[SMEM, VMEM, VMEM, VMEM],
        out_specs=[VMEM] * 4,
        out_shape=[shaped((3, tokens, stacked), BF16)] * 3 + [shaped((2, tokens, stacked), F32)],
        compiler_params=SMALL,
        name="rank_sum_core",
    )(at, keep, got, mixed)
    with jax.named_scope("act_y"):
        first, second, third = (
            swap(v, "y", mask) for v, mask in ((first, 1), (second, 2), (third, 3))
        )
    keep, give, all_mixed = pl.pallas_call(
        act_z_kernel,
        in_specs=[SMEM] + [VMEM] * 5 + [ANY],
        out_specs=[VMEM] * 3,
        out_shape=[
            shaped((tokens, stacked), F32),
            shaped((tokens, stacked), BF16),
            shaped((4, tokens, stacked), BF16),
        ],
        compiler_params=SMALL,
        name="rank_sum_y",
    )(at, rest, first, second, third, mixed, own_s)
    one, far_piece = fence((one, far_piece), give)
    with jax.named_scope("tokens_y"):
        two = ring(one, "y")
    with jax.named_scope("tokens_core"):
        one_s = swap(one, "c", 1)
    with jax.named_scope("weight_x"):
        w_first = pairs(far_piece, "x", True)
        w_second = pairs(far_piece, "x", False)
    with jax.named_scope("act_z"):
        message = swap(give, "zh", 1)
    with jax.named_scope("mixed_core"):
        mixed_s = swap(all_mixed, "c", 1)

    def products(name, first, near, near_s, more, more_s, weights, downs, tie):
        return pl.pallas_call(
            functools.partial(product_kernel, first),
            in_specs=[SMEM] + [VMEM] * 8 + [ANY],
            out_specs=VMEM,
            out_shape=shaped((2, 2 * tokens, features), BF16),
            compiler_params=MIDDLE,
            cost_estimate=cost(8 * tokens * depth * features, 12 * tokens * depth),
            name=name,
        )(at, near, near_s, more, more_s, all_mixed, mixed_s, weights, downs, tie)

    own_near = products("own_near", 0, grad, own_s, one, one_s, weight, down, give)

    total, give = pl.pallas_call(
        gate_kernel,
        in_specs=[SMEM] + [VMEM] * 5 + [ANY],
        out_specs=[VMEM, VMEM],
        out_shape=[shaped((adapters, width // 2), F32)] * 2,
        compiler_params=SMALL,
        name="gate_products",
    )(at, keep, message, back, gates, hidden, own_near)

    def add(left, right, *ties):
        return pl.pallas_call(
            add_kernel,
            in_specs=[VMEM, VMEM] + [ANY] * len(ties),
            out_specs=[VMEM, VMEM],
            out_shape=[shaped(left.shape, F32), shaped(left.shape, BF16)],
            compiler_params=SMALL,
            name="gate_sum",
        )(left, right, *ties)

    def add4(*parts):
        return pl.pallas_call(
            add4_kernel,
            in_specs=[VMEM] * 4 + [ANY] * (len(parts) - 4),
            out_specs=VMEM,
            out_shape=shaped(parts[0].shape, F32),
            compiler_params=SMALL,
        name="gate_sum",
        )(*parts)

    def step(total, axis, *ties, message=None):
        message = total if message is None else message
        with jax.named_scope("gate_" + axis):
            got = [swap(message, axis, mask) for mask in (1, 2, 3)]
        return add4(total, *got, *ties)

    with jax.named_scope("gate_core"):
        got = swap(give, "c", 1)
    total, message = add(total, got, w_first, w_second)
    (w_first,) = fence((w_first,), total)
    with jax.named_scope("weight_x_far"):
        w_far = pairs(w_first, "x", False)
    (two,) = fence((two,), w_first)
    with jax.named_scope("tokens_y"):
        three = ring(two, "y")
    total = step(total, "zl", mixed_s, w_far, two, message=message)
    with jax.named_scope("tokens_core"):
        two_s = swap(two, "c", 1)

    far, far_weight, far_down = pl.pallas_call(
        far_kernel,
        in_specs=[SMEM] + [VMEM] * 12 + [ANY],
        out_specs=[VMEM] * 3,
        out_shape=[
            shaped((3, 2 * tokens, features), BF16),
            shaped((features, width), BF16),
            shaped((features, stacked), BF16),
        ],
        compiler_params=MIDDLE,
        cost_estimate=cost(12 * tokens * depth * features, 18 * tokens * depth),
        name="far_products",
    )(
        at, grad, own_s, one, one_s, two, two_s, all_mixed, mixed_s,
        far_piece, w_first, w_second, w_far, total,
    )
    with jax.named_scope("out_z"):
        far_got = swap(far, "zh", 1)
    total = step(total, "x", far)
    (three,) = fence((three,), total)
    with jax.named_scope("tokens_core"):
        three_s = swap(three, "c", 1)

    total = step(total, "y")
    last = pl.pallas_call(
        far_last_kernel,
        in_specs=[SMEM] + [VMEM] * 6 + [ANY],
        out_specs=VMEM,
        out_shape=shaped((2 * tokens, features), BF16),
        cost_estimate=cost(4 * tokens * depth * features, 6 * tokens * depth),
        compiler_params=MIDDLE,
        name="far_products_last",
    )(at, three, three_s, all_mixed, mixed_s, far_weight, far_down, total)
    with jax.named_scope("out_z_last"):
        last_got = swap(last, "zh", 1)

    own_rest = products("own_rest", 2, two, two_s, three, three_s, weight, down, far)
    with jax.named_scope("gate_zh"):
        got = swap(total, "zh", 1)
    total, _ = add(total, got, last, far_got)
    with jax.named_scope("gate_core_back"):
        other = swap(total, "c", 1)
    gate_grad = pl.pallas_call(
        halves_kernel,
        in_specs=[SMEM, VMEM, VMEM],
        out_specs=VMEM,
        out_shape=shaped((adapters, width), F32),
        compiler_params=SMALL,
        name="gate_halves",
    )(at, total, other)

    out = pl.pallas_call(
        place_kernel,
        in_specs=[SMEM] + [VMEM] * 4,
        out_specs=HBM,
        out_shape=shaped((4, 2, 2, tokens, features), BF16),
        scratch_shapes=[pltpu.SemaphoreType.DMA((16,))],
        compiler_params=MIDDLE,
        name="place",
    )(at, own_near, own_rest, far_got, last_got)
    return gate_grad, out.reshape(16 * tokens, features)


def solution(mesh):
    grid = Mesh(mesh.devices.reshape(4, 4, 4, 2, 2), AXES)
    dp, tensor = ("x", "zl"), ("y", "zh", "c")
    return jax.shard_map(
        on_device,
        mesh=grid,
        in_specs=(
            P(AXES, None),
            P(AXES, None),
            P(dp, tensor),
            P(tensor, None),
            P(tensor, None),
            P(),
            P(),
        ),
        out_specs=(P(), P(dp, tensor)),
        check_vma=False,
    )
```

```python
import functools

import jax
import jax.numpy as jnp
from jax import lax
from jax.experimental import pallas as pl
from jax.experimental.pallas import tpu as pltpu
from jax.sharding import Mesh
from jax.sharding import PartitionSpec as P

F32 = jnp.float32
BF16 = jnp.bfloat16
AXES = ("x", "zl", "y", "zh", "c")
VMEM = pl.BlockSpec(memory_space=pltpu.VMEM)
SMEM = pl.BlockSpec(memory_space=pltpu.SMEM)
ANY = pl.BlockSpec(memory_space=pl.ANY)
HBM = pl.BlockSpec(memory_space=pltpu.HBM)
SMALL = pltpu.CompilerParams(vmem_limit_bytes=8 * 1024 * 1024)
MIDDLE = pltpu.CompilerParams(vmem_limit_bytes=16 * 1024 * 1024)


def ring(value, axis):
    size = lax.axis_size(axis)
    pairs = [
        (2 * i + c, 2 * ((i + 1 - 2 * c) % size) + c) for i in range(size) for c in range(2)
    ]
    return lax.ppermute(value, (axis, "c"), pairs)


def pairs(value, axis, first):
    size = lax.axis_size(axis)
    partner = lambda i, c: i ^ 1 if (c == 0) == first else size - 1 - i
    return lax.ppermute(
        value, (axis, "c"), [(2 * i + c, 2 * partner(i, c) + c) for i in range(size) for c in range(2)]
    )


def fence_kernel(*refs):
    del refs


def fence(values, *ties):
    return pl.pallas_call(
        fence_kernel,
        in_specs=[ANY] * (len(values) + len(ties)),
        out_specs=[ANY] * len(values),
        out_shape=[shaped(v.shape, v.dtype) for v in values],
        input_output_aliases={i: i for i in range(len(values))},
        compiler_params=SMALL,
        name="fence",
    )(*values, *ties)


def back_at(place, core, steps):
    return lax.rem(place - steps * (1 - 2 * core) + 4, 4)


def swap(value, axis, mask):
    size = lax.axis_size(axis)
    return lax.ppermute(value, axis, [(i, i ^ mask) for i in range(size)])


def dot_t(left, right, precision=None):
    return lax.dot_general(
        left, right, (((1,), (1,)), ((), ())), precision=precision, preferred_element_type=F32
    )


def shaped(shape, dtype):
    return jax.ShapeDtypeStruct(shape, dtype)


def cost(flops, moved):
    return pl.CostEstimate(flops=flops, bytes_accessed=moved, transcendentals=0)


def membership(adapters, stacked):
    row = lax.broadcasted_iota(jnp.int32, (adapters, stacked), 0)
    column = lax.broadcasted_iota(jnp.int32, (adapters, stacked), 1)
    low = row * (stacked // adapters)
    return jnp.where((column >= low) & (column < low + stacked // adapters), 1.0, 0.0)


def piece_kernel(at, weight, down, piece, sems):
    width = weight.shape[1]
    quarter = piece.shape[0]
    rows = pl.ds(pl.multiple_of(at[0] * quarter, quarter), quarter)
    copies = [
        pltpu.make_async_copy(weight.at[rows], piece.at[:, pl.ds(0, width)], sems.at[0]),
        pltpu.make_async_copy(
            down.at[rows], piece.at[:, pl.ds(width, down.shape[1])], sems.at[1]
        ),
    ]
    for copy in copies:
        copy.start()
    for copy in copies:
        copy.wait()


def token_kernel(at, hidden, grad, up, gate, mixed, gates, back):
    stacked = up.shape[0]
    ones = membership(gate.shape[0], stacked)
    wide = lax.dot_general(
        ones.astype(BF16), gate[...], (((0,), (0,)), ((), ())), preferred_element_type=F32
    ).astype(BF16)
    gates[...] = jax.nn.sigmoid(dot_t(gate[...], hidden[...]))
    factor = 2.0 * jax.nn.sigmoid(dot_t(hidden[...], wide))
    pulled = dot_t(grad[...], up[...])
    back[...] = pulled
    mixed[...] = (factor * pulled).astype(BF16)


def act_kernel(at, mixture, down, keep, give):
    c = at[3]
    blocks, _, tokens, depth = mixture.shape
    for out, side in ((give, 1 - c), (keep, c)):
        rows = mixture[:, side].reshape(blocks * tokens, depth)
        value = jnp.dot(rows, down[...], preferred_element_type=F32)
        out[...] = value.reshape(out.shape).astype(out.dtype)


def act_y_kernel(at, keep, got, mixed, first, second, third, rest):
    y = at[1]
    for out, mask in ((first, 1), (second, 2), (third, 3)):
        row = jnp.bitwise_xor(y, mask)
        out[pl.ds(0, 2)] = (keep[row] + got[row].astype(F32)).astype(out.dtype)
        out[2] = mixed[...]
    rest[...] = keep[y] + got[y].astype(F32)


def act_z_kernel(at, rest, first, second, third, mixed, tie, keep, give, all_mixed):
    y, zh = at[1], at[2]
    for out, side in ((give, 1 - zh), (keep, zh)):
        total = (rest[side] + first[side].astype(F32)) + (
            second[side].astype(F32) + third[side].astype(F32)
        )
        out[...] = total.astype(out.dtype)
    all_mixed[y] = mixed[...]
    for ref, mask in ((first, 1), (second, 2), (third, 3)):
        all_mixed[jnp.bitwise_xor(y, mask)] = ref[2]


def gate_kernel(at, keep, got, back, gates, hidden, tie, result, give):
    stacked = keep.shape[1]
    adapters = gates.shape[0]
    half = result.shape[1]
    product = (keep[...] + got[...].astype(F32)) * back[...]
    ones = membership(adapters, stacked)
    delta = 2.0 * dot_t(ones, product, lax.Precision.HIGHEST)
    dlogit = delta * gates[...] * (1.0 - gates[...])
    top = dlogit.astype(BF16).astype(F32)
    middle = (dlogit - top).astype(BF16).astype(F32)
    parts = jnp.concatenate([top, middle, dlogit - top - middle], axis=0).astype(BF16)
    c = at[3]
    for out, side in ((result, c), (give, 1 - c)):
        columns = pl.ds(pl.multiple_of(side * half, 128), half)
        total = jnp.dot(parts, hidden[:, columns], preferred_element_type=F32)
        out[...] = total[:adapters] + (
            total[adapters : 2 * adapters] + total[2 * adapters :]
        )


def add_kernel(left, right, *refs):
    total = left[...] + right[...]
    refs[-2][...] = total
    refs[-1][...] = total.astype(refs[-1].dtype)


def halves_kernel(at, mine, other, out):
    half = mine.shape[1]
    c = at[3]
    for side, ref in ((c, mine), (1 - c, other)):
        out[:, pl.ds(pl.multiple_of(side * half, 128), half)] = ref[...]


def add4_kernel(first, second, third, fourth, *refs):
    own = first[...].astype(second.dtype).astype(F32)
    refs[-1][...] = (own + second[...].astype(F32)) + (
        third[...].astype(F32) + fourth[...].astype(F32)
    )


def rows_product(at, steps, refs, mixed, weights, downs, out):
    y, c = at[1], at[3]
    both = jnp.concatenate([ref[...] for ref in refs], axis=0)
    ranks = jnp.concatenate(
        [mixed[0][back_at(y, c, steps)], mixed[1][back_at(y, 1 - c, steps)]], axis=0
    )
    value = dot_t(both, weights[...]) + dot_t(ranks, downs[...])
    out[...] = value.astype(out.dtype)


def far_kernel(at, own, own_s, one, one_s, two, two_s, mixed, mixed_s, *refs):
    pieces, (tie, out, weight, down) = refs[:4], refs[4:]
    width = weight.shape[1]
    rows = pieces[0].shape[0]
    x, c = at[0], at[3]
    up, turned = jnp.bitwise_xor(x, 1), 3 - x
    first, second = jnp.where(c == 0, up, turned), jnp.where(c == 0, turned, up)
    for place, ref in zip((x, first, second, jnp.bitwise_xor(x, 2)), pieces):
        place = pl.ds(pl.multiple_of(place * rows, rows), rows)
        weight[place, :] = ref[:, :width]
        down[place, :] = ref[:, width:]
    for steps, group in enumerate(((own, own_s), (one, one_s), (two, two_s))):
        rows_product(at, steps, group, (mixed, mixed_s), weight, down, out.at[steps])


def far_last_kernel(at, three, three_s, mixed, mixed_s, weight, down, tie, out):
    rows_product(at, 3, (three, three_s), (mixed, mixed_s), weight, down, out)


def product_kernel(first, at, near, near_s, more, more_s, mixed, mixed_s, weight, down, tie, out):
    for number, group in enumerate(((near, near_s), (more, more_s))):
        rows_product(at, first + number, group, (mixed, mixed_s), weight, down, out.at[number])


def place_kernel(at, near, rest, got, last, out, sems):
    y, zh, c = at[1], at[2], at[3]
    tokens = out.shape[3]
    copies = []
    for steps in range(4):
        own = near.at[steps] if steps < 2 else rest.at[steps - 2]
        other = got.at[steps] if steps < 3 else last
        for ref, side in ((own, zh), (other, 1 - zh)):
            for half, core in ((0, c), (1, 1 - c)):
                copies.append(
                    pltpu.make_async_copy(
                        ref.at[pl.ds(half * tokens, tokens)],
                        out.at[back_at(y, core, steps), side, core],
                        sems.at[len(copies)],
                    )
                )
    for copy in copies:
        copy.start()
    for copy in copies:
        copy.wait()


def on_device(hidden, grad, mixture, weight, down, up, gate_matrix):
    tokens, width = grad.shape
    adapters = gate_matrix.shape[0]
    stacked = up.shape[0]
    features = weight.shape[0]
    depth = width + stacked
    quarter = features // 4
    x, y, zh, c = (lax.axis_index(a) for a in ("x", "y", "zh", "c"))
    at = jnp.stack([x, y, zh, c]).astype(jnp.int32)

    with jax.named_scope("weight_z"):
        piece = pl.pallas_call(
            piece_kernel,
            in_specs=[SMEM, ANY, ANY],
            out_specs=VMEM,
            out_shape=shaped((quarter, depth), BF16),
            scratch_shapes=[pltpu.SemaphoreType.DMA((2,))],
            compiler_params=pltpu.CompilerParams(vmem_limit_bytes=56 * 1024 * 1024),
            name="weight_piece",
        )(at, weight, down)
        far_piece = swap(piece, "zh", 1)
    with jax.named_scope("tokens_y"):
        one = ring(grad, "y")
    with jax.named_scope("tokens_core"):
        own_s = swap(grad, "c", 1)

    keep, give = pl.pallas_call(
        act_kernel,
        in_specs=[SMEM, VMEM, VMEM],
        out_specs=[VMEM, VMEM],
        out_shape=[
            shaped((4, 2, tokens, stacked), F32),
            shaped((4, 2, tokens, stacked), BF16),
        ],
        compiler_params=SMALL,
        cost_estimate=cost(2 * mixture.size * stacked, 4 * mixture.size),
        name="rank_products",
    )(at, mixture.reshape(8, 2, tokens, -1), down)
    with jax.named_scope("act_core"):
        got = swap(give, "c", 1)
    mixed, gates, back = pl.pallas_call(
        token_kernel,
        in_specs=[SMEM] + [VMEM] * 4,
        out_specs=[VMEM, VMEM, VMEM],
        out_shape=[
            shaped((tokens, stacked), BF16),
            shaped((adapters, tokens), F32),
            shaped((tokens, stacked), F32),
        ],
        compiler_params=SMALL,
        cost_estimate=cost(6 * tokens * width * stacked, 12 * tokens * width),
        name="token_values",
    )(at, hidden, grad, up, gate_matrix)
    first, second, third, rest = pl.pallas_call(
        act_y_kernel,
        in_specs=[SMEM, VMEM, VMEM, VMEM],
        out_specs=[VMEM] * 4,
        out_shape=[shaped((3, tokens, stacked), BF16)] * 3 + [shaped((2, tokens, stacked), F32)],
        compiler_params=SMALL,
        name="rank_sum_core",
    )(at, keep, got, mixed)
    with jax.named_scope("act_y"):
        first, second, third = (
            swap(v, "y", mask) for v, mask in ((first, 1), (second, 2), (third, 3))
        )
    keep, give, all_mixed = pl.pallas_call(
        act_z_kernel,
        in_specs=[SMEM] + [VMEM] * 5 + [ANY],
        out_specs=[VMEM] * 3,
        out_shape=[
            shaped((tokens, stacked), F32),
            shaped((tokens, stacked), BF16),
            shaped((4, tokens, stacked), BF16),
        ],
        compiler_params=SMALL,
        name="rank_sum_y",
    )(at, rest, first, second, third, mixed, own_s)
    one, far_piece = fence((one, far_piece), give)
    with jax.named_scope("tokens_y"):
        two = ring(one, "y")
    with jax.named_scope("tokens_core"):
        one_s = swap(one, "c", 1)
    with jax.named_scope("weight_x"):
        w_first = pairs(far_piece, "x", True)
        w_second = pairs(far_piece, "x", False)
    with jax.named_scope("act_z"):
        message = swap(give, "zh", 1)
    with jax.named_scope("mixed_core"):
        mixed_s = swap(all_mixed, "c", 1)

    def products(name, first, near, near_s, more, more_s, weights, downs, tie):
        return pl.pallas_call(
            functools.partial(product_kernel, first),
            in_specs=[SMEM] + [VMEM] * 8 + [ANY],
            out_specs=VMEM,
            out_shape=shaped((2, 2 * tokens, features), BF16),
            compiler_params=MIDDLE,
            cost_estimate=cost(8 * tokens * depth * features, 12 * tokens * depth),
            name=name,
        )(at, near, near_s, more, more_s, all_mixed, mixed_s, weights, downs, tie)

    own_near = products("own_near", 0, grad, own_s, one, one_s, weight, down, give)

    total, give = pl.pallas_call(
        gate_kernel,
        in_specs=[SMEM] + [VMEM] * 5 + [ANY],
        out_specs=[VMEM, VMEM],
        out_shape=[shaped((adapters, width // 2), F32)] * 2,
        compiler_params=SMALL,
        name="gate_products",
    )(at, keep, message, back, gates, hidden, own_near)

    def add(left, right, *ties):
        return pl.pallas_call(
            add_kernel,
            in_specs=[VMEM, VMEM] + [ANY] * len(ties),
            out_specs=[VMEM, VMEM],
            out_shape=[shaped(left.shape, F32), shaped(left.shape, BF16)],
            compiler_params=SMALL,
            name="gate_sum",
        )(left, right, *ties)

    def add4(*parts):
        return pl.pallas_call(
            add4_kernel,
            in_specs=[VMEM] * 4 + [ANY] * (len(parts) - 4),
            out_specs=VMEM,
            out_shape=shaped(parts[0].shape, F32),
            compiler_params=SMALL,
        name="gate_sum",
        )(*parts)

    def step(total, axis, *ties, message=None):
        message = total if message is None else message
        with jax.named_scope("gate_" + axis):
            got = [swap(message, axis, mask) for mask in (1, 2, 3)]
        return add4(total, *got, *ties)

    with jax.named_scope("gate_core"):
        got = swap(give, "c", 1)
    total, message = add(total, got, w_first, w_second)
    (w_first,) = fence((w_first,), total)
    with jax.named_scope("weight_x_far"):
        w_far = pairs(w_first, "x", False)
    (two,) = fence((two,), w_first)
    with jax.named_scope("tokens_y"):
        three = ring(two, "y")
    total = step(total, "zl", mixed_s, w_far, two, message=message)
    with jax.named_scope("tokens_core"):
        two_s = swap(two, "c", 1)

    far, far_weight, far_down = pl.pallas_call(
        far_kernel,
        in_specs=[SMEM] + [VMEM] * 12 + [ANY],
        out_specs=[VMEM] * 3,
        out_shape=[
            shaped((3, 2 * tokens, features), BF16),
            shaped((features, width), BF16),
            shaped((features, stacked), BF16),
        ],
        compiler_params=MIDDLE,
        cost_estimate=cost(12 * tokens * depth * features, 18 * tokens * depth),
        name="far_products",
    )(
        at, grad, own_s, one, one_s, two, two_s, all_mixed, mixed_s,
        far_piece, w_first, w_second, w_far, total,
    )
    with jax.named_scope("out_z"):
        far_got = swap(far, "zh", 1)
    total = step(total, "x", far)
    (three,) = fence((three,), total)
    with jax.named_scope("tokens_core"):
        three_s = swap(three, "c", 1)

    total = step(total, "y")
    last = pl.pallas_call(
        far_last_kernel,
        in_specs=[SMEM] + [VMEM] * 6 + [ANY],
        out_specs=VMEM,
        out_shape=shaped((2 * tokens, features), BF16),
        cost_estimate=cost(4 * tokens * depth * features, 6 * tokens * depth),
        compiler_params=MIDDLE,
        name="far_products_last",
    )(at, three, three_s, all_mixed, mixed_s, far_weight, far_down, total)
    with jax.named_scope("out_z_last"):
        last_got = swap(last, "zh", 1)

    own_rest = products("own_rest", 2, two, two_s, three, three_s, weight, down, far)
    with jax.named_scope("gate_zh"):
        got = swap(total, "zh", 1)
    total, _ = add(total, got, last, far_got, own_rest)
    with jax.named_scope("gate_core_back"):
        other = swap(total, "c", 1)
    gate_grad = pl.pallas_call(
        halves_kernel,
        in_specs=[SMEM, VMEM, VMEM],
        out_specs=VMEM,
        out_shape=shaped((adapters, width), F32),
        compiler_params=SMALL,
        name="gate_halves",
    )(at, total, other)

    out = pl.pallas_call(
        place_kernel,
        in_specs=[SMEM] + [VMEM] * 4,
        out_specs=HBM,
        out_shape=shaped((4, 2, 2, tokens, features), BF16),
        scratch_shapes=[pltpu.SemaphoreType.DMA((16,))],
        compiler_params=MIDDLE,
        name="place",
    )(at, own_near, own_rest, far_got, last_got)
    return gate_grad, out.reshape(16 * tokens, features)


def solution(mesh):
    grid = Mesh(mesh.devices.reshape(4, 4, 4, 2, 2), AXES)
    dp, tensor = ("x", "zl"), ("y", "zh", "c")
    return jax.shard_map(
        on_device,
        mesh=grid,
        in_specs=(
            P(AXES, None),
            P(AXES, None),
            P(dp, tensor),
            P(tensor, None),
            P(tensor, None),
            P(),
            P(),
        ),
        out_specs=(P(), P(dp, tensor)),
        check_vma=False,
    )
```

```python
import functools

import jax
import jax.numpy as jnp
from jax import lax
from jax.experimental import pallas as pl
from jax.experimental.pallas import tpu as pltpu
from jax.sharding import Mesh
from jax.sharding import PartitionSpec as P

F32 = jnp.float32
BF16 = jnp.bfloat16
AXES = ("x", "zl", "y", "zh", "c")
VMEM = pl.BlockSpec(memory_space=pltpu.VMEM)
SMEM = pl.BlockSpec(memory_space=pltpu.SMEM)
ANY = pl.BlockSpec(memory_space=pl.ANY)
HBM = pl.BlockSpec(memory_space=pltpu.HBM)
SMALL = pltpu.CompilerParams(vmem_limit_bytes=8 * 1024 * 1024)
MIDDLE = pltpu.CompilerParams(vmem_limit_bytes=16 * 1024 * 1024)


def ring(value, axis):
    size = lax.axis_size(axis)
    pairs = [
        (2 * i + c, 2 * ((i + 1 - 2 * c) % size) + c) for i in range(size) for c in range(2)
    ]
    return lax.ppermute(value, (axis, "c"), pairs)


def pairs(value, axis, first):
    size = lax.axis_size(axis)
    partner = lambda i, c: i ^ 1 if (c == 0) == first else size - 1 - i
    return lax.ppermute(
        value, (axis, "c"), [(2 * i + c, 2 * partner(i, c) + c) for i in range(size) for c in range(2)]
    )


def fence_kernel(*refs):
    del refs


def fence(values, *ties):
    return pl.pallas_call(
        fence_kernel,
        in_specs=[ANY] * (len(values) + len(ties)),
        out_specs=[ANY] * len(values),
        out_shape=[shaped(v.shape, v.dtype) for v in values],
        input_output_aliases={i: i for i in range(len(values))},
        compiler_params=SMALL,
        name="fence",
    )(*values, *ties)


def back_at(place, core, steps):
    return lax.rem(place - steps * (1 - 2 * core) + 4, 4)


def swap(value, axis, mask):
    size = lax.axis_size(axis)
    return lax.ppermute(value, axis, [(i, i ^ mask) for i in range(size)])


def dot_t(left, right, precision=None):
    return lax.dot_general(
        left, right, (((1,), (1,)), ((), ())), precision=precision, preferred_element_type=F32
    )


def shaped(shape, dtype):
    return jax.ShapeDtypeStruct(shape, dtype)


def cost(flops, moved):
    return pl.CostEstimate(flops=flops, bytes_accessed=moved, transcendentals=0)


def membership(adapters, stacked):
    row = lax.broadcasted_iota(jnp.int32, (adapters, stacked), 0)
    column = lax.broadcasted_iota(jnp.int32, (adapters, stacked), 1)
    low = row * (stacked // adapters)
    return jnp.where((column >= low) & (column < low + stacked // adapters), 1.0, 0.0)


def token_kernel(at, hidden, grad, up, gate, mixed, gates, back):
    stacked = up.shape[0]
    ones = membership(gate.shape[0], stacked)
    wide = lax.dot_general(
        ones.astype(BF16), gate[...], (((0,), (0,)), ((), ())), preferred_element_type=F32
    ).astype(BF16)
    gates[...] = jax.nn.sigmoid(dot_t(gate[...], hidden[...]))
    factor = 2.0 * jax.nn.sigmoid(dot_t(hidden[...], wide))
    pulled = dot_t(grad[...], up[...])
    back[...] = pulled
    mixed[...] = (factor * pulled).astype(BF16)


def act_kernel(at, mixture, down, keep, give):
    c = at[3]
    blocks, _, tokens, depth = mixture.shape
    for out, side in ((give, 1 - c), (keep, c)):
        rows = mixture[:, side].reshape(blocks * tokens, depth)
        value = jnp.dot(rows, down[...], preferred_element_type=F32)
        out[...] = value.reshape(out.shape).astype(out.dtype)


def act_y_kernel(at, keep, got, mixed, first, second, third, rest):
    y = at[1]
    for out, mask in ((first, 1), (second, 2), (third, 3)):
        row = jnp.bitwise_xor(y, mask)
        out[pl.ds(0, 2)] = (keep[row] + got[row].astype(F32)).astype(out.dtype)
        out[2] = mixed[...]
    rest[...] = keep[y] + got[y].astype(F32)


def act_z_kernel(at, rest, first, second, third, mixed, tie, keep, give, all_mixed):
    y, zh = at[1], at[2]
    for out, side in ((give, 1 - zh), (keep, zh)):
        total = (rest[side] + first[side].astype(F32)) + (
            second[side].astype(F32) + third[side].astype(F32)
        )
        out[...] = total.astype(out.dtype)
    all_mixed[y] = mixed[...]
    for ref, mask in ((first, 1), (second, 2), (third, 3)):
        all_mixed[jnp.bitwise_xor(y, mask)] = ref[2]


def gate_kernel(at, keep, got, back, gates, hidden, tie, result, give):
    stacked = keep.shape[1]
    adapters = gates.shape[0]
    half = result.shape[1]
    product = (keep[...] + got[...].astype(F32)) * back[...]
    ones = membership(adapters, stacked)
    delta = 2.0 * dot_t(ones, product, lax.Precision.HIGHEST)
    dlogit = delta * gates[...] * (1.0 - gates[...])
    top = dlogit.astype(BF16).astype(F32)
    middle = (dlogit - top).astype(BF16).astype(F32)
    parts = jnp.concatenate([top, middle, dlogit - top - middle], axis=0).astype(BF16)
    c = at[3]
    for out, side in ((result, c), (give, 1 - c)):
        columns = pl.ds(pl.multiple_of(side * half, 128), half)
        total = jnp.dot(parts, hidden[:, columns], preferred_element_type=F32)
        out[...] = total[:adapters] + (
            total[adapters : 2 * adapters] + total[2 * adapters :]
        )


def add_kernel(left, right, *refs):
    total = left[...] + right[...]
    refs[-2][...] = total
    refs[-1][...] = total.astype(refs[-1].dtype)


def halves_kernel(at, mine, other, out):
    half = mine.shape[1]
    c = at[3]
    for side, ref in ((c, mine), (1 - c, other)):
        out[:, pl.ds(pl.multiple_of(side * half, 128), half)] = ref[...]


def add4_kernel(first, second, third, fourth, *refs):
    own = first[...].astype(second.dtype).astype(F32)
    refs[-1][...] = (own + second[...].astype(F32)) + (
        third[...].astype(F32) + fourth[...].astype(F32)
    )


def rows_product(at, steps, refs, mixed, weights, downs, out):
    y, c = at[1], at[3]
    both = jnp.concatenate([ref[...] for ref in refs], axis=0)
    ranks = jnp.concatenate(
        [mixed[0][back_at(y, c, steps)], mixed[1][back_at(y, 1 - c, steps)]], axis=0
    )
    value = dot_t(both, weights[...]) + dot_t(ranks, downs[...])
    out[...] = value.astype(out.dtype)


def far_kernel(at, own, own_s, one, one_s, two, two_s, mixed, mixed_s, *refs):
    pieces, (tie, out, weight, down) = refs[:4], refs[4:]
    width = weight.shape[1]
    rows = pieces[0].shape[0]
    x, c = at[0], at[3]
    up, turned = jnp.bitwise_xor(x, 1), 3 - x
    first, second = jnp.where(c == 0, up, turned), jnp.where(c == 0, turned, up)
    for place, ref in zip((x, first, second, jnp.bitwise_xor(x, 2)), pieces):
        place = pl.ds(pl.multiple_of(place * rows, rows), rows)
        weight[place, :] = ref[:, :width]
        down[place, :] = ref[:, width:]
    for steps, group in enumerate(((own, own_s), (one, one_s), (two, two_s))):
        rows_product(at, steps, group, (mixed, mixed_s), weight, down, out.at[steps])


def far_last_kernel(at, three, three_s, mixed, mixed_s, weight, down, tie, out):
    rows_product(at, 3, (three, three_s), (mixed, mixed_s), weight, down, out)


def product_kernel(first, at, near, near_s, more, more_s, mixed, mixed_s, weight, down, tie, out):
    for number, group in enumerate(((near, near_s), (more, more_s))):
        rows_product(at, first + number, group, (mixed, mixed_s), weight, down, out.at[number])


def place_kernel(at, near, rest, got, last, out, sems):
    y, zh, c = at[1], at[2], at[3]
    tokens = out.shape[3]
    copies = []
    for steps in range(4):
        own = near.at[steps] if steps < 2 else rest.at[steps - 2]
        other = got.at[steps] if steps < 3 else last
        for ref, side in ((own, zh), (other, 1 - zh)):
            for half, core in ((0, c), (1, 1 - c)):
                copies.append(
                    pltpu.make_async_copy(
                        ref.at[pl.ds(half * tokens, tokens)],
                        out.at[back_at(y, core, steps), side, core],
                        sems.at[len(copies)],
                    )
                )
    for copy in copies:
        copy.start()
    for copy in copies:
        copy.wait()


def on_device(hidden, grad, mixture, weight, down, up, gate_matrix):
    tokens, width = grad.shape
    adapters = gate_matrix.shape[0]
    stacked = up.shape[0]
    features = weight.shape[0]
    depth = width + stacked
    quarter = features // 4
    x, y, zh, c = (lax.axis_index(a) for a in ("x", "y", "zh", "c"))
    at = jnp.stack([x, y, zh, c]).astype(jnp.int32)

    with jax.named_scope("weight_z"):
        piece = jnp.concatenate(
            [lax.dynamic_slice_in_dim(v, x * quarter, quarter, 0) for v in (weight, down)], axis=1
        )
        far_piece = swap(piece, "zh", 1)
    with jax.named_scope("tokens_y"):
        one = ring(grad, "y")
    with jax.named_scope("tokens_core"):
        own_s = swap(grad, "c", 1)

    keep, give = pl.pallas_call(
        act_kernel,
        in_specs=[SMEM, VMEM, VMEM],
        out_specs=[VMEM, VMEM],
        out_shape=[
            shaped((4, 2, tokens, stacked), F32),
            shaped((4, 2, tokens, stacked), BF16),
        ],
        compiler_params=SMALL,
        cost_estimate=cost(2 * mixture.size * stacked, 4 * mixture.size),
        name="rank_products",
    )(at, mixture.reshape(8, 2, tokens, -1), down)
    with jax.named_scope("act_core"):
        got = swap(give, "c", 1)
    mixed, gates, back = pl.pallas_call(
        token_kernel,
        in_specs=[SMEM] + [VMEM] * 4,
        out_specs=[VMEM, VMEM, VMEM],
        out_shape=[
            shaped((tokens, stacked), BF16),
            shaped((adapters, tokens), F32),
            shaped((tokens, stacked), F32),
        ],
        compiler_params=SMALL,
        cost_estimate=cost(6 * tokens * width * stacked, 12 * tokens * width),
        name="token_values",
    )(at, hidden, grad, up, gate_matrix)
    first, second, third, rest = pl.pallas_call(
        act_y_kernel,
        in_specs=[SMEM, VMEM, VMEM, VMEM],
        out_specs=[VMEM] * 4,
        out_shape=[shaped((3, tokens, stacked), BF16)] * 3 + [shaped((2, tokens, stacked), F32)],
        compiler_params=SMALL,
        name="rank_sum_core",
    )(at, keep, got, mixed)
    with jax.named_scope("act_y"):
        first, second, third = (
            swap(v, "y", mask) for v, mask in ((first, 1), (second, 2), (third, 3))
        )
    keep, give, all_mixed = pl.pallas_call(
        act_z_kernel,
        in_specs=[SMEM] + [VMEM] * 5 + [ANY],
        out_specs=[VMEM] * 3,
        out_shape=[
            shaped((tokens, stacked), F32),
            shaped((tokens, stacked), BF16),
            shaped((4, tokens, stacked), BF16),
        ],
        compiler_params=SMALL,
        name="rank_sum_y",
    )(at, rest, first, second, third, mixed, own_s)
    one, far_piece = fence((one, far_piece), give)
    with jax.named_scope("tokens_y"):
        two = ring(one, "y")
    with jax.named_scope("tokens_core"):
        one_s = swap(one, "c", 1)
    with jax.named_scope("weight_x"):
        w_first = pairs(far_piece, "x", True)
        w_second = pairs(far_piece, "x", False)
    with jax.named_scope("act_z"):
        message = swap(give, "zh", 1)
    with jax.named_scope("mixed_core"):
        mixed_s = swap(all_mixed, "c", 1)

    def products(name, first, near, near_s, more, more_s, weights, downs, tie):
        return pl.pallas_call(
            functools.partial(product_kernel, first),
            in_specs=[SMEM] + [VMEM] * 8 + [ANY],
            out_specs=VMEM,
            out_shape=shaped((2, 2 * tokens, features), BF16),
            compiler_params=MIDDLE,
            cost_estimate=cost(8 * tokens * depth * features, 12 * tokens * depth),
            name=name,
        )(at, near, near_s, more, more_s, all_mixed, mixed_s, weights, downs, tie)

    own_near = products("own_near", 0, grad, own_s, one, one_s, weight, down, give)

    total, give = pl.pallas_call(
        gate_kernel,
        in_specs=[SMEM] + [VMEM] * 5 + [ANY],
        out_specs=[VMEM, VMEM],
        out_shape=[shaped((adapters, width // 2), F32)] * 2,
        compiler_params=SMALL,
        name="gate_products",
    )(at, keep, message, back, gates, hidden, own_near)

    def add(left, right, *ties):
        return pl.pallas_call(
            add_kernel,
            in_specs=[VMEM, VMEM] + [ANY] * len(ties),
            out_specs=[VMEM, VMEM],
            out_shape=[shaped(left.shape, F32), shaped(left.shape, BF16)],
            compiler_params=SMALL,
            name="gate_sum",
        )(left, right, *ties)

    def add4(*parts):
        return pl.pallas_call(
            add4_kernel,
            in_specs=[VMEM] * 4 + [ANY] * (len(parts) - 4),
            out_specs=VMEM,
            out_shape=shaped(parts[0].shape, F32),
            compiler_params=SMALL,
        name="gate_sum",
        )(*parts)

    def step(total, axis, *ties, message=None):
        message = total if message is None else message
        with jax.named_scope("gate_" + axis):
            got = [swap(message, axis, mask) for mask in (1, 2, 3)]
        return add4(total, *got, *ties)

    with jax.named_scope("gate_core"):
        got = swap(give, "c", 1)
    total, message = add(total, got, w_first, w_second)
    (w_first,) = fence((w_first,), total)
    with jax.named_scope("weight_x_far"):
        w_far = pairs(w_first, "x", False)
    (two,) = fence((two,), w_first)
    with jax.named_scope("tokens_y"):
        three = ring(two, "y")
    total = step(total, "zl", mixed_s, w_far, two, message=message)
    with jax.named_scope("tokens_core"):
        two_s = swap(two, "c", 1)

    far, far_weight, far_down = pl.pallas_call(
        far_kernel,
        in_specs=[SMEM] + [VMEM] * 12 + [ANY],
        out_specs=[VMEM] * 3,
        out_shape=[
            shaped((3, 2 * tokens, features), BF16),
            shaped((features, width), BF16),
            shaped((features, stacked), BF16),
        ],
        compiler_params=MIDDLE,
        cost_estimate=cost(12 * tokens * depth * features, 18 * tokens * depth),
        name="far_products",
    )(
        at, grad, own_s, one, one_s, two, two_s, all_mixed, mixed_s,
        far_piece, w_first, w_second, w_far, total,
    )
    with jax.named_scope("out_z"):
        far_got = swap(far, "zh", 1)
    (three,) = fence((three,), far)
    with jax.named_scope("tokens_core"):
        three_s = swap(three, "c", 1)
    total = step(total, "x", far)

    total = step(total, "y")
    last = pl.pallas_call(
        far_last_kernel,
        in_specs=[SMEM] + [VMEM] * 6 + [ANY],
        out_specs=VMEM,
        out_shape=shaped((2 * tokens, features), BF16),
        cost_estimate=cost(4 * tokens * depth * features, 6 * tokens * depth),
        compiler_params=MIDDLE,
        name="far_products_last",
    )(at, three, three_s, all_mixed, mixed_s, far_weight, far_down, total)
    with jax.named_scope("out_z_last"):
        last_got = swap(last, "zh", 1)

    own_rest = products("own_rest", 2, two, two_s, three, three_s, weight, down, far)
    with jax.named_scope("gate_zh"):
        got = swap(total, "zh", 1)
    total, _ = add(total, got, last, far_got, own_rest)
    with jax.named_scope("gate_core_back"):
        other = swap(total, "c", 1)
    gate_grad = pl.pallas_call(
        halves_kernel,
        in_specs=[SMEM, VMEM, VMEM],
        out_specs=VMEM,
        out_shape=shaped((adapters, width), F32),
        compiler_params=SMALL,
        name="gate_halves",
    )(at, total, other)

    out = pl.pallas_call(
        place_kernel,
        in_specs=[SMEM] + [VMEM] * 4,
        out_specs=HBM,
        out_shape=shaped((4, 2, 2, tokens, features), BF16),
        scratch_shapes=[pltpu.SemaphoreType.DMA((16,))],
        compiler_params=MIDDLE,
        name="place",
    )(at, own_near, own_rest, far_got, last_got)
    return gate_grad, out.reshape(16 * tokens, features)


def solution(mesh):
    grid = Mesh(mesh.devices.reshape(4, 4, 4, 2, 2), AXES)
    dp, tensor = ("x", "zl"), ("y", "zh", "c")
    return jax.shard_map(
        on_device,
        mesh=grid,
        in_specs=(
            P(AXES, None),
            P(AXES, None),
            P(dp, tensor),
            P(tensor, None),
            P(tensor, None),
            P(),
            P(),
        ),
        out_specs=(P(), P(dp, tensor)),
        check_vma=False,
    )
```

```python
import functools

import jax
import jax.numpy as jnp
from jax import lax
from jax.experimental import pallas as pl
from jax.experimental.pallas import tpu as pltpu
from jax.sharding import Mesh
from jax.sharding import PartitionSpec as P

F32 = jnp.float32
BF16 = jnp.bfloat16
AXES = ("x", "zl", "y", "zh", "c")
VMEM = pl.BlockSpec(memory_space=pltpu.VMEM)
SMEM = pl.BlockSpec(memory_space=pltpu.SMEM)
ANY = pl.BlockSpec(memory_space=pl.ANY)
HBM = pl.BlockSpec(memory_space=pltpu.HBM)
SMALL = pltpu.CompilerParams(vmem_limit_bytes=8 * 1024 * 1024)
MIDDLE = pltpu.CompilerParams(vmem_limit_bytes=16 * 1024 * 1024)


def ring(value, axis):
    size = lax.axis_size(axis)
    pairs = [
        (2 * i + c, 2 * ((i + 1 - 2 * c) % size) + c) for i in range(size) for c in range(2)
    ]
    return lax.ppermute(value, (axis, "c"), pairs)


def pairs(value, axis, first):
    size = lax.axis_size(axis)
    partner = lambda i, c: i ^ 1 if (c == 0) == first else size - 1 - i
    return lax.ppermute(
        value, (axis, "c"), [(2 * i + c, 2 * partner(i, c) + c) for i in range(size) for c in range(2)]
    )


def fence_kernel(*refs):
    del refs


def fence(values, *ties):
    return pl.pallas_call(
        fence_kernel,
        in_specs=[ANY] * (len(values) + len(ties)),
        out_specs=[ANY] * len(values),
        out_shape=[shaped(v.shape, v.dtype) for v in values],
        input_output_aliases={i: i for i in range(len(values))},
        compiler_params=SMALL,
        name="fence",
    )(*values, *ties)


def back_at(place, core, steps):
    return lax.rem(place - steps * (1 - 2 * core) + 4, 4)


def swap(value, axis, mask):
    size = lax.axis_size(axis)
    return lax.ppermute(value, axis, [(i, i ^ mask) for i in range(size)])


def dot_t(left, right, precision=None):
    return lax.dot_general(
        left, right, (((1,), (1,)), ((), ())), precision=precision, preferred_element_type=F32
    )


def shaped(shape, dtype):
    return jax.ShapeDtypeStruct(shape, dtype)


def cost(flops, moved):
    return pl.CostEstimate(flops=flops, bytes_accessed=moved, transcendentals=0)


def membership(adapters, stacked):
    row = lax.broadcasted_iota(jnp.int32, (adapters, stacked), 0)
    column = lax.broadcasted_iota(jnp.int32, (adapters, stacked), 1)
    low = row * (stacked // adapters)
    return jnp.where((column >= low) & (column < low + stacked // adapters), 1.0, 0.0)


def token_kernel(at, hidden, grad, up, gate, mixed, gates, back):
    stacked = up.shape[0]
    ones = membership(gate.shape[0], stacked)
    wide = lax.dot_general(
        ones.astype(BF16), gate[...], (((0,), (0,)), ((), ())), preferred_element_type=F32
    ).astype(BF16)
    gates[...] = jax.nn.sigmoid(dot_t(gate[...], hidden[...]))
    factor = 2.0 * jax.nn.sigmoid(dot_t(hidden[...], wide))
    pulled = dot_t(grad[...], up[...])
    back[...] = pulled
    mixed[...] = (factor * pulled).astype(BF16)


def act_kernel(at, mixture, down, keep, give):
    c = at[3]
    blocks, _, tokens, depth = mixture.shape
    for out, side in ((give, 1 - c), (keep, c)):
        rows = mixture[:, side].reshape(blocks * tokens, depth)
        value = jnp.dot(rows, down[...], preferred_element_type=F32)
        out[...] = value.reshape(out.shape).astype(out.dtype)


def act_y_kernel(at, keep, got, mixed, first, second, third, rest):
    y = at[1]
    for out, mask in ((first, 1), (second, 2), (third, 3)):
        row = jnp.bitwise_xor(y, mask)
        out[pl.ds(0, 2)] = (keep[row] + got[row].astype(F32)).astype(out.dtype)
        out[2] = mixed[...]
    rest[...] = keep[y] + got[y].astype(F32)


def act_z_kernel(at, rest, first, second, third, mixed, tie, keep, give, all_mixed):
    y, zh = at[1], at[2]
    for out, side in ((give, 1 - zh), (keep, zh)):
        total = (rest[side] + first[side].astype(F32)) + (
            second[side].astype(F32) + third[side].astype(F32)
        )
        out[...] = total.astype(out.dtype)
    all_mixed[y] = mixed[...]
    for ref, mask in ((first, 1), (second, 2), (third, 3)):
        all_mixed[jnp.bitwise_xor(y, mask)] = ref[2]


def gate_kernel(at, keep, got, back, gates, hidden, tie, result, give):
    stacked = keep.shape[1]
    adapters = gates.shape[0]
    half = result.shape[1]
    product = (keep[...] + got[...].astype(F32)) * back[...]
    ones = membership(adapters, stacked)
    delta = 2.0 * dot_t(ones, product, lax.Precision.HIGHEST)
    dlogit = delta * gates[...] * (1.0 - gates[...])
    top = dlogit.astype(BF16).astype(F32)
    middle = (dlogit - top).astype(BF16).astype(F32)
    parts = jnp.concatenate([top, middle, dlogit - top - middle], axis=0).astype(BF16)
    c = at[3]
    for out, side in ((result, c), (give, 1 - c)):
        columns = pl.ds(pl.multiple_of(side * half, 128), half)
        total = jnp.dot(parts, hidden[:, columns], preferred_element_type=F32)
        out[...] = total[:adapters] + (
            total[adapters : 2 * adapters] + total[2 * adapters :]
        )


def add_kernel(left, right, *refs):
    total = left[...] + right[...]
    refs[-2][...] = total
    refs[-1][...] = total.astype(refs[-1].dtype)


def halves_kernel(at, mine, other, out):
    half = mine.shape[1]
    c = at[3]
    for side, ref in ((c, mine), (1 - c, other)):
        out[:, pl.ds(pl.multiple_of(side * half, 128), half)] = ref[...]


def add4_kernel(first, second, third, fourth, *refs):
    own = first[...].astype(second.dtype).astype(F32)
    refs[-1][...] = (own + second[...].astype(F32)) + (
        third[...].astype(F32) + fourth[...].astype(F32)
    )


def rows_product(at, steps, refs, mixed, weights, downs, out):
    y, c = at[1], at[3]
    both = jnp.concatenate([ref[...] for ref in refs], axis=0)
    ranks = jnp.concatenate(
        [mixed[0][back_at(y, c, steps)], mixed[1][back_at(y, 1 - c, steps)]], axis=0
    )
    value = dot_t(both, weights[...]) + dot_t(ranks, downs[...])
    out[...] = value.astype(out.dtype)


def far_kernel(at, own, own_s, one, one_s, two, two_s, mixed, mixed_s, *refs):
    pieces, (tie, out, weight, down) = refs[:4], refs[4:]
    width = weight.shape[1]
    rows = pieces[0].shape[0]
    x, c = at[0], at[3]
    up, turned = jnp.bitwise_xor(x, 1), 3 - x
    first, second = jnp.where(c == 0, up, turned), jnp.where(c == 0, turned, up)
    for place, ref in zip((x, first, second, jnp.bitwise_xor(x, 2)), pieces):
        place = pl.ds(pl.multiple_of(place * rows, rows), rows)
        weight[place, :] = ref[:, :width]
        down[place, :] = ref[:, width:]
    for steps, group in enumerate(((own, own_s), (one, one_s), (two, two_s))):
        rows_product(at, steps, group, (mixed, mixed_s), weight, down, out.at[steps])


def far_last_kernel(at, three, three_s, mixed, mixed_s, weight, down, tie, out):
    rows_product(at, 3, (three, three_s), (mixed, mixed_s), weight, down, out)


def product_kernel(first, at, near, near_s, more, more_s, mixed, mixed_s, weight, down, tie, out):
    for number, group in enumerate(((near, near_s), (more, more_s))):
        rows_product(at, first + number, group, (mixed, mixed_s), weight, down, out.at[number])


def place_kernel(at, near, rest, got, last, tie, out, sems):
    y, zh, c = at[1], at[2], at[3]
    tokens = out.shape[3]
    copies = []
    for steps in range(4):
        own = near.at[steps] if steps < 2 else rest.at[steps - 2]
        other = got.at[steps] if steps < 3 else last
        for ref, side in ((own, zh), (other, 1 - zh)):
            for half, core in ((0, c), (1, 1 - c)):
                copies.append(
                    pltpu.make_async_copy(
                        ref.at[pl.ds(half * tokens, tokens)],
                        out.at[back_at(y, core, steps), side, core],
                        sems.at[len(copies)],
                    )
                )
    for copy in copies:
        copy.start()
    for copy in copies:
        copy.wait()


def on_device(hidden, grad, mixture, weight, down, up, gate_matrix):
    tokens, width = grad.shape
    adapters = gate_matrix.shape[0]
    stacked = up.shape[0]
    features = weight.shape[0]
    depth = width + stacked
    quarter = features // 4
    x, y, zh, c = (lax.axis_index(a) for a in ("x", "y", "zh", "c"))
    at = jnp.stack([x, y, zh, c]).astype(jnp.int32)

    with jax.named_scope("weight_z"):
        piece = jnp.concatenate(
            [lax.dynamic_slice_in_dim(v, x * quarter, quarter, 0) for v in (weight, down)], axis=1
        )
        far_piece = swap(piece, "zh", 1)
    with jax.named_scope("tokens_y"):
        one = ring(grad, "y")
    with jax.named_scope("tokens_core"):
        own_s = swap(grad, "c", 1)

    keep, give = pl.pallas_call(
        act_kernel,
        in_specs=[SMEM, VMEM, VMEM],
        out_specs=[VMEM, VMEM],
        out_shape=[
            shaped((4, 2, tokens, stacked), F32),
            shaped((4, 2, tokens, stacked), BF16),
        ],
        compiler_params=SMALL,
        cost_estimate=cost(2 * mixture.size * stacked, 4 * mixture.size),
        name="rank_products",
    )(at, mixture.reshape(8, 2, tokens, -1), down)
    with jax.named_scope("act_core"):
        got = swap(give, "c", 1)
    mixed, gates, back = pl.pallas_call(
        token_kernel,
        in_specs=[SMEM] + [VMEM] * 4,
        out_specs=[VMEM, VMEM, VMEM],
        out_shape=[
            shaped((tokens, stacked), BF16),
            shaped((adapters, tokens), F32),
            shaped((tokens, stacked), F32),
        ],
        compiler_params=SMALL,
        cost_estimate=cost(6 * tokens * width * stacked, 12 * tokens * width),
        name="token_values",
    )(at, hidden, grad, up, gate_matrix)
    first, second, third, rest = pl.pallas_call(
        act_y_kernel,
        in_specs=[SMEM, VMEM, VMEM, VMEM],
        out_specs=[VMEM] * 4,
        out_shape=[shaped((3, tokens, stacked), BF16)] * 3 + [shaped((2, tokens, stacked), F32)],
        compiler_params=SMALL,
        name="rank_sum_core",
    )(at, keep, got, mixed)
    with jax.named_scope("act_y"):
        first, second, third = (
            swap(v, "y", mask) for v, mask in ((first, 1), (second, 2), (third, 3))
        )
    keep, give, all_mixed = pl.pallas_call(
        act_z_kernel,
        in_specs=[SMEM] + [VMEM] * 5 + [ANY],
        out_specs=[VMEM] * 3,
        out_shape=[
            shaped((tokens, stacked), F32),
            shaped((tokens, stacked), BF16),
            shaped((4, tokens, stacked), BF16),
        ],
        compiler_params=SMALL,
        name="rank_sum_y",
    )(at, rest, first, second, third, mixed, own_s)
    one, far_piece = fence((one, far_piece), give)
    with jax.named_scope("tokens_y"):
        two = ring(one, "y")
    with jax.named_scope("tokens_core"):
        one_s = swap(one, "c", 1)
    with jax.named_scope("weight_x"):
        w_first = pairs(far_piece, "x", True)
        w_second = pairs(far_piece, "x", False)
    with jax.named_scope("act_z"):
        message = swap(give, "zh", 1)
    with jax.named_scope("mixed_core"):
        mixed_s = swap(all_mixed, "c", 1)

    def products(name, first, near, near_s, more, more_s, weights, downs, tie):
        return pl.pallas_call(
            functools.partial(product_kernel, first),
            in_specs=[SMEM] + [VMEM] * 8 + [ANY],
            out_specs=VMEM,
            out_shape=shaped((2, 2 * tokens, features), BF16),
            compiler_params=MIDDLE,
            cost_estimate=cost(8 * tokens * depth * features, 12 * tokens * depth),
            name=name,
        )(at, near, near_s, more, more_s, all_mixed, mixed_s, weights, downs, tie)

    own_near = products("own_near", 0, grad, own_s, one, one_s, weight, down, give)

    total, give = pl.pallas_call(
        gate_kernel,
        in_specs=[SMEM] + [VMEM] * 5 + [ANY],
        out_specs=[VMEM, VMEM],
        out_shape=[shaped((adapters, width // 2), F32)] * 2,
        compiler_params=SMALL,
        name="gate_products",
    )(at, keep, message, back, gates, hidden, own_near)

    def add(left, right, *ties):
        return pl.pallas_call(
            add_kernel,
            in_specs=[VMEM, VMEM] + [ANY] * len(ties),
            out_specs=[VMEM, VMEM],
            out_shape=[shaped(left.shape, F32), shaped(left.shape, BF16)],
            compiler_params=SMALL,
            name="gate_sum",
        )(left, right, *ties)

    def add4(*parts):
        return pl.pallas_call(
            add4_kernel,
            in_specs=[VMEM] * 4 + [ANY] * (len(parts) - 4),
            out_specs=VMEM,
            out_shape=shaped(parts[0].shape, F32),
            compiler_params=SMALL,
        name="gate_sum",
        )(*parts)

    def step(total, axis, *ties, message=None):
        message = total if message is None else message
        with jax.named_scope("gate_" + axis):
            got = [swap(message, axis, mask) for mask in (1, 2, 3)]
        return add4(total, *got, *ties)

    with jax.named_scope("gate_core"):
        got = swap(give, "c", 1)
    total, message = add(total, got, w_first, w_second)
    (w_first,) = fence((w_first,), total)
    with jax.named_scope("weight_x_far"):
        w_far = pairs(w_first, "x", False)
    (two,) = fence((two,), w_first)
    with jax.named_scope("tokens_y"):
        three = ring(two, "y")
    total = step(total, "zl", mixed_s, w_far, two, message=message)
    with jax.named_scope("tokens_core"):
        two_s = swap(two, "c", 1)

    far, far_weight, far_down = pl.pallas_call(
        far_kernel,
        in_specs=[SMEM] + [VMEM] * 12 + [ANY],
        out_specs=[VMEM] * 3,
        out_shape=[
            shaped((3, 2 * tokens, features), BF16),
            shaped((features, width), BF16),
            shaped((features, stacked), BF16),
        ],
        compiler_params=MIDDLE,
        cost_estimate=cost(12 * tokens * depth * features, 18 * tokens * depth),
        name="far_products",
    )(
        at, grad, own_s, one, one_s, two, two_s, all_mixed, mixed_s,
        far_piece, w_first, w_second, w_far, total,
    )
    with jax.named_scope("out_z"):
        far_got = swap(far, "zh", 1)
    (three,) = fence((three,), far)
    with jax.named_scope("tokens_core"):
        three_s = swap(three, "c", 1)
    total = step(total, "x", far)

    own_rest = products("own_rest", 2, two, two_s, three, three_s, weight, down, far)
    total = step(total, "y", own_rest)
    last = pl.pallas_call(
        far_last_kernel,
        in_specs=[SMEM] + [VMEM] * 6 + [ANY],
        out_specs=VMEM,
        out_shape=shaped((2 * tokens, features), BF16),
        cost_estimate=cost(4 * tokens * depth * features, 6 * tokens * depth),
        compiler_params=MIDDLE,
        name="far_products_last",
    )(at, three, three_s, all_mixed, mixed_s, far_weight, far_down, total)
    with jax.named_scope("out_z_last"):
        last_got = swap(last, "zh", 1)

    with jax.named_scope("gate_zh"):
        got = swap(total, "zh", 1)
    total, _ = add(total, got, last, far_got)
    with jax.named_scope("gate_core_back"):
        other = swap(total, "c", 1)
    gate_grad = pl.pallas_call(
        halves_kernel,
        in_specs=[SMEM, VMEM, VMEM],
        out_specs=VMEM,
        out_shape=shaped((adapters, width), F32),
        compiler_params=SMALL,
        name="gate_halves",
    )(at, total, other)

    out = pl.pallas_call(
        place_kernel,
        in_specs=[SMEM] + [VMEM] * 4 + [ANY],
        out_specs=HBM,
        out_shape=shaped((4, 2, 2, tokens, features), BF16),
        scratch_shapes=[pltpu.SemaphoreType.DMA((16,))],
        compiler_params=MIDDLE,
        name="place",
    )(at, own_near, own_rest, far_got, last_got, gate_grad)
    return gate_grad, out.reshape(16 * tokens, features)


def solution(mesh):
    grid = Mesh(mesh.devices.reshape(4, 4, 4, 2, 2), AXES)
    dp, tensor = ("x", "zl"), ("y", "zh", "c")
    return jax.shard_map(
        on_device,
        mesh=grid,
        in_specs=(
            P(AXES, None),
            P(AXES, None),
            P(dp, tensor),
            P(tensor, None),
            P(tensor, None),
            P(),
            P(),
        ),
        out_specs=(P(), P(dp, tensor)),
        check_vma=False,
    )
```

```python
import functools

import jax
import jax.numpy as jnp
from jax import lax
from jax.experimental import pallas as pl
from jax.experimental.pallas import tpu as pltpu
from jax.sharding import Mesh
from jax.sharding import PartitionSpec as P

F32 = jnp.float32
BF16 = jnp.bfloat16
AXES = ("x", "zl", "y", "zh", "c")
VMEM = pl.BlockSpec(memory_space=pltpu.VMEM)
SMEM = pl.BlockSpec(memory_space=pltpu.SMEM)
ANY = pl.BlockSpec(memory_space=pl.ANY)
HBM = pl.BlockSpec(memory_space=pltpu.HBM)
SMALL = pltpu.CompilerParams(vmem_limit_bytes=8 * 1024 * 1024)
MIDDLE = pltpu.CompilerParams(vmem_limit_bytes=16 * 1024 * 1024)


def ring(value, axis):
    size = lax.axis_size(axis)
    pairs = [
        (2 * i + c, 2 * ((i + 1 - 2 * c) % size) + c) for i in range(size) for c in range(2)
    ]
    return lax.ppermute(value, (axis, "c"), pairs)


def pairs(value, axis, first):
    size = lax.axis_size(axis)
    partner = lambda i, c: i ^ 1 if (c == 0) == first else size - 1 - i
    return lax.ppermute(
        value, (axis, "c"), [(2 * i + c, 2 * partner(i, c) + c) for i in range(size) for c in range(2)]
    )


def fence_kernel(*refs):
    del refs


def fence(values, *ties):
    return pl.pallas_call(
        fence_kernel,
        in_specs=[ANY] * (len(values) + len(ties)),
        out_specs=[ANY] * len(values),
        out_shape=[shaped(v.shape, v.dtype) for v in values],
        input_output_aliases={i: i for i in range(len(values))},
        compiler_params=SMALL,
        name="fence",
    )(*values, *ties)


def back_at(place, core, steps):
    return lax.rem(place - steps * (1 - 2 * core) + 4, 4)


def swap(value, axis, mask):
    size = lax.axis_size(axis)
    return lax.ppermute(value, axis, [(i, i ^ mask) for i in range(size)])


def dot_t(left, right, precision=None):
    return lax.dot_general(
        left, right, (((1,), (1,)), ((), ())), precision=precision, preferred_element_type=F32
    )


def shaped(shape, dtype):
    return jax.ShapeDtypeStruct(shape, dtype)


def cost(flops, moved):
    return pl.CostEstimate(flops=flops, bytes_accessed=moved, transcendentals=0)


def membership(adapters, stacked):
    row = lax.broadcasted_iota(jnp.int32, (adapters, stacked), 0)
    column = lax.broadcasted_iota(jnp.int32, (adapters, stacked), 1)
    low = row * (stacked // adapters)
    return jnp.where((column >= low) & (column < low + stacked // adapters), 1.0, 0.0)


def token_kernel(at, hidden, grad, up, gate, mixed, gates, back):
    stacked = up.shape[0]
    ones = membership(gate.shape[0], stacked)
    wide = lax.dot_general(
        ones.astype(BF16), gate[...], (((0,), (0,)), ((), ())), preferred_element_type=F32
    ).astype(BF16)
    gates[...] = jax.nn.sigmoid(dot_t(gate[...], hidden[...]))
    factor = 2.0 * jax.nn.sigmoid(dot_t(hidden[...], wide))
    pulled = dot_t(grad[...], up[...])
    back[...] = pulled
    mixed[...] = (factor * pulled).astype(BF16)


def act_kernel(at, mixture, down, keep, give):
    c = at[3]
    blocks, _, tokens, depth = mixture.shape
    for out, side in ((give, 1 - c), (keep, c)):
        rows = mixture[:, side].reshape(blocks * tokens, depth)
        value = jnp.dot(rows, down[...], preferred_element_type=F32)
        out[...] = value.reshape(out.shape).astype(out.dtype)


def act_y_kernel(at, keep, got, mixed, first, second, third, rest):
    y = at[1]
    for out, mask in ((first, 1), (second, 2), (third, 3)):
        row = jnp.bitwise_xor(y, mask)
        out[pl.ds(0, 2)] = (keep[row] + got[row].astype(F32)).astype(out.dtype)
        out[2] = mixed[...]
    rest[...] = keep[y] + got[y].astype(F32)


def act_z_kernel(at, rest, first, second, third, mixed, tie, keep, give, all_mixed):
    y, zh = at[1], at[2]
    for out, side in ((give, 1 - zh), (keep, zh)):
        total = (rest[side] + first[side].astype(F32)) + (
            second[side].astype(F32) + third[side].astype(F32)
        )
        out[...] = total.astype(out.dtype)
    all_mixed[y] = mixed[...]
    for ref, mask in ((first, 1), (second, 2), (third, 3)):
        all_mixed[jnp.bitwise_xor(y, mask)] = ref[2]


def gate_kernel(at, keep, got, back, gates, hidden, tie, result, give):
    stacked = keep.shape[1]
    adapters = gates.shape[0]
    half = result.shape[1]
    product = (keep[...] + got[...].astype(F32)) * back[...]
    ones = membership(adapters, stacked)
    delta = 2.0 * dot_t(ones, product, lax.Precision.HIGHEST)
    dlogit = delta * gates[...] * (1.0 - gates[...])
    top = dlogit.astype(BF16).astype(F32)
    middle = (dlogit - top).astype(BF16).astype(F32)
    parts = jnp.concatenate([top, middle, dlogit - top - middle], axis=0).astype(BF16)
    c = at[3]
    for out, side in ((result, c), (give, 1 - c)):
        columns = pl.ds(pl.multiple_of(side * half, 128), half)
        total = jnp.dot(parts, hidden[:, columns], preferred_element_type=F32)
        out[...] = total[:adapters] + (
            total[adapters : 2 * adapters] + total[2 * adapters :]
        )


def add_kernel(left, right, *refs):
    total = left[...].astype(right.dtype).astype(F32) + right[...].astype(F32)
    refs[-2][...] = total
    refs[-1][...] = total.astype(refs[-1].dtype)


def halves_kernel(at, mine, other, out):
    half = mine.shape[1]
    c = at[3]
    for side, ref in ((c, mine), (1 - c, other)):
        out[:, pl.ds(pl.multiple_of(side * half, 128), half)] = ref[...]


def add4_kernel(first, second, third, fourth, *refs):
    own = first[...].astype(second.dtype).astype(F32)
    total = (own + second[...].astype(F32)) + (third[...].astype(F32) + fourth[...].astype(F32))
    refs[-2][...] = total
    refs[-1][...] = total.astype(refs[-1].dtype)


def rows_product(at, steps, refs, mixed, weights, downs, out):
    y, c = at[1], at[3]
    both = jnp.concatenate([ref[...] for ref in refs], axis=0)
    ranks = jnp.concatenate(
        [mixed[0][back_at(y, c, steps)], mixed[1][back_at(y, 1 - c, steps)]], axis=0
    )
    value = dot_t(both, weights[...]) + dot_t(ranks, downs[...])
    out[...] = value.astype(out.dtype)


def far_kernel(at, own, own_s, one, one_s, two, two_s, mixed, mixed_s, *refs):
    pieces, (tie, out, weight, down) = refs[:4], refs[4:]
    width = weight.shape[1]
    rows = pieces[0].shape[0]
    x, c = at[0], at[3]
    up, turned = jnp.bitwise_xor(x, 1), 3 - x
    first, second = jnp.where(c == 0, up, turned), jnp.where(c == 0, turned, up)
    for place, ref in zip((x, first, second, jnp.bitwise_xor(x, 2)), pieces):
        place = pl.ds(pl.multiple_of(place * rows, rows), rows)
        weight[place, :] = ref[:, :width]
        down[place, :] = ref[:, width:]
    for steps, group in enumerate(((own, own_s), (one, one_s), (two, two_s))):
        rows_product(at, steps, group, (mixed, mixed_s), weight, down, out.at[steps])


def far_last_kernel(at, three, three_s, mixed, mixed_s, weight, down, tie, out):
    rows_product(at, 3, (three, three_s), (mixed, mixed_s), weight, down, out)


def product_kernel(first, at, near, near_s, more, more_s, mixed, mixed_s, weight, down, tie, out):
    for number, group in enumerate(((near, near_s), (more, more_s))):
        rows_product(at, first + number, group, (mixed, mixed_s), weight, down, out.at[number])


def place_kernel(at, near, rest, got, last, tie, out, sems):
    y, zh, c = at[1], at[2], at[3]
    tokens = out.shape[3]
    copies = []
    for steps in range(4):
        own = near.at[steps] if steps < 2 else rest.at[steps - 2]
        other = got.at[steps] if steps < 3 else last
        for ref, side in ((own, zh), (other, 1 - zh)):
            for half, core in ((0, c), (1, 1 - c)):
                copies.append(
                    pltpu.make_async_copy(
                        ref.at[pl.ds(half * tokens, tokens)],
                        out.at[back_at(y, core, steps), side, core],
                        sems.at[len(copies)],
                    )
                )
    for copy in copies:
        copy.start()
    for copy in copies:
        copy.wait()


def on_device(hidden, grad, mixture, weight, down, up, gate_matrix):
    tokens, width = grad.shape
    adapters = gate_matrix.shape[0]
    stacked = up.shape[0]
    features = weight.shape[0]
    depth = width + stacked
    quarter = features // 4
    x, y, zh, c = (lax.axis_index(a) for a in ("x", "y", "zh", "c"))
    at = jnp.stack([x, y, zh, c]).astype(jnp.int32)

    with jax.named_scope("weight_z"):
        piece = jnp.concatenate(
            [lax.dynamic_slice_in_dim(v, x * quarter, quarter, 0) for v in (weight, down)], axis=1
        )
        far_piece = swap(piece, "zh", 1)
    with jax.named_scope("tokens_y"):
        one = ring(grad, "y")
    with jax.named_scope("tokens_core"):
        own_s = swap(grad, "c", 1)

    keep, give = pl.pallas_call(
        act_kernel,
        in_specs=[SMEM, VMEM, VMEM],
        out_specs=[VMEM, VMEM],
        out_shape=[
            shaped((4, 2, tokens, stacked), F32),
            shaped((4, 2, tokens, stacked), BF16),
        ],
        compiler_params=SMALL,
        cost_estimate=cost(2 * mixture.size * stacked, 4 * mixture.size),
        name="rank_products",
    )(at, mixture.reshape(8, 2, tokens, -1), down)
    with jax.named_scope("act_core"):
        got = swap(give, "c", 1)
    mixed, gates, back = pl.pallas_call(
        token_kernel,
        in_specs=[SMEM] + [VMEM] * 4,
        out_specs=[VMEM, VMEM, VMEM],
        out_shape=[
            shaped((tokens, stacked), BF16),
            shaped((adapters, tokens), F32),
            shaped((tokens, stacked), F32),
        ],
        compiler_params=SMALL,
        cost_estimate=cost(6 * tokens * width * stacked, 12 * tokens * width),
        name="token_values",
    )(at, hidden, grad, up, gate_matrix)
    first, second, third, rest = pl.pallas_call(
        act_y_kernel,
        in_specs=[SMEM, VMEM, VMEM, VMEM],
        out_specs=[VMEM] * 4,
        out_shape=[shaped((3, tokens, stacked), BF16)] * 3 + [shaped((2, tokens, stacked), F32)],
        compiler_params=SMALL,
        name="rank_sum_core",
    )(at, keep, got, mixed)
    with jax.named_scope("act_y"):
        first, second, third = (
            swap(v, "y", mask) for v, mask in ((first, 1), (second, 2), (third, 3))
        )
    keep, give, all_mixed = pl.pallas_call(
        act_z_kernel,
        in_specs=[SMEM] + [VMEM] * 5 + [ANY],
        out_specs=[VMEM] * 3,
        out_shape=[
            shaped((tokens, stacked), F32),
            shaped((tokens, stacked), BF16),
            shaped((4, tokens, stacked), BF16),
        ],
        compiler_params=SMALL,
        name="rank_sum_y",
    )(at, rest, first, second, third, mixed, own_s)
    one, far_piece = fence((one, far_piece), give)
    with jax.named_scope("tokens_y"):
        two = ring(one, "y")
    with jax.named_scope("tokens_core"):
        one_s = swap(one, "c", 1)
    with jax.named_scope("weight_x"):
        w_first = pairs(far_piece, "x", True)
        w_second = pairs(far_piece, "x", False)
    with jax.named_scope("act_z"):
        message = swap(give, "zh", 1)
    with jax.named_scope("mixed_core"):
        mixed_s = swap(all_mixed, "c", 1)

    def products(name, first, near, near_s, more, more_s, weights, downs, tie):
        return pl.pallas_call(
            functools.partial(product_kernel, first),
            in_specs=[SMEM] + [VMEM] * 8 + [ANY],
            out_specs=VMEM,
            out_shape=shaped((2, 2 * tokens, features), BF16),
            compiler_params=MIDDLE,
            cost_estimate=cost(8 * tokens * depth * features, 12 * tokens * depth),
            name=name,
        )(at, near, near_s, more, more_s, all_mixed, mixed_s, weights, downs, tie)

    own_near = products("own_near", 0, grad, own_s, one, one_s, weight, down, give)

    total, give = pl.pallas_call(
        gate_kernel,
        in_specs=[SMEM] + [VMEM] * 5 + [ANY],
        out_specs=[VMEM, VMEM],
        out_shape=[shaped((adapters, width // 2), F32)] * 2,
        compiler_params=SMALL,
        name="gate_products",
    )(at, keep, message, back, gates, hidden, own_near)

    def add(left, right, *ties):
        return pl.pallas_call(
            add_kernel,
            in_specs=[VMEM, VMEM] + [ANY] * len(ties),
            out_specs=[VMEM, VMEM],
            out_shape=[shaped(left.shape, F32), shaped(left.shape, BF16)],
            compiler_params=SMALL,
            name="gate_sum",
        )(left, right, *ties)

    def add4(*parts):
        return pl.pallas_call(
            add4_kernel,
            in_specs=[VMEM] * 4 + [ANY] * (len(parts) - 4),
            out_specs=[VMEM, VMEM],
            out_shape=[shaped(parts[0].shape, F32), shaped(parts[0].shape, BF16)],
            compiler_params=SMALL,
        name="gate_sum",
        )(*parts)

    def step(total, axis, *ties, message=None):
        message = total if message is None else message
        with jax.named_scope("gate_" + axis):
            got = [swap(message, axis, mask) for mask in (1, 2, 3)]
        return add4(total, *got, *ties)

    with jax.named_scope("gate_core"):
        got = swap(give, "c", 1)
    total, message = add(total, got, w_first, w_second)
    (w_first,) = fence((w_first,), total)
    with jax.named_scope("weight_x_far"):
        w_far = pairs(w_first, "x", False)
    (two,) = fence((two,), w_first)
    with jax.named_scope("tokens_y"):
        three = ring(two, "y")
    total, _ = step(total, "zl", mixed_s, w_far, two, message=message)
    with jax.named_scope("tokens_core"):
        two_s = swap(two, "c", 1)

    far, far_weight, far_down = pl.pallas_call(
        far_kernel,
        in_specs=[SMEM] + [VMEM] * 12 + [ANY],
        out_specs=[VMEM] * 3,
        out_shape=[
            shaped((3, 2 * tokens, features), BF16),
            shaped((features, width), BF16),
            shaped((features, stacked), BF16),
        ],
        compiler_params=MIDDLE,
        cost_estimate=cost(12 * tokens * depth * features, 18 * tokens * depth),
        name="far_products",
    )(
        at, grad, own_s, one, one_s, two, two_s, all_mixed, mixed_s,
        far_piece, w_first, w_second, w_far, total,
    )
    with jax.named_scope("out_z"):
        far_got = swap(far, "zh", 1)
    (three,) = fence((three,), far)
    with jax.named_scope("tokens_core"):
        three_s = swap(three, "c", 1)
    total, _ = step(total, "x", far)

    own_rest = products("own_rest", 2, two, two_s, three, three_s, weight, down, far)
    total, message = step(total, "y", own_rest)
    last = pl.pallas_call(
        far_last_kernel,
        in_specs=[SMEM] + [VMEM] * 6 + [ANY],
        out_specs=VMEM,
        out_shape=shaped((2 * tokens, features), BF16),
        cost_estimate=cost(4 * tokens * depth * features, 6 * tokens * depth),
        compiler_params=MIDDLE,
        name="far_products_last",
    )(at, three, three_s, all_mixed, mixed_s, far_weight, far_down, total)
    with jax.named_scope("out_z_last"):
        last_got = swap(last, "zh", 1)

    with jax.named_scope("gate_zh"):
        got = swap(message, "zh", 1)
    total, _ = add(total, got, last, far_got)
    with jax.named_scope("gate_core_back"):
        other = swap(total, "c", 1)
    gate_grad = pl.pallas_call(
        halves_kernel,
        in_specs=[SMEM, VMEM, VMEM],
        out_specs=VMEM,
        out_shape=shaped((adapters, width), F32),
        compiler_params=SMALL,
        name="gate_halves",
    )(at, total, other)

    out = pl.pallas_call(
        place_kernel,
        in_specs=[SMEM] + [VMEM] * 4 + [ANY],
        out_specs=HBM,
        out_shape=shaped((4, 2, 2, tokens, features), BF16),
        scratch_shapes=[pltpu.SemaphoreType.DMA((16,))],
        compiler_params=MIDDLE,
        name="place",
    )(at, own_near, own_rest, far_got, last_got, gate_grad)
    return gate_grad, out.reshape(16 * tokens, features)


def solution(mesh):
    grid = Mesh(mesh.devices.reshape(4, 4, 4, 2, 2), AXES)
    dp, tensor = ("x", "zl"), ("y", "zh", "c")
    return jax.shard_map(
        on_device,
        mesh=grid,
        in_specs=(
            P(AXES, None),
            P(AXES, None),
            P(dp, tensor),
            P(tensor, None),
            P(tensor, None),
            P(),
            P(),
        ),
        out_specs=(P(), P(dp, tensor)),
        check_vma=False,
    )
```
